32 devices in a mesh: dp: 2 (over x), gx: 4 (over y, core), gy: 4 (over z).
Axes of the slice: x: 2, y: 2, z: 4, core: 2. Of those that a mesh axis runs over, the one named last changes fastest.
Arguments:
- tokens: bfloat16 [8, 2048, 768], P(('dp', 'gy'), 'gx'), may hold values from -6 to 6
- teacher: bfloat16 [8, 2048, 768], P(('dp', 'gy'), 'gx'), may hold values from -6 to 6
- picture_lengths: int32 [8, 20], P(('dp', 'gy')), may hold values from 0 to 1024, as said below
- first_gain: float32 [768], replicated, may hold values from 0.25 to 1.75
- first_shift: float32 [768], replicated, may hold values from -1.5 to 1.5
- input_weight: bfloat16 [768, 2304], P(('dp', 'gy'), 'gx'), may hold values from -0.21875 to 0.21875
- input_bias: float32 [2304], replicated, may hold values from -1.5 to 1.5
- query_gain: float32 [64], replicated, may hold values from 0.25 to 1.75
- key_gain: float32 [64], replicated, may hold values from 0.25 to 1.75
- output_weight: bfloat16 [768, 768], P('gx', ('dp', 'gy')), may hold values from -1.75 to 1.75
- output_bias: float32 [768], replicated, may hold values from -1.5 to 1.5
- second_gain: float32 [768], replicated, may hold values from 0.25 to 1.75
- second_shift: float32 [768], replicated, may hold values from -1.5 to 1.5
- expand_weight: bfloat16 [768, 3072], P(('dp', 'gy'), 'gx'), may hold values from -0.21875 to 0.21875
- expand_bias: float32 [3072], replicated, may hold values from -1.5 to 1.5
- reduce_weight: bfloat16 [3072, 768], P('gx', ('dp', 'gy')), may hold values from -0.109375 to 0.109375
- reduce_bias: float32 [768], replicated, may hold values from -1.5 to 1.5
Outputs:
- layer_output: bfloat16 [8, 2048, 768], P(('dp', 'gy'), 'gx')
- loss_value: float32 [], replicated
- tokens_gradient: float32 [8, 2048, 768], P(('dp', 'gy'), 'gx')
- first_gain_gradient: float32 [768], replicated
- first_shift_gradient: float32 [768], replicated
- input_weight_gradient: float32 [768, 2304], P(('dp', 'gy'), 'gx')
- input_bias_gradient: float32 [2304], replicated
- query_gain_gradient: float32 [64], replicated
- key_gain_gradient: float32 [64], replicated
- output_weight_gradient: float32 [768, 768], P('gx', ('dp', 'gy'))
- output_bias_gradient: float32 [768], replicated
- second_gain_gradient: float32 [768], replicated
- second_shift_gradient: float32 [768], replicated
- expand_weight_gradient: float32 [768, 3072], P(('dp', 'gy'), 'gx')
- expand_bias_gradient: float32 [3072], replicated
- reduce_weight_gradient: float32 [3072, 768], P('gx', ('dp', 'gy'))
- reduce_bias_gradient: float32 [768], replicated
The draws below stay inside these ranges and needn't reach their ends.
Inputs may be any that keep to these rules, and one draw needn't show every extreme that they name: `picture_lengths`: in each row the nonzero entries come first, each is 100 to 1024, and they sum to at most 2048; every row holds one picture or more, and some row holds a picture of 1024 patches.
All inputs are finite; a program needn't handle non-finite values.
Results may differ from the reference program's by a relative error of at most 0.0055.
Values may be sent and summed in bfloat16 or wider, within the bound.
No kernel may reach another device: no remote copies, remote signals or barrier semaphores. Data moves between devices by JAX's collectives and lax.ppermute only.
A program may use at most 128 MiB of HBM per device.

```python
import jax
import jax.numpy as jnp
from jax import lax

D = 768
HEADS = 12
HD = 64
FF = 3072
ROW_LEN = 2048
PIC_MIN = 100
PIC_MAX = 1024
PICS = 20
ROWS = 8
TOKENS = 16384


def draw_picture_lengths(key, part):
    key = jax.random.fold_in(key, 7)
    first_key, second_key, third_key = jax.random.split(key, 3)
    slots = ROW_LEN // PIC_MIN
    place = jnp.arange(ROWS, dtype=jnp.int32)
    target = ROW_LEN * (30 + 65 * place // max(ROWS - 1, 1)) // 100
    candidate = jax.random.randint(first_key, (ROWS, slots), PIC_MIN, PIC_MAX + 1)
    opening = jax.random.randint(second_key, (ROWS,), PIC_MIN, jnp.minimum(target, PIC_MAX) + 1)
    chosen = jax.random.randint(third_key, (), ROWS // 2, ROWS)
    opening = jnp.where(place == chosen, PIC_MAX, opening)
    candidate = candidate.at[:, 0].set(opening)
    ends = jnp.cumsum(candidate, axis=1)
    return jnp.where(ends <= target[:, None], candidate, 0).astype(jnp.int32)


def level_of(own_key, extent, shards, low, high):
    level, own = 1.0, jax.random.fold_in(own_key, 6)
    for dim, parts in shards:
        steps = jnp.exp(jax.random.uniform(jax.random.fold_in(own, dim), (parts,), jnp.float32, low / len(shards), high / len(shards)))
        level = level * jnp.repeat(steps, extent[dim] // parts).reshape([-1 if axis == dim else 1 for axis in range(len(extent))])
    return level


def centred(rng, extent, spread, most, shards=(), held_as=jnp.bfloat16):
    factor_of = level_of(rng, extent, shards, -0.22, 0.18) if shards else 1.0
    values = jax.random.normal(rng, extent, jnp.float32) * spread * factor_of
    return jnp.minimum(jnp.maximum(values, -most), most).astype(held_as)


def setup_inputs(seed: int = 0) -> dict:
    key_of = jax.random.split(jax.random.key(seed), 18)
    tokens = centred(key_of[0], (ROWS, ROW_LEN, D), 1.0, 6.0, ((0, 8), (1, 4)))
    teacher = centred(key_of[1], (ROWS, ROW_LEN, D), 1.0, 6.0, ((0, 8), (1, 4)))
    picture_lengths = draw_picture_lengths(jax.random.fold_in(key_of[17], 71), 0)
    first_gain = jnp.clip(1.0 + 0.15 * jax.random.normal(key_of[3], (D,), jnp.float32), 0.25, 1.75)
    first_shift = centred(key_of[4], (D,), 0.3, 1.5, (), jnp.float32)
    input_weight = centred(key_of[5], (D, 3 * D), D ** -0.5, 0.21875, ((0, 8), (1, 4)))
    input_bias = centred(key_of[6], (3 * D,), 0.3, 1.5, (), jnp.float32)
    query_gain = jnp.clip(1.0 + 0.15 * jax.random.normal(key_of[7], (HD,), jnp.float32), 0.25, 1.75)
    key_gain = jnp.clip(1.0 + 0.15 * jax.random.normal(key_of[8], (HD,), jnp.float32), 0.25, 1.75)
    output_weight = centred(key_of[9], (D, D), (D // 64) ** -0.5, 1.75, ((0, 4), (1, 8)))
    output_bias = centred(key_of[10], (D,), 0.3, 1.5, (), jnp.float32)
    second_gain = jnp.clip(1.0 + 0.15 * jax.random.normal(key_of[11], (D,), jnp.float32), 0.25, 1.75)
    second_shift = centred(key_of[12], (D,), 0.3, 1.5, (), jnp.float32)
    expand_weight = centred(key_of[13], (D, FF), D ** -0.5, 0.21875, ((0, 8), (1, 4)))
    expand_bias = centred(key_of[14], (FF,), 0.3, 1.5, (), jnp.float32)
    reduce_weight = centred(key_of[15], (FF, D), FF ** -0.5, 0.109375, ((0, 4), (1, 8)))
    reduce_bias = centred(key_of[16], (D,), 0.3, 1.5, (), jnp.float32)
    return dict(tokens=tokens, teacher=teacher, picture_lengths=picture_lengths, first_gain=first_gain, first_shift=first_shift, input_weight=input_weight, input_bias=input_bias, query_gain=query_gain, key_gain=key_gain, output_weight=output_weight, output_bias=output_bias, second_gain=second_gain, second_shift=second_shift, expand_weight=expand_weight, expand_bias=expand_bias, reduce_weight=reduce_weight, reduce_bias=reduce_bias)


@jax.custom_vjp
def low(v):
    return lax.optimization_barrier(v.astype(jnp.bfloat16)).astype(jnp.float32)

@jax.custom_vjp
def low_back(v):
    return v

def low_keep(v):
    return (low(v), None)

def low_pass(kept, grad):
    return (grad,)

def back_keep(v):
    return (v, None)

def back_low(kept, grad):
    return (low(grad),)
low.defvjp(low_keep, low_pass)
low_back.defvjp(back_keep, back_low)
EPS = 1e-06
MASKED = -1e+30
HIGH = lax.Precision.HIGHEST

def picture_numbers(lengths):
    ends = jnp.cumsum(lengths, axis=1)
    place = jnp.arange(ROW_LEN, dtype=jnp.int32)
    return lax.optimization_barrier(jnp.sum((ends[:, None, :] <= place[None, :, None]).astype(jnp.int32), axis=2))

def norm_rows(values, gain, shift):
    mean = lax.optimization_barrier(jnp.mean(values, axis=-1, keepdims=True))
    centered = values - mean
    factor = lax.rsqrt(lax.optimization_barrier(jnp.mean(centered * centered, axis=-1, keepdims=True)) + EPS)
    return centered * factor * gain + shift

def row_attention(pieces):
    queries, row_keys, row_values, numbers = pieces
    scores = jnp.einsum('hqd,hkd->hqk', queries, row_keys, precision=HIGH) * HD ** (-0.5)
    allowed = numbers[:, None] == numbers[None, :]
    scores = low_back(jnp.where(allowed[None], scores, MASKED))
    chance = low(jax.nn.softmax(scores, axis=-1))
    return jnp.einsum('hqk,hkd->hqd', chance, row_values, precision=HIGH)

def to_rows(array):
    return array.reshape(ROWS, ROW_LEN, HEADS, HD).transpose(0, 2, 1, 3)

def layer(tokens, first_gain, first_shift, input_weight, input_bias, query_gain, key_gain, output_weight, output_bias, second_gain, second_shift, expand_weight, expand_bias, reduce_weight, reduce_bias, teacher, numbers, valid):
    tokens = tokens.reshape(TOKENS, D)
    count = jnp.sum(valid)
    first_low = low(norm_rows(tokens, first_gain, first_shift))
    mixed = low_back(jnp.dot(first_low, input_weight, precision=HIGH) + input_bias)
    mixed = mixed.reshape(TOKENS, HEADS, 3, HD)
    queries = low(norm_rows(mixed[:, :, 0], query_gain, 0.0))
    row_keys = low(norm_rows(mixed[:, :, 1], key_gain, 0.0))
    row_values = low(mixed[:, :, 2])
    attended = lax.map(jax.checkpoint(row_attention), (to_rows(queries), to_rows(row_keys), to_rows(row_values), numbers))
    attended = attended.transpose(0, 2, 1, 3).reshape(TOKENS, HEADS * HD)
    heads_low = low(low_back(attended))
    branch = low_back(jnp.dot(heads_low, output_weight, precision=HIGH) + output_bias)
    stream = tokens + branch
    second_low = low(norm_rows(stream, second_gain, second_shift))
    hidden = low_back(jnp.dot(second_low, expand_weight, precision=HIGH) + expand_bias)
    active = low(jax.nn.gelu(hidden, approximate=False))
    result = stream + low_back(jnp.dot(active, reduce_weight, precision=HIGH) + reduce_bias)
    error = (result - teacher) * valid[:, None]
    return (jnp.sum(error * error) / count, result)

def reference(tokens, teacher, picture_lengths, first_gain, first_shift, input_weight, input_bias, query_gain, key_gain, output_weight, output_bias, second_gain, second_shift, expand_weight, expand_bias, reduce_weight, reduce_bias):
    numbers = picture_numbers(picture_lengths)
    valid = (numbers.reshape(-1) < PICS).astype(jnp.float32)
    target = teacher.astype(jnp.float32).reshape(TOKENS, D)
    params = [p.astype(jnp.float32) for p in (tokens, first_gain, first_shift, input_weight, input_bias, query_gain, key_gain, output_weight, output_bias, second_gain, second_shift, expand_weight, expand_bias, reduce_weight, reduce_bias)]

    def loss_of(*values):
        return layer(*values, target, numbers, valid)
    loss_value, pullback, result = jax.vjp(loss_of, *params, has_aux=True)
    grads = pullback(jnp.ones((), jnp.float32))
    return (result.reshape(ROWS, ROW_LEN, D).astype(jnp.bfloat16), loss_value, grads[0].reshape(ROWS, ROW_LEN, D), grads[1], grads[2], grads[3], grads[4], grads[5], grads[6], grads[7], grads[8], grads[9], grads[10], grads[11], grads[12], grads[13], grads[14])
```

```python
from functools import partial

import jax
import jax.numpy as jnp
from jax import lax
from jax.experimental import pallas as pl
from jax.experimental.pallas import tpu as pltpu
from jax.sharding import PartitionSpec as P

EPS = 1e-06
APART = 1024.0
TILE = 256
MIB = 1 << 20
F32 = jnp.float32
BF16 = jnp.bfloat16

NN = (((1,), (0,)), ((), ()))
NT = (((1,), (1,)), ((), ()))


def mm(left, right, dims=NN):
    return lax.dot_general(left, right, dims, preferred_element_type=F32)


def params(limit=40):
    return pltpu.CompilerParams(vmem_limit_bytes=limit * MIB)


def whole(shape):
    rank = len(shape)
    return pl.BlockSpec(shape, lambda *_: (0,) * rank)


def once(shape):
    rank = len(shape)
    return pl.BlockSpec(shape, lambda *_: (0,) * rank, pipeline_mode=pl.Buffered(1))


def rows_hat(values):
    mean = jnp.mean(values, axis=-1, keepdims=True)
    centered = values - mean
    factor = lax.rsqrt(jnp.mean(centered * centered, axis=-1, keepdims=True) + EPS)
    return centered * factor, factor


def rows_back(grad_hat, hat, factor):
    return factor * (
        grad_hat
        - jnp.mean(grad_hat, axis=-1, keepdims=True)
        - hat * jnp.mean(grad_hat * hat, axis=-1, keepdims=True)
    )


def swap(array, axis, mask):
    size = lax.axis_size(axis)
    return lax.ppermute(array, axis, [(i, i ^ mask) for i in range(size)])


def bits_of(axis):
    size = lax.axis_size(axis)
    masks = []
    mask = 1
    while mask < size:
        masks.append(mask)
        mask *= 2
    return masks


def gather_rows(shard):
    rows, cols = shard.shape
    held = shard.reshape(1, rows, cols)
    for mask in reversed(bits_of("gy")):
        mine = (lax.axis_index("gy") & mask) != 0
        other = swap(held, "gy", mask)
        held = jnp.where(
            mine, jnp.stack([other, held], axis=1), jnp.stack([held, other], axis=1)
        ).reshape(-1, rows, cols)
    for mask in bits_of("dp"):
        mine = (lax.axis_index("dp") & mask) != 0
        other = swap(held, "dp", mask)
        held = jnp.where(
            mine, jnp.concatenate([other, held]), jnp.concatenate([held, other])
        )
    return held.reshape(-1, cols)


def scatter_rows(terms, rows):
    cols = terms.shape[1]
    held = terms.reshape(-1, rows, cols)
    for mask in reversed(bits_of("dp")):
        bit = ((lax.axis_index("dp") & mask) != 0).astype(jnp.int32)
        halves = held.reshape(2, -1, rows, cols)
        out = lax.dynamic_index_in_dim(halves, 1 - bit, 0, False).astype(BF16)
        keep = lax.dynamic_index_in_dim(halves, bit, 0, False)
        held = keep.astype(F32) + swap(out, "dp", mask).astype(F32)
    for mask in bits_of("gy"):
        bit = ((lax.axis_index("gy") & mask) != 0).astype(jnp.int32)
        halves = held.reshape(-1, 2, rows, cols)
        out = lax.dynamic_index_in_dim(halves, 1 - bit, 1, False).astype(BF16)
        keep = lax.dynamic_index_in_dim(halves, bit, 1, False)
        held = keep.astype(F32) + swap(out, "gy", mask).astype(F32)
    return held.reshape(rows, cols)


def sum_all(values):
    for mask in bits_of("gx"):
        values = values + swap(values, "gx", mask)
    for axis in ("dp", "gy"):
        for mask in bits_of(axis):
            values = values + swap(values, axis, mask)
    return values


def packed(parts):
    flat = jnp.concatenate([part.reshape(-1) for part in parts])
    return jnp.pad(flat, (0, -flat.shape[0] % 1024)).reshape(-1, 128)


def unpacked(flat, shapes):
    flat = flat.reshape(-1)
    outs = []
    start = 0
    for amount in shapes:
        outs.append(flat[start : start + amount])
        start += amount
    return outs


def mixed_kernel(count, heads, hd, *refs):
    toks = refs[:count]
    gain, shift, weight, bias, q_gain, k_gain = refs[count : count + 6]
    low_ref, mixed_ref, hat_ref, scale_ref = refs[count + 6 :]
    wide = heads * 3 * hd
    for j in range(count):
        hat, _ = rows_hat(toks[j][...].astype(F32))
        low = (hat * gain[...] + shift[...]).astype(BF16)
        low_ref[j] = low
        mixed = (mm(low, weight[:, :wide]) + bias[...]).T
        scales = []
        for h in range(heads):
            for kind, a_gain, factor in ((0, q_gain, hd**-0.5), (1, k_gain, 1.0)):
                start = (h * 3 + kind) * hd
                raw = mixed[start : start + hd]
                centered = raw - jnp.mean(raw, axis=0, keepdims=True)
                scale = lax.rsqrt(jnp.mean(centered * centered, axis=0, keepdims=True) + EPS)
                unit = centered * scale
                hat_ref[j, (h * 2 + kind) * hd : (h * 2 + kind + 1) * hd, :] = unit
                scales.append(scale)
                normed = (unit * a_gain[...]).astype(BF16)
                if factor != 1.0:
                    normed = normed * jnp.asarray(factor, BF16)
                mixed_ref[j, start : start + hd, :] = normed
            start = (h * 3 + 2) * hd
            mixed_ref[j, start : start + hd, :] = mixed[start : start + hd].astype(BF16)
        for n, scale in enumerate(scales):
            scale_ref[j, n : n + 1, :] = scale


def mixed_call(pieces, gain, shift, weight, bias, q_gain, k_gain, heads, hd):
    count = len(pieces)
    part, width = pieces[0].shape
    block = min(TILE, part)
    wide = heads * 3 * hd
    piece_spec = pl.BlockSpec((block, width), lambda i: (i, 0))

    def lanes(rows):
        return pl.BlockSpec((count, rows, block), lambda i: (0, 0, i))

    scale_rows = 8 * -(-2 * heads // 8)
    return pl.pallas_call(
        partial(mixed_kernel, count, heads, hd),
        grid=(part // block,),
        in_specs=[piece_spec] * count
        + [whole(a.shape) for a in (gain, shift, weight, bias, q_gain, k_gain)],
        out_specs=[
            pl.BlockSpec((count, block, width), lambda i: (0, i, 0)),
            lanes(wide),
            lanes(heads * 2 * hd),
            lanes(scale_rows),
        ],
        out_shape=[
            jax.ShapeDtypeStruct((count, part, width), BF16),
            jax.ShapeDtypeStruct((count, wide, part), BF16),
            jax.ShapeDtypeStruct((count, heads * 2 * hd, part), F32),
            jax.ShapeDtypeStruct((count, scale_rows, part), F32),
        ],
        compiler_params=params(),
        cost_estimate=pl.CostEstimate(
            flops=2 * count * part * width * wide,
            bytes_accessed=count * part * width * 8,
            transcendentals=0,
        ),
        name="mixed",
    )(*pieces, gain, shift, weight, bias, q_gain, k_gain)


def one_hot(num_ref, start, amount):
    place = lax.broadcasted_iota(jnp.int32, (32, amount), 0)
    return (place == num_ref[:, pl.ds(start, amount)]).astype(F32)


def lay_out(me, num_ref, sources, heads, hd, part, keys_tok, queries_lane):
    for j in range(2 * len(sources)):
        source = sources[j // 2]
        start = pl.multiple_of((me ^ j) * part, part)
        marks = one_hot(num_ref, start, part)
        away = ((marks - 1.0) * APART).astype(BF16)
        blank = jnp.zeros((32, part), F32)
        for h in range(heads):
            base = h * 3 * hd
            queries_lane[h, 0:hd, pl.ds(start, part)] = source[j % 2, base : base + hd, :]
            queries_lane[h, hd : hd + 32, pl.ds(start, part)] = away
            queries_lane[h, hd + 32 : hd + 64, pl.ds(start, part)] = blank.astype(BF16)
            key = source[j % 2, base + hd : base + 2 * hd, :].astype(F32)
            keys_tok[h, pl.ds(start, part), :] = (
                jnp.concatenate([key, marks, blank], axis=0).T.astype(BF16)
            )


def attend_kernel(
    heads, hd, part, pos, num, mixed_a, mixed_b, att, raw, log, keys_tok, queries_lane, vals, acc
):
    i = pl.program_id(0)
    block = att.shape[2]
    me = pos[0]

    @pl.when(i == 0)
    def _():
        lay_out(me, num, (mixed_a, mixed_b), heads, hd, part, keys_tok, queries_lane)
        for j in range(4):
            source = (mixed_a, mixed_b)[j // 2]
            start = pl.multiple_of((me ^ j) * part, part)
            for h in range(heads):
                base = (h * 3 + 2) * hd
                vals[h, 0:hd, pl.ds(start, part)] = source[j % 2, base : base + hd, :]
                vals[h, hd : hd + 16, pl.ds(start, part)] = jnp.ones((16, part), BF16)

    own = pl.ds(pl.multiple_of(i * block, block), block)
    acc[...] = jnp.zeros_like(acc)

    def step(t, carry):
        there = pl.ds(pl.multiple_of(t * block, block), block)
        for h in range(heads):
            scores = mm(keys_tok[h, there, :], queries_lane[h, :, own])
            acc[h] += mm(vals[h, :, there], jnp.exp(scores).astype(BF16))
        return carry

    lax.fori_loop(pos[1 + i], pos[1 + pl.num_programs(0) + i], step, 0)
    for h in range(heads):
        total = acc[h, hd : hd + 1, :]
        out = acc[h, 0:hd, :] / total
        raw[0, h * hd : (h + 1) * hd, :] = out
        att[0, h * hd : (h + 1) * hd, :] = out.astype(BF16)
        log[0, h : h + 1, :] = jnp.log(total)


def attend_call(pos, num, mixed_a, mixed_b, heads, hd):
    part = mixed_a.shape[2]
    row = num.shape[1]
    block = min(TILE, part)
    per = part // block

    def lanes(rows):
        return pl.BlockSpec((1, rows, block), lambda i, s: ((i // per) ^ s[0], 0, i % per))

    return pl.pallas_call(
        partial(attend_kernel, heads, hd, part),
        grid_spec=pltpu.PrefetchScalarGridSpec(
            num_scalar_prefetch=1,
            grid=(row // block,),
            in_specs=[whole(num.shape), once(mixed_a.shape), once(mixed_b.shape)],
            out_specs=[lanes(heads * hd), lanes(heads * hd), lanes(8)],
            scratch_shapes=[
                pltpu.VMEM((heads, row, 2 * hd), BF16),
                pltpu.VMEM((heads, 2 * hd, row), BF16),
                pltpu.VMEM((heads, hd + 16, row), BF16),
                pltpu.VMEM((heads, hd + 16, block), F32),
            ],
        ),
        out_shape=[
            jax.ShapeDtypeStruct((4, heads * hd, part), BF16),
            jax.ShapeDtypeStruct((4, heads * hd, part), F32),
            jax.ShapeDtypeStruct((4, 8, part), F32),
        ],
        compiler_params=params(),
        cost_estimate=pl.CostEstimate(
            flops=heads * row * row * hd * 4, bytes_accessed=12 * MIB, transcendentals=0
        ),
        name="attend",
    )(pos, num, mixed_a, mixed_b)


def attend_back_kernel(
    heads,
    hd,
    part,
    pos,
    num,
    mixed_a,
    mixed_b,
    hat_a,
    hat_b,
    scale_a,
    scale_b,
    raw,
    log,
    d0,
    d1,
    d2,
    d3,
    q_gain,
    k_gain,
    out_ref,
    gain_ref,
    bias_ref,
    keys_tok,
    queries_lane,
    vals_tok,
    keys_lane,
    grads_lane,
    log_row,
    inner_row,
    d_key,
    d_val,
    d_query,
):
    i = pl.program_id(0)
    blocks = pl.num_programs(0)
    block = min(TILE, part)
    me = pos[0]
    grads = (d0, d1, d2, d3)

    @pl.when(i == 0)
    def _():
        lay_out(me, num, (mixed_a, mixed_b), heads, hd, part, keys_tok, queries_lane)
        for j in range(4):
            source = (mixed_a, mixed_b)[j // 2]
            start = pl.multiple_of((me ^ j) * part, part)
            there = pl.ds(start, part)
            log_row[:, there] = log[j]
            for h in range(heads):
                base = h * 3 * hd
                keys_lane[h, :, there] = source[j % 2, base + hd : base + 2 * hd, :]
                vals_tok[h, there, :] = (
                    source[j % 2, base + 2 * hd : base + 3 * hd, :].astype(F32).T.astype(BF16)
                )
                grad = grads[j][h * hd : (h + 1) * hd, :]
                grads_lane[h, :, there] = grad
                inner_row[h : h + 1, there] = jnp.sum(
                    grad.astype(F32) * raw[j, h * hd : (h + 1) * hd, :], axis=0, keepdims=True
                )
        d_key[...] = jnp.zeros_like(d_key)
        d_val[...] = jnp.zeros_like(d_val)

    own = pl.ds(pl.multiple_of(i * block, block), block)
    d_query[:, :, own] = jnp.zeros((heads, hd, block), F32)
    low, high = pos[1 + i], pos[1 + blocks + i]

    @pl.when(high > low)
    def _():
        queries_tok = [queries_lane[h, 0:hd, own].astype(F32).T.astype(BF16) for h in range(heads)]
        grads_tok = [grads_lane[h, :, own].astype(F32).T.astype(BF16) for h in range(heads)]

        def step(t, carry):
            there = pl.ds(pl.multiple_of(t * block, block), block)
            for h in range(heads):
                scores = mm(keys_tok[h, there, :], queries_lane[h, :, own])
                chance = jnp.exp(scores - log_row[h : h + 1, own])
                chance_grad = mm(vals_tok[h, there, :], grads_lane[h, :, own])
                score_grad = (chance * (chance_grad - inner_row[h : h + 1, own])).astype(BF16)
                d_val[h, there, :] += mm(chance.astype(BF16), grads_tok[h])
                d_key[h, there, :] += mm(score_grad, queries_tok[h])
                d_query[h, :, own] += mm(keys_lane[h, :, there], score_grad)
            return carry

        lax.fori_loop(low, high, step, 0)

    @pl.when(i == blocks - 1)
    def _():
        def fold(values):
            return sum(values[:, n * 128 : (n + 1) * 128] for n in range(values.shape[1] // 128))

        gain_ref[...] = jnp.zeros_like(gain_ref)
        bias_ref[...] = jnp.zeros_like(bias_ref)
        for j in range(4):
            hats = (hat_a, hat_b)[j // 2]
            scales = (scale_a, scale_b)[j // 2]
            start = pl.multiple_of((me ^ j) * part, part)
            there = pl.ds(start, part)
            for h in range(heads):
                for kind, a_gain in ((0, q_gain), (1, k_gain)):
                    if kind == 0:
                        grad = d_query[h, :, there] * hd**-0.5
                    else:
                        grad = d_key[h, there, :].T
                    slot = h * 2 + kind
                    hat = hats[j % 2, slot * hd : (slot + 1) * hd, :]
                    scale = scales[j % 2, slot : slot + 1, :]
                    gain_ref[kind * hd : (kind + 1) * hd, :] += fold(grad * hat)
                    inner = grad * a_gain[...]
                    back = scale * (
                        inner
                        - jnp.mean(inner, axis=0, keepdims=True)
                        - hat * jnp.mean(inner * hat, axis=0, keepdims=True)
                    )
                    rows = slice((h * 3 + kind) * hd, (h * 3 + kind + 1) * hd)
                    back = back.astype(BF16)
                    out_ref[j, rows, :] = back
                    bias_ref[rows, :] += fold(back.astype(F32))
                rows = slice((h * 3 + 2) * hd, (h * 3 + 3) * hd)
                back = d_val[h, there, :].T.astype(BF16)
                out_ref[j, rows, :] = back
                bias_ref[rows, :] += fold(back.astype(F32))


def attend_back_call(pos, num, mixed, hats, scales, raw, log, grads, q_gain, k_gain, heads, hd):
    part = mixed[0].shape[2]
    row = num.shape[1]
    block = min(TILE, part)
    wide = heads * 3 * hd
    operands = (num, *mixed, *hats, *scales, raw, log, *grads, q_gain, k_gain)
    return pl.pallas_call(
        partial(attend_back_kernel, heads, hd, part),
        grid_spec=pltpu.PrefetchScalarGridSpec(
            num_scalar_prefetch=1,
            grid=(row // block,),
            in_specs=[once(a.shape) for a in operands],
            out_specs=[once((4, wide, part)), once((2 * hd, 128)), once((wide, 128))],
            scratch_shapes=[
                pltpu.VMEM((heads, row, 2 * hd), BF16),
                pltpu.VMEM((heads, 2 * hd, row), BF16),
                pltpu.VMEM((heads, row, hd), BF16),
                pltpu.VMEM((heads, hd, row), BF16),
                pltpu.VMEM((heads, hd, row), BF16),
                pltpu.VMEM((8, row), F32),
                pltpu.VMEM((8, row), F32),
                pltpu.VMEM((heads, row, hd), F32),
                pltpu.VMEM((heads, row, hd), F32),
                pltpu.VMEM((heads, hd, row), F32),
            ],
        ),
        out_shape=[
            jax.ShapeDtypeStruct((4, wide, part), BF16),
            jax.ShapeDtypeStruct((2 * hd, 128), F32),
            jax.ShapeDtypeStruct((wide, 128), F32),
        ],
        compiler_params=params(48),
        cost_estimate=pl.CostEstimate(
            flops=heads * row * row * hd * 5, bytes_accessed=20 * MIB, transcendentals=0
        ),
        name="attend_back",
    )(pos, *operands)


def gelu_parts(x):
    size = jnp.abs(x)
    t = 1.0 / (1.0 + (0.3275911 * 2.0**-0.5) * size)
    bell = jnp.exp(-0.5 * x * x)
    poly = t * (
        0.127414796
        + t * (-0.142248368 + t * (0.7107068705 + t * (-0.7265760135 + t * 0.5307027145)))
    )
    upper = poly * bell
    below = jnp.where(x >= 0, 1.0 - upper, upper)
    return x * below, below + x * bell * 0.3989422804014327


def forward_kernel(groups, hidden, *refs):
    atts = refs[:groups]
    (tok, w_own, w_sib, out_bias, gain, shift, up_bias) = refs[groups : groups + 7]
    (stream_ref, low_ref, active_ref, slope_ref, part_ref) = refs[groups + 7 :]
    heads_here = atts[0].shape[0]
    base = 2 * hidden
    branch = None
    for j in range(groups):
        source = (w_own, w_sib)[j % 2]
        start = base + (j // 2) * heads_here
        term = mm(source[:, start : start + heads_here], atts[j][...])
        branch = term if branch is None else branch + term
    stream = tok[...].astype(F32) + branch.T + out_bias[...]
    stream_ref[...] = stream
    hat, _ = rows_hat(stream)
    low = (hat * gain[...] + shift[...]).astype(BF16)
    low_ref[...] = low
    total = None
    for n, source in enumerate((w_own, w_sib)):
        cols = slice(n * hidden, (n + 1) * hidden)
        raised = mm(low, source[:, 0:hidden]) + up_bias[:, cols]
        active, slope = gelu_parts(raised)
        active = active.astype(BF16)
        active_ref[:, cols] = active
        slope_ref[:, cols] = slope
        term = mm(active, source[:, hidden : 2 * hidden], NT)
        total = term if total is None else total + term
    part_ref[...] = total.astype(part_ref.dtype)


def forward_call(atts, tok, w_own, w_sib, out_bias, gain, shift, up_bias, hidden, part_type):
    groups = len(atts)
    part, width = tok.shape
    block = min(TILE, part)
    heads_here = atts[0].shape[0]

    def rows(cols):
        return pl.BlockSpec((block, cols), lambda i: (i, 0))

    fixed = (w_own, w_sib, out_bias, gain, shift, up_bias)
    return pl.pallas_call(
        partial(forward_kernel, groups, hidden),
        grid=(part // block,),
        in_specs=[pl.BlockSpec((heads_here, block), lambda i: (0, i))] * groups
        + [rows(width)]
        + [once(a.shape) for a in fixed],
        out_specs=[rows(width), rows(width), rows(2 * hidden), rows(2 * hidden), rows(width)],
        out_shape=[
            jax.ShapeDtypeStruct((part, width), F32),
            jax.ShapeDtypeStruct((part, width), BF16),
            jax.ShapeDtypeStruct((part, 2 * hidden), BF16),
            jax.ShapeDtypeStruct((part, 2 * hidden), F32),
            jax.ShapeDtypeStruct((part, width), part_type),
        ],
        compiler_params=params(),
        cost_estimate=pl.CostEstimate(
            flops=2 * part * width * (width + 4 * hidden), bytes_accessed=16 * MIB, transcendentals=0
        ),
        name="forward",
    )(*atts, tok, *fixed)


def backward_kernel(hidden, grad, slope, w_own, w_sib, low_ref, part_ref, bias_ref):
    @pl.when(pl.program_id(0) == 0)
    def _():
        bias_ref[...] = jnp.zeros_like(bias_ref)

    total = None
    for n, source in enumerate((w_own, w_sib)):
        cols = slice(n * hidden, (n + 1) * hidden)
        low = (mm(grad[...], source[:, hidden : 2 * hidden]) * slope[:, cols]).astype(BF16)
        low_ref[:, cols] = low
        bias_ref[:, cols] += jnp.sum(low.astype(F32), axis=0, keepdims=True)
        term = mm(low, source[:, 0:hidden], NT)
        total = term if total is None else total + term
    part_ref[...] = total.astype(part_ref.dtype)


def backward_call(grad, slope, w_own, w_sib, hidden, part_type):
    part, width = grad.shape
    block = min(TILE, part)

    def rows(cols):
        return pl.BlockSpec((block, cols), lambda i: (i, 0))

    return pl.pallas_call(
        partial(backward_kernel, hidden),
        grid=(part // block,),
        in_specs=[rows(width), rows(2 * hidden), once(w_own.shape), once(w_sib.shape)],
        out_specs=[rows(2 * hidden), rows(width), whole((1, 2 * hidden))],
        out_shape=[
            jax.ShapeDtypeStruct((part, 2 * hidden), BF16),
            jax.ShapeDtypeStruct((part, width), part_type),
            jax.ShapeDtypeStruct((1, 2 * hidden), F32),
        ],
        compiler_params=params(),
        cost_estimate=pl.CostEstimate(
            flops=2 * part * width * 4 * hidden, bytes_accessed=10 * MIB, transcendentals=0
        ),
        name="backward",
    )(grad, slope, w_own, w_sib)


def second_kernel(groups, hidden, own, other, stream, result_grad, gain, w_own, w_sib, *outs):
    grad_ref, low_ref, sums_ref = outs[:3]
    heads_refs = outs[3:]
    heads_here = heads_refs[0].shape[0]

    @pl.when(pl.program_id(0) == 0)
    def _():
        sums_ref[...] = jnp.zeros_like(sums_ref)

    second_grad = own[...] + other[...].astype(F32)
    hat, factor = rows_hat(stream[...])
    sums_ref[0:1, :] += jnp.sum(second_grad * hat, axis=0, keepdims=True)
    sums_ref[1:2, :] += jnp.sum(second_grad, axis=0, keepdims=True)
    stream_grad = result_grad[...] + rows_back(second_grad * gain[...], hat, factor)
    grad_ref[...] = stream_grad
    low = stream_grad.astype(BF16)
    low_ref[...] = low
    sums_ref[2:3, :] += jnp.sum(low.astype(F32), axis=0, keepdims=True)
    for n, source in enumerate((w_own, w_sib)):
        base = 2 * hidden
        both = mm(low, source[:, base : base + (groups // 2) * heads_here]).T
        for m in range(groups // 2):
            heads_refs[m * 2 + n][...] = both[m * heads_here : (m + 1) * heads_here].astype(BF16)


def second_call(own, other, stream, result_grad, gain, w_own, w_sib, hidden, groups, heads_here):
    part, width = own.shape
    block = min(TILE, part)
    rows = pl.BlockSpec((block, width), lambda i: (i, 0))
    lanes = pl.BlockSpec((heads_here, block), lambda i: (0, i))
    return pl.pallas_call(
        partial(second_kernel, groups, hidden),
        grid=(part // block,),
        in_specs=[rows] * 4 + [once(gain.shape), once(w_own.shape), once(w_sib.shape)],
        out_specs=[rows, rows, whole((8, width))] + [lanes] * groups,
        out_shape=[
            jax.ShapeDtypeStruct((part, width), F32),
            jax.ShapeDtypeStruct((part, width), BF16),
            jax.ShapeDtypeStruct((8, width), F32),
        ]
        + [jax.ShapeDtypeStruct((heads_here, part), BF16)] * groups,
        compiler_params=params(),
        cost_estimate=pl.CostEstimate(
            flops=2 * part * width * width, bytes_accessed=10 * MIB, transcendentals=0
        ),
        name="second_back",
    )(own, other, stream, result_grad, gain, w_own, w_sib)


def first_grad_kernel(wide, order, mixed, weight, *refs):
    count = len(order)
    toks = refs[:count]
    sums_ref = refs[count]
    outs = refs[count + 1 :]

    @pl.when(pl.program_id(0) == 0)
    def _():
        sums_ref[...] = jnp.zeros_like(sums_ref)

    for n, j in enumerate(order):
        grad = mm(weight[:, :wide], mixed[j]).T
        hat, _ = rows_hat(toks[n][...].astype(F32))
        sums_ref[0:1, :] += jnp.sum(grad * hat, axis=0, keepdims=True)
        sums_ref[1:2, :] += jnp.sum(grad, axis=0, keepdims=True)
        outs[n][...] = grad.astype(outs[n].dtype)


def first_grad_call(mixed, weight, toks, order, out_type):
    groups, wide, part = mixed.shape
    width = weight.shape[0]
    block = min(TILE, part)
    rows = pl.BlockSpec((block, width), lambda i: (i, 0))
    return pl.pallas_call(
        partial(first_grad_kernel, wide, order),
        grid=(part // block,),
        in_specs=[pl.BlockSpec((groups, wide, block), lambda i: (0, 0, i)), once(weight.shape)]
        + [rows] * len(order),
        out_specs=[whole((8, width))] + [rows] * len(order),
        out_shape=[jax.ShapeDtypeStruct((8, width), F32)]
        + [jax.ShapeDtypeStruct((part, width), out_type)] * len(order),
        compiler_params=params(),
        cost_estimate=pl.CostEstimate(
            flops=2 * len(order) * part * width * wide, bytes_accessed=8 * MIB, transcendentals=0
        ),
        name="first_grad",
    )(mixed, weight, *[toks[j] for j in order])


def first_back_kernel(own, other, tok, stream_grad, gain, out_ref):
    hat, factor = rows_hat(tok[...].astype(F32))
    grad = own[...] + other[...].astype(F32)
    out_ref[...] = stream_grad[...] + rows_back(grad * gain[...], hat, factor)


def first_back_call(own, other, tok, stream_grad, gain):
    part, width = own.shape
    block = min(TILE, part)
    rows = pl.BlockSpec((block, width), lambda i: (i, 0))
    return pl.pallas_call(
        first_back_kernel,
        grid=(part // block,),
        in_specs=[rows] * 4 + [whole(gain.shape)],
        out_specs=rows,
        out_shape=jax.ShapeDtypeStruct((part, width), F32),
        compiler_params=params(),
        cost_estimate=pl.CostEstimate(
            flops=part * width * 20, bytes_accessed=8 * MIB, transcendentals=0
        ),
        name="first_back",
    )(own, other, tok, stream_grad, gain)


def own_rows(vector, group, amount):
    return lax.dynamic_slice_in_dim(vector, group * amount, amount)


def local(
    tokens,
    teacher,
    picture_lengths,
    first_gain,
    first_shift,
    input_weight,
    input_bias,
    query_gain,
    key_gain,
    output_weight,
    output_bias,
    second_gain,
    second_shift,
    expand_weight,
    expand_bias,
    reduce_weight,
    reduce_bias,
):
    assert tokens.shape[0] == 1 and lax.axis_size("gx") == 4
    part, width = tokens.shape[1:]
    groups = 4
    row = part * groups
    group = lax.axis_index("gx")
    hd = query_gain.shape[0]
    wide = input_weight.shape[1]
    heads = wide // (3 * hd)
    heads_here = heads * hd
    hidden = expand_weight.shape[1]
    shard_rows = input_weight.shape[0]
    slots = picture_lengths.shape[1]
    block = min(TILE, part)

    tok0 = tokens[0]
    tok2 = swap(tok0, "gx", 2)
    tok1 = swap(tok0, "gx", 1)
    tok3 = swap(tok2, "gx", 1)
    toks = (tok0, tok1, tok2, tok3)
    row_total = jnp.sum(picture_lengths[0])
    digits = jnp.stack([row_total // 16, row_total % 16]).astype(BF16)
    side = jnp.zeros((shard_rows, 128 - wide % 128), BF16)
    side = lax.dynamic_update_slice(
        side, jnp.broadcast_to(digits[None, :], (shard_rows, 2)), (0, 0)
    )
    w_in = gather_rows(jnp.concatenate([input_weight, side], axis=1))
    out_shard = output_weight.T
    out_pair = swap(out_shard, "gx", 2)
    w_own = lax.all_gather(
        jnp.concatenate([expand_weight, reduce_weight.T, out_shard, out_pair], axis=1),
        ("dp", "gy"),
        axis=0,
        tiled=True,
    )
    w_sib = swap(w_own, "gx", 1)

    ends = jnp.cumsum(picture_lengths[0])
    place = jnp.arange(row, dtype=jnp.int32)
    numbers = jnp.sum((ends[None, :] <= place[:, None]).astype(jnp.int32), axis=1)
    edges = jnp.concatenate([jnp.zeros((1,), jnp.int32), ends, jnp.full((1,), row, jnp.int32)])
    first_place = place[::block]
    last_place = first_place + (block - 1)
    begin = jnp.max(jnp.where(edges[None, :-1] <= first_place[:, None], edges[None, :-1], 0), axis=1)
    until = jnp.min(jnp.where(edges[None, 1:] > last_place[:, None], edges[None, 1:], row), axis=1)
    low_tile = begin // block
    high_tile = (until + block - 1) // block
    filled = (row_total + block - 1) // block
    me = group.reshape(1).astype(jnp.int32)
    pos = jnp.concatenate([me, low_tile, high_tile])
    pos_back = jnp.concatenate([me, low_tile, jnp.minimum(high_tile, filled)])
    num = numbers.reshape(1, row)
    own_place = group * part + jnp.arange(part, dtype=jnp.int32)
    own_valid = (own_place < row_total).astype(F32)[:, None]

    q_gain = query_gain.reshape(hd, 1)
    k_gain = key_gain.reshape(hd, 1)
    gain_1 = first_gain.reshape(1, width)
    shift_1 = first_shift.reshape(1, width)
    bias_1 = own_rows(input_bias, group, wide).reshape(1, wide)

    def mixed_of(pieces):
        return mixed_call(
            pieces, gain_1, shift_1, w_in, bias_1, q_gain, k_gain, heads, hd
        )

    low_a, mixed_a, hat_a, scale_a = mixed_of(toks[:2])
    low_b, mixed_b, hat_b, scale_b = mixed_of(toks[2:])
    att, raw, log = attend_call(pos, num, mixed_a, mixed_b, heads, hd)
    count_digits = w_in[::shard_rows, wide : wide + 2].astype(F32)
    counted = jnp.sum(count_digits[:, 0] * 16.0 + count_digits[:, 1])

    att_own = [att[0]] + [swap(att[j], "gx", j) for j in range(1, 4)]
    att_pair = [att[2]] + [swap(att[j ^ 2], "gx", j) for j in range(1, 4)]

    out_bias = output_bias.reshape(1, width)
    gain_2 = second_gain.reshape(1, width)
    shift_2 = second_shift.reshape(1, width)
    up_bias = jnp.concatenate(
        [own_rows(expand_bias, group, hidden), own_rows(expand_bias, group ^ 1, hidden)]
    ).reshape(1, 2 * hidden)

    def forward_of(atts, tok, part_type):
        return forward_call(
            atts, tok, w_own, w_sib, out_bias, gain_2, shift_2, up_bias, hidden, part_type
        )

    _, low_p, active_p, slope_p, part_p = forward_of(att_pair, tok2, BF16)
    part_in = swap(part_p, "gx", 2)
    stream, low_o, active_o, slope_o, part_o = forward_of(att_own, tok0, F32)
    result = stream + (part_o + part_in.astype(F32)) + reduce_bias
    layer_output = result.astype(BF16)
    error = (result - teacher[0].astype(F32)) * own_valid
    squares = jnp.sum(error * error)
    result_grad = error * (2.0 / counted)
    reduce_low = result_grad.astype(BF16)

    reduce_pair = swap(reduce_low, "gx", 2)
    hidden_o, back_o, up_sum_o = backward_call(reduce_low, slope_o, w_own, w_sib, hidden, F32)
    hidden_p, back_p, up_sum_p = backward_call(reduce_pair, slope_p, w_own, w_sib, hidden, BF16)
    back_in = swap(back_p, "gx", 2)

    def over_tokens(left_o, right_o, left_p, right_p):
        dims = (((0,), (0,)), ((), ()))
        return mm(left_o, right_o, dims) + mm(left_p, right_p, dims)

    def weight_terms(n):
        cols = slice(n * hidden, (n + 1) * hidden)
        return jnp.concatenate(
            [
                over_tokens(low_o, hidden_o[:, cols], low_p, hidden_p[:, cols]).astype(BF16),
                over_tokens(reduce_low, active_o[:, cols], reduce_pair, active_p[:, cols]).astype(
                    BF16
                ),
            ],
            axis=1,
        )

    sib_terms = swap(weight_terms(1), "gx", 1)
    own_terms = weight_terms(0)

    stream_grad, branch_low, sums_2, *heads_grad = second_call(
        back_o, back_in, stream, result_grad, gain_2, w_own, w_sib, hidden, groups, heads_here
    )
    grads = [heads_grad[0]] + [swap(heads_grad[j], "gx", j) for j in range(1, 4)]

    def out_terms(j):
        return lax.dot_general(
            branch_low, att_own[j], (((0,), (1,)), ((), ())), preferred_element_type=F32
        )

    out_sent = jnp.concatenate([out_terms(1), out_terms(3)], axis=1).astype(BF16)
    out_held = jnp.concatenate([out_terms(0), out_terms(2)], axis=1)
    out_held = out_held + swap(out_sent, "gx", 1).astype(F32)
    out_own = out_held[:, :heads_here] + swap(
        out_held[:, heads_here:].astype(BF16), "gx", 2
    ).astype(F32)
    weight_grads = jnp.concatenate(
        [(own_terms.astype(F32) + sib_terms.astype(F32)).astype(BF16), out_own.astype(BF16)], axis=1
    )
    weight_grads = jnp.pad(weight_grads, ((0, 0), (0, -weight_grads.shape[1] % 128)))
    weight_grads = lax.psum_scatter(
        weight_grads, ("dp", "gy"), scatter_dimension=0, tiled=True
    ).astype(F32)
    expand_out = weight_grads[:, :hidden]
    reduce_out = weight_grads[:, hidden : 2 * hidden].T
    output_out = weight_grads[:, 2 * hidden : 2 * hidden + heads_here].T

    mixed_low, gain_sums, bias_sums = attend_back_call(
        pos_back,
        num,
        (mixed_a, mixed_b),
        (hat_a, hat_b),
        (scale_a, scale_b),
        raw,
        log,
        grads,
        q_gain,
        k_gain,
        heads,
        hd,
    )
    sums_s, sent_1, sent_3 = first_grad_call(mixed_low, w_in, toks, (1, 3), BF16)
    in_0 = swap(sent_1, "gx", 1)
    in_2 = swap(sent_3, "gx", 1)
    sums_k, kept_0, kept_2 = first_grad_call(mixed_low, w_in, toks, (0, 2), F32)
    pair_in = swap((kept_2 + in_2.astype(F32)).astype(BF16), "gx", 2)
    dims = (((0,), (1,)), ((), ()))
    in_terms = sum(
        mm(low[n], mixed_low[2 * m + n], dims)
        for m, low in enumerate((low_a, low_b))
        for n in range(2)
    )
    input_out = scatter_rows(in_terms, shard_rows)
    tokens_gradient = first_back_call(
        kept_0 + in_0.astype(F32), pair_in, tok0, stream_grad, gain_1
    )

    def placed(vector, start, total):
        return lax.dynamic_update_slice_in_dim(jnp.zeros((total,), F32), vector, start, 0)

    up_sum = (up_sum_o + up_sum_p)[0]
    up_total = placed(up_sum[:hidden], group * hidden, groups * hidden) + placed(
        up_sum[hidden:], (group ^ 1) * hidden, groups * hidden
    )
    early = sum_all(
        packed(
            [
                squares.reshape(1),
                up_total,
                jnp.sum(reduce_low.astype(F32), axis=0),
                sums_2[0],
                sums_2[1],
                sums_2[2],
            ]
        )
    )
    late = sum_all(
        packed(
            [
                sums_s[0] + sums_k[0],
                sums_s[1] + sums_k[1],
                placed(jnp.sum(bias_sums, axis=1), group * wide, groups * wide),
                jnp.sum(gain_sums, axis=1),
            ]
        )
    )
    total_squares, expand_bias_grad, reduce_bias_grad, gain_2_grad, shift_2_grad, out_bias_grad = (
        unpacked(early, [1, groups * hidden, width, width, width, width])
    )
    gain_1_grad, shift_1_grad, input_bias_grad, q_gain_grad, k_gain_grad = unpacked(
        late, [width, width, groups * wide, hd, hd]
    )
    return (
        layer_output[None],
        total_squares[0] / counted,
        tokens_gradient[None],
        gain_1_grad,
        shift_1_grad,
        input_out[:, :wide],
        input_bias_grad,
        q_gain_grad,
        k_gain_grad,
        output_out,
        out_bias_grad,
        gain_2_grad,
        shift_2_grad,
        expand_out,
        expand_bias_grad,
        reduce_out,
        reduce_bias_grad,
    )


def solution(mesh):
    rows = P(("dp", "gy"), "gx", None)
    by_rows = P(("dp", "gy"), "gx")
    by_cols = P("gx", ("dp", "gy"))
    return jax.shard_map(
        local,
        mesh=mesh,
        in_specs=(
            rows,
            rows,
            P(("dp", "gy"), None),
            P(),
            P(),
            by_rows,
            P(),
            P(),
            P(),
            by_cols,
            P(),
            P(),
            P(),
            by_rows,
            P(),
            by_cols,
            P(),
        ),
        out_specs=(
            rows,
            P(),
            rows,
            P(),
            P(),
            by_rows,
            P(),
            P(),
            P(),
            by_cols,
            P(),
            P(),
            P(),
            by_rows,
            P(),
            by_cols,
            P(),
        ),
        check_vma=False,
    )
```

```python
from functools import partial

import jax
import jax.numpy as jnp
from jax import lax
from jax.experimental import pallas as pl
from jax.experimental.pallas import tpu as pltpu
from jax.sharding import PartitionSpec as P

EPS = 1e-06
APART = 1024.0
TILE = 256
QUERY_TILE = 512
KEY_TILE = 512
MIB = 1 << 20
F32 = jnp.float32
BF16 = jnp.bfloat16

NN = (((1,), (0,)), ((), ()))
NT = (((1,), (1,)), ((), ()))


def mm(left, right, dims=NN):
    return lax.dot_general(left, right, dims, preferred_element_type=F32)


def took(us):
    return pl.CostEstimate(flops=int(us * 1.15e9), bytes_accessed=0, transcendentals=0)


def params(limit):
    return pltpu.CompilerParams(vmem_limit_bytes=limit * MIB)


def whole(shape):
    rank = len(shape)
    return pl.BlockSpec(shape, lambda *_: (0,) * rank)


def once(shape):
    rank = len(shape)
    return pl.BlockSpec(shape, lambda *_: (0,) * rank, pipeline_mode=pl.Buffered(1))


def rows_hat(values):
    mean = jnp.mean(values, axis=-1, keepdims=True)
    centered = values - mean
    factor = lax.rsqrt(jnp.mean(centered * centered, axis=-1, keepdims=True) + EPS)
    return centered * factor, factor


def rows_back(grad_hat, hat, factor):
    return factor * (
        grad_hat
        - jnp.mean(grad_hat, axis=-1, keepdims=True)
        - hat * jnp.mean(grad_hat * hat, axis=-1, keepdims=True)
    )


def swap(array, axis, mask):
    size = lax.axis_size(axis)
    return lax.ppermute(array, axis, [(i, i ^ mask) for i in range(size)])


def bits_of(axis):
    size = lax.axis_size(axis)
    masks = []
    mask = 1
    while mask < size:
        masks.append(mask)
        mask *= 2
    return masks


def gather_rows(shard):
    rows, cols = shard.shape
    held = shard.reshape(1, rows, cols)
    for mask in reversed(bits_of("gy")):
        mine = (lax.axis_index("gy") & mask) != 0
        other = swap(held, "gy", mask)
        held = jnp.where(
            mine, jnp.stack([other, held], axis=1), jnp.stack([held, other], axis=1)
        ).reshape(-1, rows, cols)
    for mask in bits_of("dp"):
        mine = (lax.axis_index("dp") & mask) != 0
        other = swap(held, "dp", mask)
        held = jnp.where(
            mine, jnp.concatenate([other, held]), jnp.concatenate([held, other])
        )
    return held.reshape(-1, cols)


def top_bit(axis):
    mask = bits_of(axis)[-1]
    return ((lax.axis_index(axis) & mask) != 0).astype(jnp.int32), mask


def scatter_rest(kept, come, rows):
    cols = kept.shape[1]
    steps = [("dp", mask, 0) for mask in reversed(bits_of("dp")[:-1])]
    steps += [("gy", mask, 1) for mask in bits_of("gy")]
    for axis, mask, dim in steps:
        held = (kept + come.astype(F32)).reshape(-1, rows, cols)
        bit = ((lax.axis_index(axis) & mask) != 0).astype(jnp.int32)
        halves = held.reshape((2, -1, rows, cols) if dim == 0 else (-1, 2, rows, cols))
        out = lax.dynamic_index_in_dim(halves, 1 - bit, dim, False).astype(BF16)
        kept = lax.dynamic_index_in_dim(halves, bit, dim, False).reshape(-1, cols)
        come = swap(out.reshape(-1, cols), axis, mask)
    return kept, come


def sum_all(values):
    for mask in bits_of("gx"):
        values = values + swap(values, "gx", mask)
    for axis in ("dp", "gy"):
        for mask in bits_of(axis):
            values = values + swap(values, axis, mask)
    return values


def packed(parts):
    flat = jnp.concatenate([part.reshape(-1) for part in parts])
    return jnp.pad(flat, (0, -flat.shape[0] % 1024)).reshape(-1, 128)


def unpacked(flat, shapes):
    flat = flat.reshape(-1)
    outs = []
    start = 0
    for amount in shapes:
        outs.append(flat[start : start + amount])
        start += amount
    return outs


def mixed_kernel(count, heads, hd, *refs):
    toks = refs[:count]
    gain, shift, weight, bias, q_gain, k_gain = refs[count : count + 6]
    low_ref, mixed_ref, hat_ref, scale_ref = refs[count + 6 :]
    wide = heads * 3 * hd
    for j in range(count):
        hat, _ = rows_hat(toks[j][...].astype(F32))
        low = (hat * gain[...] + shift[...]).astype(BF16)
        low_ref[j] = low
        mixed = (mm(low, weight[:, :wide]) + bias[...]).T
        scales = []
        for h in range(heads):
            for kind, a_gain, factor in ((0, q_gain, hd**-0.5), (1, k_gain, 1.0)):
                start = (h * 3 + kind) * hd
                raw = mixed[start : start + hd]
                centered = raw - jnp.mean(raw, axis=0, keepdims=True)
                scale = lax.rsqrt(jnp.mean(centered * centered, axis=0, keepdims=True) + EPS)
                unit = centered * scale
                hat_ref[j, (h * 2 + kind) * hd : (h * 2 + kind + 1) * hd, :] = unit
                scales.append(scale)
                normed = (unit * a_gain[...]).astype(BF16)
                if factor != 1.0:
                    normed = normed * jnp.asarray(factor, BF16)
                mixed_ref[j, start : start + hd, :] = normed
            start = (h * 3 + 2) * hd
            mixed_ref[j, start : start + hd, :] = mixed[start : start + hd].astype(BF16)
        for n, scale in enumerate(scales):
            scale_ref[j, n : n + 1, :] = scale


def mixed_call(pieces, gain, shift, weight, bias, q_gain, k_gain, heads, hd):
    count = len(pieces)
    part, width = pieces[0].shape
    block = min(TILE, part)
    wide = heads * 3 * hd
    piece_spec = pl.BlockSpec((block, width), lambda i: (i, 0))

    def lanes(rows):
        return pl.BlockSpec((count, rows, block), lambda i: (0, 0, i))

    scale_rows = 8 * -(-2 * heads // 8)
    return pl.pallas_call(
        partial(mixed_kernel, count, heads, hd),
        grid=(part // block,),
        in_specs=[piece_spec] * count
        + [whole(a.shape) for a in (gain, shift, weight, bias, q_gain, k_gain)],
        out_specs=[
            pl.BlockSpec((count, block, width), lambda i: (0, i, 0)),
            lanes(wide),
            lanes(heads * 2 * hd),
            lanes(scale_rows),
        ],
        out_shape=[
            jax.ShapeDtypeStruct((count, part, width), BF16),
            jax.ShapeDtypeStruct((count, wide, part), BF16),
            jax.ShapeDtypeStruct((count, heads * 2 * hd, part), F32),
            jax.ShapeDtypeStruct((count, scale_rows, part), F32),
        ],
        compiler_params=params(14),
        cost_estimate=took(3),
        name="mixed",
    )(*pieces, gain, shift, weight, bias, q_gain, k_gain)


def one_hot(num_ref, start, amount):
    place = lax.broadcasted_iota(jnp.int32, (32, amount), 0)
    return (place == num_ref[:, pl.ds(start, amount)]).astype(F32)


def lay_out(me, num_ref, sources, heads, hd, part, keys_tok, queries_lane):
    for j in range(2 * len(sources)):
        source = sources[j // 2]
        start = pl.multiple_of((me ^ j) * part, part)
        marks = one_hot(num_ref, start, part)
        away = ((marks - 1.0) * APART).astype(BF16)
        blank = jnp.zeros((32, part), F32)
        for h in range(heads):
            base = h * 3 * hd
            queries_lane[h, 0:hd, pl.ds(start, part)] = source[j % 2, base : base + hd, :]
            queries_lane[h, hd : hd + 32, pl.ds(start, part)] = away
            queries_lane[h, hd + 32 : hd + 64, pl.ds(start, part)] = blank.astype(BF16)
            key = source[j % 2, base + hd : base + 2 * hd, :].astype(F32)
            keys_tok[h, pl.ds(start, part), :] = (
                jnp.concatenate([key, marks, blank], axis=0).T.astype(BF16)
            )


def attend_kernel(
    heads, hd, part, pos, num, mixed_a, mixed_b, att, raw, log, keys_tok, queries_lane, vals, acc
):
    i = pl.program_id(0)
    block = att.shape[2]
    me = pos[0]

    @pl.when(i == 0)
    def _():
        lay_out(me, num, (mixed_a, mixed_b), heads, hd, part, keys_tok, queries_lane)
        for j in range(4):
            source = (mixed_a, mixed_b)[j // 2]
            start = pl.multiple_of((me ^ j) * part, part)
            for h in range(heads):
                base = (h * 3 + 2) * hd
                vals[h, 0:hd, pl.ds(start, part)] = source[j % 2, base : base + hd, :]
                vals[h, hd : hd + 16, pl.ds(start, part)] = jnp.ones((16, part), BF16)

    own = pl.ds(pl.multiple_of(i * block, block), block)
    acc[...] = jnp.zeros_like(acc)

    def step(t, carry):
        there = pl.ds(pl.multiple_of(t * KEY_TILE, KEY_TILE), KEY_TILE)
        scores = [mm(keys_tok[h, there, :], queries_lane[h, :, own]) for h in range(heads)]
        weights = [jnp.exp(scores[h]).astype(BF16) for h in range(heads)]
        for h in range(heads):
            acc[h] += mm(vals[h, :, there], weights[h])
        return carry

    lax.fori_loop(pos[1 + i], pos[1 + pl.num_programs(0) + i], step, 0)
    for h in range(heads):
        total = acc[h, hd : hd + 1, :]
        out = acc[h, 0:hd, :] / total
        raw[0, h * hd : (h + 1) * hd, :] = out
        att[0, h * hd : (h + 1) * hd, :] = out.astype(BF16)
        log[0, h : h + 1, :] = jnp.log(total)


def attend_call(pos, num, mixed_a, mixed_b, heads, hd):
    part = mixed_a.shape[2]
    row = num.shape[1]
    block = min(QUERY_TILE, part)
    per = part // block

    def lanes(rows):
        return pl.BlockSpec((1, rows, block), lambda i, s: ((i // per) ^ s[0], 0, i % per))

    return pl.pallas_call(
        partial(attend_kernel, heads, hd, part),
        grid_spec=pltpu.PrefetchScalarGridSpec(
            num_scalar_prefetch=1,
            grid=(row // block,),
            in_specs=[whole(num.shape), once(mixed_a.shape), once(mixed_b.shape)],
            out_specs=[lanes(heads * hd), lanes(heads * hd), lanes(8)],
            scratch_shapes=[
                pltpu.VMEM((heads, row, 2 * hd), BF16),
                pltpu.VMEM((heads, 2 * hd, row), BF16),
                pltpu.VMEM((heads, hd + 16, row), BF16),
                pltpu.VMEM((heads, hd + 16, block), F32),
            ],
        ),
        out_shape=[
            jax.ShapeDtypeStruct((4, heads * hd, part), BF16),
            jax.ShapeDtypeStruct((4, heads * hd, part), F32),
            jax.ShapeDtypeStruct((4, 8, part), F32),
        ],
        compiler_params=params(24),
        cost_estimate=took(13),
        name="attend",
    )(pos, num, mixed_a, mixed_b)


def attend_back_kernel(
    heads,
    hd,
    part,
    pos,
    num,
    mixed_a,
    mixed_b,
    hat_a,
    hat_b,
    scale_a,
    scale_b,
    raw,
    log,
    d0,
    d1,
    d2,
    d3,
    q_gain,
    k_gain,
    out_ref,
    gain_ref,
    bias_ref,
    keys_tok,
    queries_lane,
    vals_tok,
    keys_lane,
    grads_lane,
    log_row,
    inner_row,
    d_key,
    d_val,
    d_query,
):
    i = pl.program_id(0)
    blocks = pl.num_programs(0)
    block = min(QUERY_TILE, part)
    me = pos[0]
    grads = (d0, d1, d2, d3)

    @pl.when(i == 0)
    def _():
        lay_out(me, num, (mixed_a, mixed_b), heads, hd, part, keys_tok, queries_lane)
        for j in range(4):
            source = (mixed_a, mixed_b)[j // 2]
            start = pl.multiple_of((me ^ j) * part, part)
            there = pl.ds(start, part)
            log_row[:, there] = log[j]
            for h in range(heads):
                base = h * 3 * hd
                keys_lane[h, :, there] = source[j % 2, base + hd : base + 2 * hd, :]
                vals_tok[h, there, :] = (
                    source[j % 2, base + 2 * hd : base + 3 * hd, :].astype(F32).T.astype(BF16)
                )
                grad = grads[j][h * hd : (h + 1) * hd, :]
                grads_lane[h, :, there] = grad
                inner_row[h : h + 1, there] = jnp.sum(
                    grad.astype(F32) * raw[j, h * hd : (h + 1) * hd, :], axis=0, keepdims=True
                )
        d_key[...] = jnp.zeros_like(d_key)
        d_val[...] = jnp.zeros_like(d_val)

    own = pl.ds(pl.multiple_of(i * block, block), block)
    d_query[:, :, own] = jnp.zeros((heads, hd, block), F32)
    low, high = pos[1 + i], pos[1 + blocks + i]

    @pl.when(high > low)
    def _():
        queries_tok = [queries_lane[h, 0:hd, own].astype(F32).T.astype(BF16) for h in range(heads)]
        grads_tok = [grads_lane[h, :, own].astype(F32).T.astype(BF16) for h in range(heads)]

        def step(t, carry):
            there = pl.ds(pl.multiple_of(t * KEY_TILE, KEY_TILE), KEY_TILE)
            each = range(heads)
            scores = [mm(keys_tok[h, there, :], queries_lane[h, :, own]) for h in each]
            chance_grad = [mm(vals_tok[h, there, :], grads_lane[h, :, own]) for h in each]
            chance = [jnp.exp(scores[h] - log_row[h : h + 1, own]) for h in each]
            chance_low = [chance[h].astype(BF16) for h in each]
            score_grad = [
                (chance[h] * (chance_grad[h] - inner_row[h : h + 1, own])).astype(BF16)
                for h in each
            ]
            for h in each:
                d_val[h, there, :] += mm(chance_low[h], grads_tok[h])
                d_key[h, there, :] += mm(score_grad[h], queries_tok[h])
                d_query[h, :, own] += mm(keys_lane[h, :, there], score_grad[h])
            return carry

        lax.fori_loop(low, high, step, 0)

    @pl.when(i == blocks - 1)
    def _():
        def fold(values):
            return sum(values[:, n * 128 : (n + 1) * 128] for n in range(values.shape[1] // 128))

        gain_ref[...] = jnp.zeros_like(gain_ref)
        bias_ref[...] = jnp.zeros_like(bias_ref)
        for j in range(4):
            hats = (hat_a, hat_b)[j // 2]
            scales = (scale_a, scale_b)[j // 2]
            start = pl.multiple_of((me ^ j) * part, part)
            there = pl.ds(start, part)
            for h in range(heads):
                for kind, a_gain in ((0, q_gain), (1, k_gain)):
                    if kind == 0:
                        grad = d_query[h, :, there] * hd**-0.5
                    else:
                        grad = d_key[h, there, :].T
                    slot = h * 2 + kind
                    hat = hats[j % 2, slot * hd : (slot + 1) * hd, :]
                    scale = scales[j % 2, slot : slot + 1, :]
                    gain_ref[kind * hd : (kind + 1) * hd, :] += fold(grad * hat)
                    inner = grad * a_gain[...]
                    back = scale * (
                        inner
                        - jnp.mean(inner, axis=0, keepdims=True)
                        - hat * jnp.mean(inner * hat, axis=0, keepdims=True)
                    )
                    rows = slice((h * 3 + kind) * hd, (h * 3 + kind + 1) * hd)
                    back = back.astype(BF16)
                    out_ref[j, rows, :] = back
                    bias_ref[rows, :] += fold(back.astype(F32))
                rows = slice((h * 3 + 2) * hd, (h * 3 + 3) * hd)
                back = d_val[h, there, :].T.astype(BF16)
                out_ref[j, rows, :] = back
                bias_ref[rows, :] += fold(back.astype(F32))


def attend_back_call(pos, num, mixed, hats, scales, raw, log, grads, q_gain, k_gain, heads, hd):
    part = mixed[0].shape[2]
    row = num.shape[1]
    block = min(QUERY_TILE, part)
    wide = heads * 3 * hd
    operands = (num, *mixed, *hats, *scales, raw, log, *grads, q_gain, k_gain)
    return pl.pallas_call(
        partial(attend_back_kernel, heads, hd, part),
        grid_spec=pltpu.PrefetchScalarGridSpec(
            num_scalar_prefetch=1,
            grid=(row // block,),
            in_specs=[once(a.shape) for a in operands],
            out_specs=[once((4, wide, part)), once((2 * hd, 128)), once((wide, 128))],
            scratch_shapes=[
                pltpu.VMEM((heads, row, 2 * hd), BF16),
                pltpu.VMEM((heads, 2 * hd, row), BF16),
                pltpu.VMEM((heads, row, hd), BF16),
                pltpu.VMEM((heads, hd, row), BF16),
                pltpu.VMEM((heads, hd, row), BF16),
                pltpu.VMEM((8, row), F32),
                pltpu.VMEM((8, row), F32),
                pltpu.VMEM((heads, row, hd), F32),
                pltpu.VMEM((heads, row, hd), F32),
                pltpu.VMEM((heads, hd, row), F32),
            ],
        ),
        out_shape=[
            jax.ShapeDtypeStruct((4, wide, part), BF16),
            jax.ShapeDtypeStruct((2 * hd, 128), F32),
            jax.ShapeDtypeStruct((wide, 128), F32),
        ],
        compiler_params=params(46),
        cost_estimate=took(1),
        name="attend_back",
    )(pos, *operands)


def gelu_parts(x):
    size = jnp.abs(x)
    t = 1.0 / (1.0 + (0.3275911 * 2.0**-0.5) * size)
    bell = jnp.exp(-0.5 * x * x)
    poly = t * (
        0.127414796
        + t * (-0.142248368 + t * (0.7107068705 + t * (-0.7265760135 + t * 0.5307027145)))
    )
    upper = poly * bell
    below = jnp.where(x >= 0, 1.0 - upper, upper)
    return x * below, below + x * bell * 0.3989422804014327


def forward_kernel(groups, hidden, *refs):
    atts = refs[:groups]
    (tok, w_own, w_sib, out_bias, gain, shift, up_bias) = refs[groups : groups + 7]
    (stream_ref, low_ref, active_ref, slope_ref, part_ref) = refs[groups + 7 :]
    heads_here = atts[0].shape[0]
    base = 2 * hidden
    branch = None
    for j in range(groups):
        source = (w_own, w_sib)[j % 2]
        start = base + (j // 2) * heads_here
        term = mm(source[:, start : start + heads_here], atts[j][...])
        branch = term if branch is None else branch + term
    stream = tok[...].astype(F32) + branch.T + out_bias[...]
    stream_ref[...] = stream
    hat, _ = rows_hat(stream)
    low = (hat * gain[...] + shift[...]).astype(BF16)
    low_ref[...] = low
    total = None
    for n, source in enumerate((w_own, w_sib)):
        cols = slice(n * hidden, (n + 1) * hidden)
        raised = mm(low, source[:, 0:hidden]) + up_bias[:, cols]
        active, slope = gelu_parts(raised)
        active = active.astype(BF16)
        active_ref[:, cols] = active
        slope_ref[:, cols] = slope
        term = mm(active, source[:, hidden : 2 * hidden], NT)
        total = term if total is None else total + term
    part_ref[...] = total.astype(part_ref.dtype)


def forward_call(atts, tok, w_own, w_sib, out_bias, gain, shift, up_bias, hidden, part_type):
    groups = len(atts)
    part, width = tok.shape
    block = min(TILE, part)
    heads_here = atts[0].shape[0]

    def rows(cols):
        return pl.BlockSpec((block, cols), lambda i: (i, 0))

    fixed = (w_own, w_sib, out_bias, gain, shift, up_bias)
    return pl.pallas_call(
        partial(forward_kernel, groups, hidden),
        grid=(part // block,),
        in_specs=[pl.BlockSpec((heads_here, block), lambda i: (0, i))] * groups
        + [rows(width)]
        + [once(a.shape) for a in fixed],
        out_specs=[rows(width), rows(width), rows(2 * hidden), rows(2 * hidden), rows(width)],
        out_shape=[
            jax.ShapeDtypeStruct((part, width), F32),
            jax.ShapeDtypeStruct((part, width), BF16),
            jax.ShapeDtypeStruct((part, 2 * hidden), BF16),
            jax.ShapeDtypeStruct((part, 2 * hidden), F32),
            jax.ShapeDtypeStruct((part, width), part_type),
        ],
        compiler_params=params(28),
        cost_estimate=took(10),
        name="forward",
    )(*atts, tok, *fixed)


def loss_kernel(stream, own, other, bias, teacher, valid, factor, out, grad_ref, low_ref, sums_ref):
    @pl.when(pl.program_id(0) == 0)
    def _():
        sums_ref[...] = jnp.zeros_like(sums_ref)

    result = stream[...] + (own[...] + other[...].astype(F32)) + bias[...]
    out[...] = result.astype(BF16)
    error = (result - teacher[...].astype(F32)) * valid[...]
    grad = error * factor[...]
    grad_ref[...] = grad
    low = grad.astype(BF16)
    low_ref[...] = low
    sums_ref[0:1, :] += jnp.sum(error * error, axis=0, keepdims=True)
    sums_ref[1:2, :] += jnp.sum(low.astype(F32), axis=0, keepdims=True)


def loss_call(stream, own, other, bias, teacher, valid, factor):
    part, width = stream.shape
    block = min(TILE, part)
    rows = pl.BlockSpec((block, width), lambda i: (i, 0))
    return pl.pallas_call(
        loss_kernel,
        grid=(part // block,),
        in_specs=[
            rows,
            rows,
            rows,
            whole(bias.shape),
            rows,
            pl.BlockSpec((block, 1), lambda i: (i, 0)),
            whole(factor.shape),
        ],
        out_specs=[rows, rows, rows, whole((8, width))],
        out_shape=[
            jax.ShapeDtypeStruct((part, width), BF16),
            jax.ShapeDtypeStruct((part, width), F32),
            jax.ShapeDtypeStruct((part, width), BF16),
            jax.ShapeDtypeStruct((8, width), F32),
        ],
        compiler_params=params(12),
        cost_estimate=took(3),
        name="loss",
    )(stream, own, other, bias, teacher, valid, factor)


def backward_kernel(hidden, grad, slope, w_own, w_sib, low_ref, part_ref, bias_ref):
    @pl.when(pl.program_id(0) == 0)
    def _():
        bias_ref[...] = jnp.zeros_like(bias_ref)

    total = None
    for n, source in enumerate((w_own, w_sib)):
        cols = slice(n * hidden, (n + 1) * hidden)
        low = (mm(grad[...], source[:, hidden : 2 * hidden]) * slope[:, cols]).astype(BF16)
        low_ref[:, cols] = low
        bias_ref[:, cols] += jnp.sum(low.astype(F32), axis=0, keepdims=True)
        term = mm(low, source[:, 0:hidden], NT)
        total = term if total is None else total + term
    part_ref[...] = total.astype(part_ref.dtype)


def backward_call(grad, slope, w_own, w_sib, hidden, part_type):
    part, width = grad.shape
    block = min(TILE, part)

    def rows(cols):
        return pl.BlockSpec((block, cols), lambda i: (i, 0))

    return pl.pallas_call(
        partial(backward_kernel, hidden),
        grid=(part // block,),
        in_specs=[rows(width), rows(2 * hidden), once(w_own.shape), once(w_sib.shape)],
        out_specs=[rows(2 * hidden), rows(width), whole((1, 2 * hidden))],
        out_shape=[
            jax.ShapeDtypeStruct((part, 2 * hidden), BF16),
            jax.ShapeDtypeStruct((part, width), part_type),
            jax.ShapeDtypeStruct((1, 2 * hidden), F32),
        ],
        compiler_params=params(22),
        cost_estimate=took(6),
        name="backward",
    )(grad, slope, w_own, w_sib)


def second_kernel(groups, hidden, own, other, stream, result_grad, gain, w_own, w_sib, *outs):
    grad_ref, low_ref, sums_ref = outs[:3]
    heads_refs = outs[3:]
    heads_here = heads_refs[0].shape[0]

    @pl.when(pl.program_id(0) == 0)
    def _():
        sums_ref[...] = jnp.zeros_like(sums_ref)

    second_grad = own[...] + other[...].astype(F32)
    hat, factor = rows_hat(stream[...])
    sums_ref[0:1, :] += jnp.sum(second_grad * hat, axis=0, keepdims=True)
    sums_ref[1:2, :] += jnp.sum(second_grad, axis=0, keepdims=True)
    stream_grad = result_grad[...] + rows_back(second_grad * gain[...], hat, factor)
    grad_ref[...] = stream_grad
    low = stream_grad.astype(BF16)
    low_ref[...] = low
    sums_ref[2:3, :] += jnp.sum(low.astype(F32), axis=0, keepdims=True)
    for n, source in enumerate((w_own, w_sib)):
        base = 2 * hidden
        both = mm(low, source[:, base : base + (groups // 2) * heads_here]).T
        for m in range(groups // 2):
            heads_refs[m * 2 + n][...] = both[m * heads_here : (m + 1) * heads_here].astype(BF16)


def second_call(own, other, stream, result_grad, gain, w_own, w_sib, hidden, groups, heads_here):
    part, width = own.shape
    block = min(TILE, part)
    rows = pl.BlockSpec((block, width), lambda i: (i, 0))
    lanes = pl.BlockSpec((heads_here, block), lambda i: (0, i))
    return pl.pallas_call(
        partial(second_kernel, groups, hidden),
        grid=(part // block,),
        in_specs=[rows] * 4 + [once(gain.shape), once(w_own.shape), once(w_sib.shape)],
        out_specs=[rows, rows, whole((8, width))] + [lanes] * groups,
        out_shape=[
            jax.ShapeDtypeStruct((part, width), F32),
            jax.ShapeDtypeStruct((part, width), BF16),
            jax.ShapeDtypeStruct((8, width), F32),
        ]
        + [jax.ShapeDtypeStruct((heads_here, part), BF16)] * groups,
        compiler_params=params(22),
        cost_estimate=took(5),
        name="second_back",
    )(own, other, stream, result_grad, gain, w_own, w_sib)


def first_grad_kernel(wide, order, mixed, weight, *refs):
    count = len(order)
    toks = refs[:count]
    sums_ref = refs[count]
    outs = refs[count + 1 :]

    @pl.when(pl.program_id(0) == 0)
    def _():
        sums_ref[...] = jnp.zeros_like(sums_ref)

    for n, j in enumerate(order):
        grad = mm(weight[:, :wide], mixed[j]).T
        hat, _ = rows_hat(toks[n][...].astype(F32))
        sums_ref[0:1, :] += jnp.sum(grad * hat, axis=0, keepdims=True)
        sums_ref[1:2, :] += jnp.sum(grad, axis=0, keepdims=True)
        outs[n][...] = grad.astype(outs[n].dtype)


def first_grad_call(mixed, weight, toks, order, out_type):
    groups, wide, part = mixed.shape
    width = weight.shape[0]
    block = min(TILE, part)
    rows = pl.BlockSpec((block, width), lambda i: (i, 0))
    return pl.pallas_call(
        partial(first_grad_kernel, wide, order),
        grid=(part // block,),
        in_specs=[pl.BlockSpec((groups, wide, block), lambda i: (0, 0, i)), once(weight.shape)]
        + [rows] * len(order),
        out_specs=[whole((8, width))] + [rows] * len(order),
        out_shape=[jax.ShapeDtypeStruct((8, width), F32)]
        + [jax.ShapeDtypeStruct((part, width), out_type)] * len(order),
        compiler_params=params(16),
        cost_estimate=took(1),
        name="first_grad",
    )(mixed, weight, *[toks[j] for j in order])


def late_terms_kernel(bit, low_a, low_b, mixed, out_terms, sent, kept):
    total = None
    for j in range(4):
        low = (low_a, low_b)[j // 2][j % 2]
        term = mm(mixed[j], low)
        total = term if total is None else total + term
    wide = total.shape[0]

    @pl.when(pl.program_id(0) == 0)
    def _():
        sent[:, :wide] = total.T.astype(BF16)
        sent[:, wide:] = out_terms[...].astype(BF16)

    @pl.when(pl.program_id(0) == 1)
    def _():
        kept[:, :wide] = total.T
        kept[:, wide:] = out_terms[...]


def late_terms_call(lows, mixed, out_terms):
    part, width = lows[0].shape[1:]
    wide = mixed.shape[1]
    cols = wide + out_terms.shape[1]
    half = width // 2
    bit = top_bit("dp")[0].reshape(1)

    def side(i, s):
        return s[0] ^ 1 ^ i

    return pl.pallas_call(
        late_terms_kernel,
        grid_spec=pltpu.PrefetchScalarGridSpec(
            num_scalar_prefetch=1,
            grid=(2,),
            in_specs=[pl.BlockSpec((2, part, half), lambda i, s: (0, 0, side(i, s)))] * 2
            + [
                once(mixed.shape),
                pl.BlockSpec((half, out_terms.shape[1]), lambda i, s: (side(i, s), 0)),
            ],
            out_specs=[whole((half, cols)), whole((half, cols))],
        ),
        out_shape=[
            jax.ShapeDtypeStruct((half, cols), BF16),
            jax.ShapeDtypeStruct((half, cols), F32),
        ],
        compiler_params=params(20),
        cost_estimate=took(1),
        name="late_terms",
    )(bit, *lows, mixed, out_terms)


def late_final_kernel(kept, come, in_ref, out_ref):
    total = kept[...] + come[...].astype(F32)
    wide = in_ref.shape[1]
    in_ref[...] = total[:, :wide]
    out_ref[...] = total[:, wide:].T


def late_final_call(kept, come, wide):
    rows, cols = kept.shape
    return pl.pallas_call(
        late_final_kernel,
        out_shape=[
            jax.ShapeDtypeStruct((rows, wide), F32),
            jax.ShapeDtypeStruct((cols - wide, rows), F32),
        ],
        compiler_params=params(6),
        cost_estimate=took(1),
        name="late_final",
    )(kept, come)


def weight_final_kernel(grads, up_ref, down_ref):
    half = up_ref.shape[1]
    up_ref[...] = grads[:, :half].astype(F32)
    down_ref[...] = grads[:, half:].astype(F32).T


def weight_final_call(grads):
    rows, cols = grads.shape
    half = cols // 2
    return pl.pallas_call(
        weight_final_kernel,
        out_shape=[
            jax.ShapeDtypeStruct((rows, half), F32),
            jax.ShapeDtypeStruct((half, rows), F32),
        ],
        compiler_params=params(6),
        cost_estimate=took(1),
        name="weight_final",
    )(grads)


def first_back_kernel(own, other, tok, stream_grad, gain, out_ref):
    hat, factor = rows_hat(tok[...].astype(F32))
    grad = own[...] + other[...].astype(F32)
    out_ref[...] = stream_grad[...] + rows_back(grad * gain[...], hat, factor)


def first_back_call(own, other, tok, stream_grad, gain):
    part, width = own.shape
    block = min(TILE, part)
    rows = pl.BlockSpec((block, width), lambda i: (i, 0))
    return pl.pallas_call(
        first_back_kernel,
        grid=(part // block,),
        in_specs=[rows] * 4 + [whole(gain.shape)],
        out_specs=rows,
        out_shape=jax.ShapeDtypeStruct((part, width), F32),
        compiler_params=params(10),
        cost_estimate=took(1),
        name="first_back",
    )(own, other, tok, stream_grad, gain)


def placed(vector, start, total):
    return lax.dynamic_update_slice_in_dim(jnp.zeros((total,), F32), vector, start, 0)


def own_rows(vector, group, amount):
    return lax.dynamic_slice_in_dim(vector, group * amount, amount)


def local(
    tokens,
    teacher,
    picture_lengths,
    first_gain,
    first_shift,
    input_weight,
    input_bias,
    query_gain,
    key_gain,
    output_weight,
    output_bias,
    second_gain,
    second_shift,
    expand_weight,
    expand_bias,
    reduce_weight,
    reduce_bias,
):
    assert tokens.shape[0] == 1 and lax.axis_size("gx") == 4
    part, width = tokens.shape[1:]
    groups = 4
    row = part * groups
    group = lax.axis_index("gx")
    hd = query_gain.shape[0]
    wide = input_weight.shape[1]
    heads = wide // (3 * hd)
    heads_here = heads * hd
    hidden = expand_weight.shape[1]
    shard_rows = input_weight.shape[0]
    slots = picture_lengths.shape[1]

    out_shard = output_weight.T
    out_pair = swap(out_shard, "gx", 2)
    tok0, out_pair = lax.optimization_barrier((tokens[0], out_pair))
    tok2 = swap(tok0, "gx", 2)
    tok1 = swap(tok0, "gx", 1)
    tok3 = swap(tok2, "gx", 1)
    toks = (tok0, tok1, tok2, tok3)
    row_total = jnp.sum(picture_lengths[0])
    w_in = gather_rows(input_weight)
    w_own = lax.all_gather(
        jnp.concatenate([expand_weight, reduce_weight.T, out_shard, out_pair], axis=1),
        ("dp", "gy"),
        axis=0,
        tiled=True,
    )

    counted = jnp.full((8, 128), row_total, jnp.int32)
    for axis in ("dp", "gy"):
        for mask in bits_of(axis):
            counted = counted + swap(counted, axis, mask)
    counted = counted[0, 0].astype(F32)
    ends = jnp.cumsum(picture_lengths[0])
    place = jnp.arange(row, dtype=jnp.int32)
    numbers = jnp.sum((ends[None, :] <= place[:, None]).astype(jnp.int32), axis=1)
    edges = jnp.concatenate([jnp.zeros((1,), jnp.int32), ends, jnp.full((1,), row, jnp.int32)])
    query_tile = min(QUERY_TILE, part)
    first_place = place[::query_tile]
    last_place = first_place + (query_tile - 1)
    begin = jnp.max(jnp.where(edges[None, :-1] <= first_place[:, None], edges[None, :-1], 0), axis=1)
    until = jnp.min(jnp.where(edges[None, 1:] > last_place[:, None], edges[None, 1:], row), axis=1)
    low_tile = begin // KEY_TILE
    high_tile = (until + KEY_TILE - 1) // KEY_TILE
    filled = (row_total + KEY_TILE - 1) // KEY_TILE
    me = group.reshape(1).astype(jnp.int32)
    pos = jnp.concatenate([me, low_tile, high_tile])
    back_tile = jnp.where(first_place < row_total, jnp.minimum(high_tile, filled), 0)
    pos_back = jnp.concatenate([me, low_tile, back_tile])
    num = numbers.reshape(1, row)
    own_place = group * part + jnp.arange(part, dtype=jnp.int32)
    own_valid = (own_place < row_total).astype(F32)[:, None]

    q_gain = query_gain.reshape(hd, 1)
    k_gain = key_gain.reshape(hd, 1)
    gain_1 = first_gain.reshape(1, width)
    shift_1 = first_shift.reshape(1, width)
    bias_1 = own_rows(input_bias, group, wide).reshape(1, wide)

    def mixed_of(pieces):
        return mixed_call(
            pieces, gain_1, shift_1, w_in, bias_1, q_gain, k_gain, heads, hd
        )

    low_a, mixed_a, hat_a, scale_a = mixed_of(toks[:2])
    low_b, mixed_b, hat_b, scale_b = mixed_of(toks[2:])
    att, raw, log = attend_call(pos, num, mixed_a, mixed_b, heads, hd)
    w_own, att = lax.optimization_barrier((w_own, att))
    w_sib = swap(w_own, "gx", 1)

    att_pair = [att[2]] + [swap(att[j ^ 2], "gx", j) for j in range(1, 4)]
    att, *att_pair = lax.optimization_barrier((att, *att_pair))
    att_own = [att[0]] + [swap(att[j], "gx", j) for j in range(1, 4)]

    out_bias = output_bias.reshape(1, width)
    gain_2 = second_gain.reshape(1, width)
    shift_2 = second_shift.reshape(1, width)
    up_bias = jnp.concatenate(
        [own_rows(expand_bias, group, hidden), own_rows(expand_bias, group ^ 1, hidden)]
    ).reshape(1, 2 * hidden)

    def forward_of(atts, tok, part_type):
        return forward_call(
            atts, tok, w_own, w_sib, out_bias, gain_2, shift_2, up_bias, hidden, part_type
        )

    _, low_p, active_p, slope_p, part_p = forward_of(att_pair, tok2, BF16)
    part_in = swap(part_p, "gx", 2)
    stream, low_o, active_o, slope_o, part_o = forward_of(att_own, tok0, F32)
    layer_output, result_grad, reduce_low, sums_3 = loss_call(
        stream,
        part_o,
        part_in,
        reduce_bias.reshape(1, width),
        teacher[0],
        own_valid,
        (2.0 / counted).reshape(1, 1),
    )

    reduce_pair = swap(reduce_low, "gx", 2)
    hidden_o, back_o, up_sum_o = backward_call(reduce_low, slope_o, w_own, w_sib, hidden, F32)
    hidden_p, back_p, up_sum_p = backward_call(reduce_pair, slope_p, w_own, w_sib, hidden, BF16)
    back_in = swap(back_p, "gx", 2)

    def over_tokens(left_o, right_o, left_p, right_p):
        dims = (((0,), (0,)), ((), ()))
        return mm(left_o, right_o, dims) + mm(left_p, right_p, dims)

    def terms_of(n):
        cols = slice(n * hidden, (n + 1) * hidden)
        return jnp.concatenate(
            [
                over_tokens(low_o, hidden_o[:, cols], low_p, hidden_p[:, cols]).astype(BF16),
                over_tokens(reduce_low, active_o[:, cols], reduce_pair, active_p[:, cols]).astype(
                    BF16
                ),
            ],
            axis=1,
        )

    sib_terms = swap(terms_of(1), "gx", 1)
    own_terms = terms_of(0)
    weight_terms = (own_terms.astype(F32) + sib_terms.astype(F32)).astype(BF16)

    back_in, weight_terms = lax.optimization_barrier((back_in, weight_terms))
    stream_grad, branch_low, sums_2, *heads_grad = second_call(
        back_o, back_in, stream, result_grad, gain_2, w_own, w_sib, hidden, groups, heads_here
    )
    grads = [heads_grad[0]] + [swap(heads_grad[j], "gx", j) for j in range(1, 4)]

    def out_terms(j):
        return lax.dot_general(
            branch_low, att_own[j], (((0,), (1,)), ((), ())), preferred_element_type=F32
        )

    out_sent = jnp.concatenate([out_terms(1), out_terms(3)], axis=1).astype(BF16)
    out_held = jnp.concatenate([out_terms(0), out_terms(2)], axis=1)
    out_held = out_held + swap(out_sent, "gx", 1).astype(F32)
    out_own = out_held[:, :heads_here] + swap(
        out_held[:, heads_here:].astype(BF16), "gx", 2
    ).astype(F32)
    up_sum = (up_sum_o + up_sum_p)[0]
    up_total = placed(up_sum[:hidden], group * hidden, groups * hidden) + placed(
        up_sum[hidden:], (group ^ 1) * hidden, groups * hidden
    )
    early_sums = packed(
        [
            up_total,
            sums_3[1],
            sums_2[0],
            sums_2[1],
            sums_2[2],
            jnp.full((128,), jnp.sum(sums_3[0]) / 128),
        ]
    )
    early_sums, *grads = lax.optimization_barrier((early_sums, *grads))
    expand_out, reduce_out = weight_final_call(
        lax.psum_scatter(weight_terms, ("dp", "gy"), scatter_dimension=0, tiled=True)
    )

    mixed_low, gain_sums, bias_sums = attend_back_call(
        pos_back,
        num,
        (mixed_a, mixed_b),
        (hat_a, hat_b),
        (scale_a, scale_b),
        raw,
        log,
        grads,
        q_gain,
        k_gain,
        heads,
        hd,
    )
    sums_s, sent_1, sent_3 = first_grad_call(mixed_low, w_in, toks, (1, 3), BF16)
    in_0 = swap(sent_1, "gx", 1)
    in_2 = swap(sent_3, "gx", 1)
    mixed_low, sent_3 = lax.optimization_barrier((mixed_low, sent_3))
    late_sent, late_kept = late_terms_call((low_a, low_b), mixed_low, out_own)
    mixed_low, late_sent = lax.optimization_barrier((mixed_low, late_sent))
    come = swap(late_sent, "dp", top_bit("dp")[1])
    sums_k, kept_0, kept_2 = first_grad_call(mixed_low, w_in, toks, (0, 2), F32)
    pair_in = swap((kept_2 + in_2.astype(F32)).astype(BF16), "gx", 2)
    tokens_gradient = first_back_call(
        kept_0 + in_0.astype(F32), pair_in, tok0, stream_grad, gain_1
    )

    late_sums = packed(
        [
            sums_s[0] + sums_k[0],
            sums_s[1] + sums_k[1],
            placed(jnp.sum(bias_sums, axis=1), group * wide, groups * wide),
            jnp.sum(gain_sums, axis=1),
        ]
    )
    sums = jnp.concatenate([early_sums, late_sums])
    come, sums = lax.optimization_barrier((come, sums))
    input_out, output_out = late_final_call(*scatter_rest(late_kept, come, shard_rows), wide)
    sums = sum_all(sums)
    expand_bias_grad, reduce_bias_grad, gain_2_grad, shift_2_grad, out_bias_grad, squares = unpacked(
        sums[: early_sums.shape[0]], [groups * hidden, width, width, width, width, 128]
    )
    gain_1_grad, shift_1_grad, input_bias_grad, q_gain_grad, k_gain_grad = unpacked(
        sums[early_sums.shape[0] :], [width, width, groups * wide, hd, hd]
    )
    return (
        layer_output[None],
        jnp.sum(squares) / counted,
        tokens_gradient[None],
        gain_1_grad,
        shift_1_grad,
        input_out,
        input_bias_grad,
        q_gain_grad,
        k_gain_grad,
        output_out,
        out_bias_grad,
        gain_2_grad,
        shift_2_grad,
        expand_out,
        expand_bias_grad,
        reduce_out,
        reduce_bias_grad,
    )


def solution(mesh):
    rows = P(("dp", "gy"), "gx", None)
    by_rows = P(("dp", "gy"), "gx")
    by_cols = P("gx", ("dp", "gy"))
    return jax.shard_map(
        local,
        mesh=mesh,
        in_specs=(
            rows,
            rows,
            P(("dp", "gy"), None),
            P(),
            P(),
            by_rows,
            P(),
            P(),
            P(),
            by_cols,
            P(),
            P(),
            P(),
            by_rows,
            P(),
            by_cols,
            P(),
        ),
        out_specs=(
            rows,
            P(),
            rows,
            P(),
            P(),
            by_rows,
            P(),
            P(),
            P(),
            by_cols,
            P(),
            P(),
            P(),
            by_rows,
            P(),
            by_cols,
            P(),
        ),
        check_vma=False,
    )
```

```python
from functools import partial

import jax
import jax.numpy as jnp
from jax import lax
from jax.experimental import pallas as pl
from jax.experimental.pallas import tpu as pltpu
from jax.sharding import PartitionSpec as P

EPS = 1e-06
APART = 1024.0
TILE = 256
KEY_TILE = 512
MIB = 1 << 20
F32 = jnp.float32
BF16 = jnp.bfloat16

NN = (((1,), (0,)), ((), ()))
NT = (((1,), (1,)), ((), ()))


def mm(left, right, dims=NN):
    return lax.dot_general(left, right, dims, preferred_element_type=F32)


def took(us):
    return pl.CostEstimate(flops=int(us * 1.15e9), bytes_accessed=0, transcendentals=0)


def params(limit):
    return pltpu.CompilerParams(vmem_limit_bytes=limit * MIB)


def whole(shape):
    rank = len(shape)
    return pl.BlockSpec(shape, lambda *_: (0,) * rank)


def inside():
    return pl.BlockSpec(memory_space=pltpu.VMEM)


def once(shape):
    rank = len(shape)
    return pl.BlockSpec(shape, lambda *_: (0,) * rank, pipeline_mode=pl.Buffered(1))


def rows_hat(values):
    mean = jnp.mean(values, axis=-1, keepdims=True)
    centered = values - mean
    factor = lax.rsqrt(jnp.mean(centered * centered, axis=-1, keepdims=True) + EPS)
    return centered * factor, factor


def rows_back(grad_hat, hat, factor):
    return factor * (
        grad_hat
        - jnp.mean(grad_hat, axis=-1, keepdims=True)
        - hat * jnp.mean(grad_hat * hat, axis=-1, keepdims=True)
    )


def swap(array, axis, mask):
    size = lax.axis_size(axis)
    return lax.ppermute(array, axis, [(i, i ^ mask) for i in range(size)])


def bits_of(axis):
    size = lax.axis_size(axis)
    masks = []
    mask = 1
    while mask < size:
        masks.append(mask)
        mask *= 2
    return masks


def order_kernel(blocks, rows, pos, *refs):
    pieces, out = refs[:-1], refs[-1]
    count = len(pieces)
    for j in range(count):
        for d in range(blocks):
            start = pl.multiple_of((d * count + (pos[0] ^ j)) * rows, rows)
            out[pl.ds(start, rows), :] = pieces[j][d * rows : (d + 1) * rows, :]


def ordered(pieces, rows, me):
    height, cols = pieces[0].shape
    count = len(pieces)
    if rows % 16:
        out = jnp.zeros((height // rows, count, rows, cols), pieces[0].dtype)
        for j, piece in enumerate(pieces):
            piece = piece.reshape(-1, 1, rows, cols)
            out = lax.dynamic_update_slice(out, piece, (0, me ^ j, 0, 0))
        return out.reshape(height * count, cols)
    return pl.pallas_call(
        partial(order_kernel, height // rows, rows),
        grid_spec=pltpu.PrefetchScalarGridSpec(
            num_scalar_prefetch=1,
            grid=(1,),
            in_specs=[whole((height, cols))] * count,
            out_specs=whole((height * count, cols)),
        ),
        out_shape=jax.ShapeDtypeStruct((height * count, cols), pieces[0].dtype),
        compiler_params=params(10),
        cost_estimate=took(1),
        name="ordered",
    )(me.reshape(1).astype(jnp.int32), *pieces)


def joined(axis, mask, held, rows, *earlier):
    mine = ((lax.axis_index(axis) & mask) != 0).astype(jnp.int32)
    return ordered([held, after(swap(held, axis, mask), *earlier)], rows, mine)


def along_gy(held, rows, *earlier):
    for mask in reversed(bits_of("gy")):
        held = joined("gy", mask, held, rows, *earlier)
    return held


def along_dp(held, *earlier):
    for mask in bits_of("dp"):
        held = joined("dp", mask, held, held.shape[0], *earlier)
    return held


def top_bit(axis):
    mask = bits_of(axis)[-1]
    return ((lax.axis_index(axis) & mask) != 0).astype(jnp.int32), mask


def step_kernel(blocks, rows, bit, kept, come, out, keep):
    for d in range(blocks):
        for side in range(2):
            span = slice((2 * d + side) * rows, (2 * d + side + 1) * rows)
            total = kept[span, :] + come[span, :].astype(F32)
            to = slice(d * rows, (d + 1) * rows)

            @pl.when(bit[0] == side)
            def _():
                keep[to, :] = total

            @pl.when(bit[0] != side)
            def _():
                out[to, :] = total.astype(BF16)


def step_call(bit, kept, come, rows):
    height, cols = kept.shape
    half = (height // 2, cols)
    return pl.pallas_call(
        partial(step_kernel, height // (2 * rows), rows),
        grid_spec=pltpu.PrefetchScalarGridSpec(
            num_scalar_prefetch=1,
            grid=(1,),
            in_specs=[whole(kept.shape)] * 2,
            out_specs=[whole(half)] * 2,
        ),
        out_shape=[jax.ShapeDtypeStruct(half, BF16), jax.ShapeDtypeStruct(half, F32)],
        compiler_params=params(12),
        cost_estimate=took(1),
        name="scatter_step",
    )(bit.reshape(1), kept, come)


def halved(axis, mask, kept, come, rows):
    bit = ((lax.axis_index(axis) & mask) != 0).astype(jnp.int32)
    out, kept = step_call(bit, kept, come, rows)
    return kept, swap(out, axis, mask)


def after(value, *earlier):
    return lax.optimization_barrier((value, *earlier))[0]


def sum_over(values, axis):
    for mask in bits_of(axis):
        values = values + swap(values, axis, mask)
    return values


GAIN_1, SHIFT_1, GAIN_2, SHIFT_2, OUT_BIAS, DOWN_BIAS, UP_BIAS, UP_BIAS_SIB, IN_BIAS = range(9)


def line(table, row):
    return table[row : row + 1, :]


def pack_kernel(groups, me, up_o, up_p, early_2, early_3, late_s, late_k, bias, gains, out):
    width = out.shape[1]
    wide = bias.shape[0]
    out[...] = jnp.zeros_like(out)
    up = up_o[...] + up_p[...]
    out[pl.ds(me[0], 1), :] = up[:, :width]
    out[pl.ds(me[0] ^ 1, 1), :] = up[:, width:]
    out[pl.ds(groups + me[0], 1), 0:wide] = jnp.sum(bias[...].T, axis=0, keepdims=True)
    row = 2 * groups
    out[row : row + 3, :] = early_2[0:3, :]
    out[row + 3 : row + 5, :] = early_3[0:2, :]
    out[row + 5 : row + 7, :] = late_s[0:2, :] + late_k[0:2, :]
    out[row + 7 : row + 8, 0 : gains.shape[0]] = jnp.sum(gains[...].T, axis=0, keepdims=True)


def pack_call(me, groups, *parts):
    width = parts[2].shape[1]
    return pl.pallas_call(
        partial(pack_kernel, groups),
        grid_spec=pltpu.PrefetchScalarGridSpec(
            num_scalar_prefetch=1,
            grid=(1,),
            in_specs=[whole(a.shape) for a in parts],
            out_specs=whole((2 * groups + 8, width)),
        ),
        out_shape=jax.ShapeDtypeStruct((2 * groups + 8, width), F32),
        compiler_params=params(6),
        cost_estimate=took(1),
        name="pack",
    )(me, *parts)


def mixed_kernel(count, heads, hd, *refs):
    toks = refs[:count]
    table, weight, gains = refs[count : count + 3]
    low_ref, mixed_ref, hat_ref, scale_ref = refs[count + 3 :]
    wide = heads * 3 * hd
    gain, shift, bias = line(table, GAIN_1), line(table, SHIFT_1), line(table, IN_BIAS)[:, :wide]
    q_gain, k_gain = gains[:, 0:1], gains[:, 1:2]
    for j in range(count):
        hat, _ = rows_hat(toks[j][...].astype(F32))
        low = (hat * gain + shift).astype(BF16)
        low_ref[j] = low
        mixed = (mm(low, weight[...]) + bias).T
        scales = []
        for h in range(heads):
            for kind, a_gain, factor in ((0, q_gain, hd**-0.5), (1, k_gain, 1.0)):
                start = (h * 3 + kind) * hd
                raw = mixed[start : start + hd]
                centered = raw - jnp.mean(raw, axis=0, keepdims=True)
                scale = lax.rsqrt(jnp.mean(centered * centered, axis=0, keepdims=True) + EPS)
                unit = centered * scale
                hat_ref[j, (h * 2 + kind) * hd : (h * 2 + kind + 1) * hd, :] = unit
                scales.append(scale)
                normed = (unit * a_gain).astype(BF16)
                if factor != 1.0:
                    normed = normed * jnp.asarray(factor, BF16)
                mixed_ref[j, start : start + hd, :] = normed
            start = (h * 3 + 2) * hd
            mixed_ref[j, start : start + hd, :] = mixed[start : start + hd].astype(BF16)
        for n, scale in enumerate(scales):
            scale_ref[j, n : n + 1, :] = scale


def mixed_call(pieces, table, weight, gains, heads, hd):
    count = len(pieces)
    part, width = pieces[0].shape
    block = min(TILE, part)
    wide = heads * 3 * hd
    piece_spec = pl.BlockSpec((block, width), lambda i: (i, 0))

    def lanes(rows):
        return pl.BlockSpec((count, rows, block), lambda i: (0, 0, i))

    scale_rows = 8 * -(-2 * heads // 8)
    return pl.pallas_call(
        partial(mixed_kernel, count, heads, hd),
        grid=(part // block,),
        in_specs=[piece_spec] * count
        + [whole(a.shape) for a in (table, weight, gains)],
        out_specs=[
            pl.BlockSpec((count, block, width), lambda i: (0, i, 0)),
            lanes(wide),
            lanes(heads * 2 * hd),
            lanes(scale_rows),
        ],
        out_shape=[
            jax.ShapeDtypeStruct((count, part, width), BF16),
            jax.ShapeDtypeStruct((count, wide, part), BF16),
            jax.ShapeDtypeStruct((count, heads * 2 * hd, part), F32),
            jax.ShapeDtypeStruct((count, scale_rows, part), F32),
        ],
        compiler_params=params(24),
        cost_estimate=took(6),
        name="mixed",
    )(*pieces, table, weight, gains)


def picture_ends(lengths):
    ends = []
    total = jnp.int32(0)
    for k in range(lengths.shape[0]):
        total = total + lengths[k]
        ends.append(total)
    return ends


def key_tiles(ends, first, amount, row):
    begin, until = jnp.int32(0), jnp.int32(row)
    for end in ends:
        begin = jnp.where(end <= first, end, begin)
    for end in reversed(ends):
        until = jnp.where(end >= first + amount, end, until)
    return lax.div(begin, KEY_TILE), lax.div(until + KEY_TILE - 1, KEY_TILE)


def one_hot(ends, start, amount):
    place = start + lax.broadcasted_iota(jnp.int32, (1, amount), 1)
    number = jnp.zeros((1, amount), jnp.int32)
    for end in ends:
        number = number + (end <= place).astype(jnp.int32)
    return (lax.broadcasted_iota(jnp.int32, (32, amount), 0) == number).astype(F32)


def lay_out(me, ends, source, heads, hd, part, keys_tok, queries_lane):
    for j in range(4):
        start = pl.multiple_of((me ^ j) * part, part)
        marks = one_hot(ends, start, part)
        away = ((marks - 1.0) * APART).astype(BF16)
        blank = jnp.zeros((32, part), F32)
        for h in range(heads):
            base = h * 3 * hd
            queries_lane[h, 0:hd, pl.ds(start, part)] = source[j, base : base + hd, :]
            queries_lane[h, hd : hd + 32, pl.ds(start, part)] = away
            queries_lane[h, hd + 32 : hd + 64, pl.ds(start, part)] = blank.astype(BF16)
            key = source[j, base + hd : base + 2 * hd, :].astype(F32)
            keys_tok[h, pl.ds(start, part), :] = (
                jnp.concatenate([key, marks, blank], axis=0).T.astype(BF16)
            )


def attend_kernel(
    heads, hd, part, pos, lens, mixed, a0, a1, a2, a3, raw, log, keys_tok, queries_lane, vals, acc
):
    i = pl.program_id(0)
    block = part
    me = pos[0]
    ends = picture_ends(lens)

    @pl.when(i == 0)
    def _():
        lay_out(me, ends, mixed, heads, hd, part, keys_tok, queries_lane)
        for j in range(4):
            start = pl.multiple_of((me ^ j) * part, part)
            for h in range(heads):
                base = (h * 3 + 2) * hd
                vals[h, 0:hd, pl.ds(start, part)] = mixed[j, base : base + hd, :]
                vals[h, hd : hd + 16, pl.ds(start, part)] = jnp.ones((16, part), BF16)

    own = pl.ds(pl.multiple_of(i * block, block), block)
    acc[...] = jnp.zeros_like(acc)

    def step(t, carry):
        there = pl.ds(pl.multiple_of(t * KEY_TILE, KEY_TILE), KEY_TILE)
        scores = [mm(keys_tok[h, there, :], queries_lane[h, :, own]) for h in range(heads)]
        weights = [jnp.exp(scores[h]).astype(BF16) for h in range(heads)]
        for h in range(heads):
            acc[h] += mm(vals[h, :, there], weights[h])
        return carry

    low, high = key_tiles(ends, i * block, block, 4 * part)
    lax.fori_loop(low, high, step, 0)
    for h in range(heads):
        total = acc[h, hd : hd + 1, :]
        raw[0, h * hd : (h + 1) * hd, :] = acc[h, 0:hd, :] / total
        log[0, h : h + 1, :] = jnp.log(total)
    for j, att in enumerate((a0, a1, a2, a3)):

        @pl.when((i ^ me) == j)
        def _():
            att[...] = raw[0].astype(BF16)


def attend_call(me, lengths, mixed, heads, hd):
    part = mixed.shape[2]
    row = 4 * part

    def lanes(rows):
        return pl.BlockSpec((1, rows, part), lambda i, s, n: (i ^ s[0], 0, 0))

    return pl.pallas_call(
        partial(attend_kernel, heads, hd, part),
        grid_spec=pltpu.PrefetchScalarGridSpec(
            num_scalar_prefetch=2,
            grid=(4,),
            in_specs=[inside()],
            out_specs=[once((heads * hd, part))] * 4 + [lanes(heads * hd), lanes(8)],
            scratch_shapes=[
                pltpu.VMEM((heads, row, 2 * hd), BF16),
                pltpu.VMEM((heads, 2 * hd, row), BF16),
                pltpu.VMEM((heads, hd + 16, row), BF16),
                pltpu.VMEM((heads, hd + 16, part), F32),
            ],
        ),
        out_shape=[jax.ShapeDtypeStruct((heads * hd, part), BF16)] * 4
        + [
            jax.ShapeDtypeStruct((4, heads * hd, part), F32),
            jax.ShapeDtypeStruct((4, 8, part), F32),
        ],
        compiler_params=params(20),
        cost_estimate=took(11),
        name="attend",
    )(me, lengths, mixed)


def attend_back_kernel(
    heads,
    hd,
    part,
    pos,
    lens,
    mixed,
    hats,
    scales,
    raw,
    log,
    d0,
    d1,
    d2,
    d3,
    gains,
    out_ref,
    gain_ref,
    bias_ref,
    keys_tok,
    queries_lane,
    vals_tok,
    keys_lane,
    grads_lane,
    log_row,
    inner_row,
    d_key,
    d_val,
    d_query,
):
    i = pl.program_id(0)
    blocks = pl.num_programs(0)
    block = part
    me = pos[0]
    grads = (d0, d1, d2, d3)
    ends = picture_ends(lens)
    q_gain, k_gain = gains[:, 0:1], gains[:, 1:2]

    @pl.when(i == 0)
    def _():
        lay_out(me, ends, mixed, heads, hd, part, keys_tok, queries_lane)
        for j in range(4):
            start = pl.multiple_of((me ^ j) * part, part)
            there = pl.ds(start, part)
            log_row[:, there] = log[j]
            for h in range(heads):
                base = h * 3 * hd
                keys_lane[h, :, there] = mixed[j, base + hd : base + 2 * hd, :]
                vals_tok[h, there, :] = (
                    mixed[j, base + 2 * hd : base + 3 * hd, :].astype(F32).T.astype(BF16)
                )
                grad = grads[j][h * hd : (h + 1) * hd, :]
                grads_lane[h, :, there] = grad
                inner_row[h : h + 1, there] = jnp.sum(
                    grad.astype(F32) * raw[j, h * hd : (h + 1) * hd, :], axis=0, keepdims=True
                )
        d_key[...] = jnp.zeros_like(d_key)
        d_val[...] = jnp.zeros_like(d_val)

    own = pl.ds(pl.multiple_of(i * block, block), block)
    d_query[:, :, own] = jnp.zeros((heads, hd, block), F32)
    low, high = key_tiles(ends, i * block, block, 4 * part)
    high = jnp.minimum(high, lax.div(ends[-1] + KEY_TILE - 1, KEY_TILE))

    @pl.when((i * block < ends[-1]) & (high > low))
    def _():
        queries_tok = [queries_lane[h, 0:hd, own].astype(F32).T.astype(BF16) for h in range(heads)]
        grads_tok = [grads_lane[h, :, own].astype(F32).T.astype(BF16) for h in range(heads)]

        def step(t, carry):
            there = pl.ds(pl.multiple_of(t * KEY_TILE, KEY_TILE), KEY_TILE)
            each = range(heads)
            scores = [mm(keys_tok[h, there, :], queries_lane[h, :, own]) for h in each]
            chance_grad = [mm(vals_tok[h, there, :], grads_lane[h, :, own]) for h in each]
            chance = [jnp.exp(scores[h] - log_row[h : h + 1, own]) for h in each]
            chance_low = [chance[h].astype(BF16) for h in each]
            score_grad = [
                (chance[h] * (chance_grad[h] - inner_row[h : h + 1, own])).astype(BF16)
                for h in each
            ]
            for h in each:
                d_val[h, there, :] += mm(chance_low[h], grads_tok[h])
                d_key[h, there, :] += mm(score_grad[h], queries_tok[h])
                d_query[h, :, own] += mm(keys_lane[h, :, there], score_grad[h])
            return carry

        lax.fori_loop(low, high, step, 0)

    @pl.when(i == blocks - 1)
    def _():
        def fold(values):
            return sum(values[:, n * 128 : (n + 1) * 128] for n in range(values.shape[1] // 128))

        gain_ref[...] = jnp.zeros_like(gain_ref)
        bias_ref[...] = jnp.zeros_like(bias_ref)
        for j in range(4):
            start = pl.multiple_of((me ^ j) * part, part)
            there = pl.ds(start, part)
            for h in range(heads):
                for kind, a_gain in ((0, q_gain), (1, k_gain)):
                    if kind == 0:
                        grad = d_query[h, :, there] * hd**-0.5
                    else:
                        grad = d_key[h, there, :].T
                    slot = h * 2 + kind
                    hat = hats[j, slot * hd : (slot + 1) * hd, :]
                    scale = scales[j, slot : slot + 1, :]
                    gain_ref[kind * hd : (kind + 1) * hd, :] += fold(grad * hat)
                    inner = grad * a_gain
                    back = scale * (
                        inner
                        - jnp.mean(inner, axis=0, keepdims=True)
                        - hat * jnp.mean(inner * hat, axis=0, keepdims=True)
                    )
                    rows = slice((h * 3 + kind) * hd, (h * 3 + kind + 1) * hd)
                    back = back.astype(BF16)
                    out_ref[j, rows, :] = back
                    bias_ref[rows, :] += fold(back.astype(F32))
                rows = slice((h * 3 + 2) * hd, (h * 3 + 3) * hd)
                back = d_val[h, there, :].T.astype(BF16)
                out_ref[j, rows, :] = back
                bias_ref[rows, :] += fold(back.astype(F32))


def attend_back_call(me, lengths, mixed, hats, scales, raw, log, grads, gains, heads, hd):
    part = mixed.shape[2]
    row = 4 * part
    wide = heads * 3 * hd
    operands = (mixed, hats, scales, raw, log, *grads, gains)
    return pl.pallas_call(
        partial(attend_back_kernel, heads, hd, part),
        grid_spec=pltpu.PrefetchScalarGridSpec(
            num_scalar_prefetch=2,
            grid=(4,),
            in_specs=[inside() for a in operands],
            out_specs=[once((4, wide, part)), once((2 * hd, 128)), once((wide, 128))],
            scratch_shapes=[
                pltpu.VMEM((heads, row, 2 * hd), BF16),
                pltpu.VMEM((heads, 2 * hd, row), BF16),
                pltpu.VMEM((heads, row, hd), BF16),
                pltpu.VMEM((heads, hd, row), BF16),
                pltpu.VMEM((heads, hd, row), BF16),
                pltpu.VMEM((8, row), F32),
                pltpu.VMEM((8, row), F32),
                pltpu.VMEM((heads, row, hd), F32),
                pltpu.VMEM((heads, row, hd), F32),
                pltpu.VMEM((heads, hd, row), F32),
            ],
        ),
        out_shape=[
            jax.ShapeDtypeStruct((4, wide, part), BF16),
            jax.ShapeDtypeStruct((2 * hd, 128), F32),
            jax.ShapeDtypeStruct((wide, 128), F32),
        ],
        compiler_params=params(36),
        cost_estimate=took(1),
        name="attend_back",
    )(me, lengths, *operands)


def gelu_parts(x):
    size = jnp.abs(x)
    t = 1.0 / (1.0 + (0.3275911 * 2.0**-0.5) * size)
    bell = jnp.exp(-0.5 * x * x)
    poly = t * (
        0.127414796
        + t * (-0.142248368 + t * (0.7107068705 + t * (-0.7265760135 + t * 0.5307027145)))
    )
    upper = poly * bell
    below = jnp.where(x >= 0, 1.0 - upper, upper)
    return x * below, below + x * bell * 0.3989422804014327


def forward_kernel(groups, hidden, to_send, *refs):
    atts = refs[:groups]
    tok, w_own, w_sib, table = refs[groups : groups + 4]
    stream_ref, low_ref, active_ref, slope_ref, *part_refs = refs[groups + 4 :]
    heads_here = atts[0].shape[0]
    branch = None
    for j in range(groups):
        start = 2 * hidden + (j // 2) * heads_here
        term = mm((w_own, w_sib)[j % 2][:, start : start + heads_here], atts[j][...])
        branch = term if branch is None else branch + term
    stream = tok[...].astype(F32) + branch.T + line(table, OUT_BIAS)
    stream_ref[...] = stream
    hat, _ = rows_hat(stream)
    low = (hat * line(table, GAIN_2) + line(table, SHIFT_2)).astype(BF16)
    low_ref[...] = low
    total = None
    for n, source in enumerate((w_own, w_sib)):
        cols = slice(n * hidden, (n + 1) * hidden)
        raised = mm(low, source[:, :hidden]) + line(table, UP_BIAS + n)[:, :hidden]
        active, slope = gelu_parts(raised)
        active = active.astype(BF16)
        active_ref[:, cols] = active
        slope_ref[:, cols] = slope
        term = mm(active, source[:, hidden : 2 * hidden], NT)
        total = term if total is None else total + term
    if to_send:
        for n, part_ref in enumerate(part_refs):

            @pl.when(pl.program_id(0) == n)
            def _():
                part_ref[...] = total.astype(BF16)

    else:
        part_refs[0][...] = total
        part_refs[1][...] = w_own[:, 2 * hidden :]
        part_refs[2][...] = w_sib[:, 2 * hidden :]


def forward_call(atts, tok, w_own, w_sib, table, hidden, to_send):
    groups = len(atts)
    part, width = tok.shape
    block = min(TILE, part)
    heads_here = atts[0].shape[0]

    def rows(cols):
        return pl.BlockSpec((block, cols), lambda i: (i, 0))

    fixed = (w_own, w_sib, table)
    return pl.pallas_call(
        partial(forward_kernel, groups, hidden, to_send),
        grid=(part // block,),
        in_specs=[pl.BlockSpec((heads_here, block), lambda i: (0, i))] * groups
        + [rows(width)]
        + [inside() for a in fixed],
        out_specs=[rows(width), rows(width), rows(2 * hidden), rows(2 * hidden)]
        + (
            [whole((block, width))] * (part // block)
            if to_send
            else [rows(width)] + [whole((width, 2 * heads_here))] * 2
        ),
        out_shape=[
            jax.ShapeDtypeStruct((part, width), F32),
            jax.ShapeDtypeStruct((part, width), BF16),
            jax.ShapeDtypeStruct((part, 2 * hidden), BF16),
            jax.ShapeDtypeStruct((part, 2 * hidden), F32),
        ]
        + (
            [jax.ShapeDtypeStruct((block, width), BF16)] * (part // block)
            if to_send
            else [jax.ShapeDtypeStruct((part, width), F32)]
            + [jax.ShapeDtypeStruct((width, 2 * heads_here), BF16)] * 2
        ),
        compiler_params=params(20),
        cost_estimate=took(10),
        name="forward",
    )(*atts, tok, *fixed)


def loss_kernel(
    part, n, pos, lens, stream, own, other, table, teacher, count, *refs
):
    out, grad_ref, low_ref, sums_ref, send = refs[-5:]
    block, width = stream.shape
    counted = count[0:1, 0:1].astype(F32)
    token = pos[0] * part + n * block + lax.broadcasted_iota(jnp.int32, (block, 1), 0)
    valid = (token < picture_ends(lens)[-1]).astype(F32)
    result = stream[...] + (own[...] + other[...].astype(F32)) + line(table, DOWN_BIAS)
    out[...] = result.astype(BF16)
    error = (result - teacher[...].astype(F32)) * valid
    grad = error * (2.0 / counted)
    grad_ref[...] = grad
    low = grad.astype(BF16)
    low_ref[...] = low
    send[...] = low
    old = refs[3][...] if len(refs) > 5 else jnp.zeros_like(sums_ref)
    sums_ref[...] = old
    sums_ref[0:1, :] += jnp.sum(low.astype(F32), axis=0, keepdims=True)
    squares = jnp.sum(error * error, axis=0, keepdims=True)
    sums_ref[1:2, :] += squares / counted


def loss_call(n, me, lengths, stream, own, other, table, teacher, count, before):
    part, width = stream.shape
    block = other.shape[0]
    rows = pl.BlockSpec((block, width), lambda i, s, r: (n, 0))
    piece = whole((block, width))
    return pl.pallas_call(
        partial(loss_kernel, part, n),
        grid_spec=pltpu.PrefetchScalarGridSpec(
            num_scalar_prefetch=2,
            grid=(1,),
            in_specs=[rows, rows, piece, whole(table.shape), rows, whole(count.shape)]
            + [pl.BlockSpec(memory_space=pl.ANY)] * (3 if before else 0)
            + [whole((8, width))] * (1 if before else 0),
            out_specs=[rows, rows, rows, whole((8, width)), piece],
        ),
        out_shape=[
            jax.ShapeDtypeStruct((part, width), BF16),
            jax.ShapeDtypeStruct((part, width), F32),
            jax.ShapeDtypeStruct((part, width), BF16),
            jax.ShapeDtypeStruct((8, width), F32),
            jax.ShapeDtypeStruct((block, width), BF16),
        ],
        input_output_aliases={8: 0, 9: 1, 10: 2} if before else {},
        compiler_params=params(8),
        cost_estimate=took(3),
        name="loss",
    )(me, lengths, stream, own, other, table, teacher, count, *before)


def backward_kernel(hidden, blocks, first, *refs):
    grad, slope, w_own, w_sib = refs[:4]
    low_ref, grad_ref, part_ref, bias_ref = refs[-4:]

    @pl.when(pl.program_id(0) == 0)
    def _():
        bias_ref[...] = jnp.zeros_like(bias_ref) if first else refs[7][...]

    total = None
    for n, source in enumerate((w_own, w_sib)):
        cols = slice(n * hidden, (n + 1) * hidden)
        low = (mm(grad[...], source[:, hidden : 2 * hidden]) * slope[:, cols]).astype(BF16)
        low_ref[:, cols] = low
        bias_ref[:, cols] += jnp.sum(low.astype(F32), axis=0, keepdims=True)
        term = mm(low, source[:, :hidden], NT)
        total = term if total is None else total + term
    grad_ref[...] = grad[...]
    part_ref[...] = total.astype(part_ref.dtype)


def backward_call(grad, slope, w_own, w_sib, hidden, part_type, n=0, before=()):
    part = slope.shape[0]
    height, width = grad.shape
    block = min(TILE, part)
    start = n * height // block

    def rows(cols):
        return pl.BlockSpec((block, cols), lambda i: (start + i, 0))

    here = pl.BlockSpec((block, width), lambda i: (i, 0))
    return pl.pallas_call(
        partial(backward_kernel, hidden, height // block, not before),
        grid=(height // block,),
        in_specs=[here, rows(2 * hidden)]
        + [inside()] * 2
        + [pl.BlockSpec(memory_space=pl.ANY)] * (3 if before else 0)
        + [whole((1, 2 * hidden))] * (1 if before else 0),
        out_specs=[rows(2 * hidden), rows(width), rows(width), whole((1, 2 * hidden))],
        out_shape=[
            jax.ShapeDtypeStruct((part, 2 * hidden), BF16),
            jax.ShapeDtypeStruct((part, width), BF16),
            jax.ShapeDtypeStruct((part, width), part_type),
            jax.ShapeDtypeStruct((1, 2 * hidden), F32),
        ],
        input_output_aliases={4: 0, 5: 1, 6: 2} if before else {},
        compiler_params=params(14),
        cost_estimate=took(6 if part_type == BF16 else 0.1),
        name="backward",
    )(grad, slope, w_own, w_sib, *before)


def weight_terms_kernel(count, *refs):
    lefts, rights = refs[: 2 * count], refs[2 * count : 4 * count]
    come, out = refs[4 * count : -1], refs[-1]
    dims = (((0,), (0,)), ((), ()))
    half = out.shape[1] // 2
    for n in range(2):
        total = sum(mm(lefts[n * count + m][...], rights[n * count + m][...], dims) for m in range(count))
        cols = slice(n * half, (n + 1) * half)
        if come:
            total = total + come[0][:, cols].astype(F32)
        out[:, cols] = total.astype(BF16)


def weight_terms_call(lefts, rights, side, hidden, come):
    count = len(lefts[0])
    part, width = lefts[0][0].shape
    shape = (width, 2 * hidden)
    more = [] if come is None else [come]
    return pl.pallas_call(
        partial(weight_terms_kernel, count),
        grid=(1,),
        in_specs=[once((part, width))] * (2 * count)
        + [
            pl.BlockSpec((part, hidden), lambda i: (0, side), pipeline_mode=pl.Buffered(1))
        ]
        * (2 * count)
        + [once(shape)] * len(more),
        out_specs=once(shape),
        out_shape=jax.ShapeDtypeStruct(shape, BF16),
        compiler_params=params(26),
        cost_estimate=took(0.1),
        name="weight_terms",
    )(*lefts[0], *lefts[1], *rights[0], *rights[1], *more)


def out_terms_kernel(low, att_0, att_1, att_2, att_3, sent, kept):
    size = att_0.shape[0]
    for n, (first, second) in enumerate(((att_1, att_3), (att_0, att_2))):
        both = mm(jnp.concatenate([first[...], second[...]], axis=0), low[...]).T
        if n == 0:
            sent[...] = both.astype(BF16)
        else:
            kept[...] = both


def out_terms_call(low, atts):
    width = low.shape[1]
    cols = 2 * atts[0].shape[0]
    return pl.pallas_call(
        out_terms_kernel,
        out_shape=[
            jax.ShapeDtypeStruct((width, cols), BF16),
            jax.ShapeDtypeStruct((width, cols), F32),
        ],
        compiler_params=params(16),
        cost_estimate=took(0.1),
        name="out_terms",
    )(low, *atts)


def second_kernel(
    own, other, stream, result_grad, table, out_own, out_sib, *outs
):
    grad_ref, low_ref, sums_ref = outs[:3]
    heads_refs = outs[3:]

    @pl.when(pl.program_id(0) == 0)
    def _():
        sums_ref[...] = jnp.zeros_like(sums_ref)

    second_grad = own[...] + other[...].astype(F32)
    hat, factor = rows_hat(stream[...])
    sums_ref[0:1, :] += jnp.sum(second_grad * hat, axis=0, keepdims=True)
    sums_ref[1:2, :] += jnp.sum(second_grad, axis=0, keepdims=True)
    stream_grad = result_grad[...] + rows_back(second_grad * line(table, GAIN_2), hat, factor)
    grad_ref[...] = stream_grad
    low = stream_grad.astype(BF16)
    low_ref[...] = low
    sums_ref[2:3, :] += jnp.sum(low.astype(F32), axis=0, keepdims=True)
    for n, weight in enumerate((out_own, out_sib)):
        both = mm(low, weight[...]).T.astype(BF16)
        rows = both.shape[0] // 2
        heads_refs[n][...] = both[:rows]
        heads_refs[n + 2][...] = both[rows:]


def second_call(own, other, stream, result_grad, table, out_weights, groups, heads_here):
    part, width = own.shape
    block = min(TILE, part)
    rows = pl.BlockSpec((block, width), lambda i: (i, 0))
    lanes = pl.BlockSpec((heads_here, block), lambda i: (0, i))
    return pl.pallas_call(
        second_kernel,
        grid=(part // block,),
        in_specs=[rows] * 4
        + [once(table.shape)]
        + [once((width, 2 * heads_here))] * 2,
        out_specs=[rows, rows, whole((8, width))] + [lanes] * groups,
        out_shape=[
            jax.ShapeDtypeStruct((part, width), F32),
            jax.ShapeDtypeStruct((part, width), BF16),
            jax.ShapeDtypeStruct((8, width), F32),
        ]
        + [jax.ShapeDtypeStruct((heads_here, part), BF16)] * groups,
        compiler_params=params(56),
        cost_estimate=took(5),
        name="second_back",
    )(own, other, stream, result_grad, table, *out_weights)


def first_grad_kernel(wide, order, mixed, weight, *refs):
    count = len(order)
    toks = refs[:count]
    sums_ref = refs[count]
    outs = refs[count + 1 :]

    @pl.when(pl.program_id(0) == 0)
    def _():
        sums_ref[...] = jnp.zeros_like(sums_ref)

    for n, j in enumerate(order):
        grad = mm(weight[...], mixed[j]).T
        hat, _ = rows_hat(toks[n][...].astype(F32))
        sums_ref[0:1, :] += jnp.sum(grad * hat, axis=0, keepdims=True)
        sums_ref[1:2, :] += jnp.sum(grad, axis=0, keepdims=True)
        outs[0][n] = grad.astype(outs[0].dtype)


def first_grad_call(mixed, weight, toks, order, out_type):
    groups, wide, part = mixed.shape
    width = weight.shape[0]
    block = min(TILE, part)
    rows = pl.BlockSpec((block, width), lambda i: (i, 0))
    return pl.pallas_call(
        partial(first_grad_kernel, wide, order),
        grid=(part // block,),
        in_specs=[pl.BlockSpec((groups, wide, block), lambda i: (0, 0, i)), inside()]
        + [rows] * len(order),
        out_specs=[
            whole((8, width)),
            pl.BlockSpec((len(order), block, width), lambda i: (0, i, 0)),
        ],
        out_shape=[
            jax.ShapeDtypeStruct((8, width), F32),
            jax.ShapeDtypeStruct((len(order), part, width), out_type),
        ],
        compiler_params=params(16),
        cost_estimate=took(0.1),
        name="first_grad",
    )(mixed, weight, *[toks[j] for j in order])


def late_terms_kernel(bit, lows, mixed, out_terms, sent, kept):
    total = None
    for j in range(4):
        term = mm(mixed[j], lows[j])
        total = term if total is None else total + term
    wide = total.shape[0]

    @pl.when(pl.program_id(0) == 0)
    def _():
        sent[:, :wide] = total.T.astype(BF16)
        sent[:, wide:] = out_terms[...].astype(BF16)

    @pl.when(pl.program_id(0) == 1)
    def _():
        kept[:, :wide] = total.T
        kept[:, wide:] = out_terms[...]


def late_terms_call(lows, mixed, out_terms):
    part, width = lows.shape[1:]
    wide = mixed.shape[1]
    cols = wide + out_terms.shape[1]
    half = width // 2
    bit = top_bit("dp")[0].reshape(1)

    def side(i, s):
        return s[0] ^ 1 ^ i

    return pl.pallas_call(
        late_terms_kernel,
        grid_spec=pltpu.PrefetchScalarGridSpec(
            num_scalar_prefetch=1,
            grid=(2,),
            in_specs=[
                pl.BlockSpec((4, part, half), lambda i, s: (0, 0, side(i, s))),
                inside(),
                pl.BlockSpec((half, out_terms.shape[1]), lambda i, s: (side(i, s), 0)),
            ],
            out_specs=[whole((half, cols)), whole((half, cols))],
        ),
        out_shape=[
            jax.ShapeDtypeStruct((half, cols), BF16),
            jax.ShapeDtypeStruct((half, cols), F32),
        ],
        compiler_params=params(20),
        cost_estimate=took(5),
        name="late_terms",
    )(bit, lows, mixed, out_terms)


def late_final_kernel(kept, come, in_ref, out_ref):
    total = kept[...] + come[...].astype(F32)
    wide = in_ref.shape[1]
    in_ref[...] = total[:, :wide]
    out_ref[...] = total[:, wide:].T


def late_final_call(kept, come, wide):
    rows, cols = kept.shape
    return pl.pallas_call(
        late_final_kernel,
        out_shape=[
            jax.ShapeDtypeStruct((rows, wide), F32),
            jax.ShapeDtypeStruct((cols - wide, rows), F32),
        ],
        compiler_params=params(6),
        cost_estimate=took(1),
        name="late_final",
    )(kept, come)


def weight_final_kernel(grads, up_ref, down_ref):
    half = up_ref.shape[1]
    up_ref[...] = grads[:, :half].astype(F32)
    down_ref[...] = grads[:, half:].astype(F32).T


def weight_final_call(grads):
    rows, cols = grads.shape
    half = cols // 2
    return pl.pallas_call(
        weight_final_kernel,
        out_shape=[
            jax.ShapeDtypeStruct((rows, half), F32),
            jax.ShapeDtypeStruct((half, rows), F32),
        ],
        compiler_params=params(6),
        cost_estimate=took(1),
        name="weight_final",
    )(grads)


def pair_kernel(own, come, out):
    out[...] = (own[0] + come[0].astype(F32)).astype(BF16)


def pair_call(own, come):
    part, width = own.shape[1:]
    block = min(TILE, part)
    second = pl.BlockSpec((1, block, width), lambda i: (1, i, 0))
    return pl.pallas_call(
        pair_kernel,
        grid=(part // block,),
        in_specs=[second] * 2,
        out_specs=pl.BlockSpec((block, width), lambda i: (i, 0)),
        out_shape=jax.ShapeDtypeStruct((part, width), BF16),
        compiler_params=params(8),
        cost_estimate=took(0.1),
        name="pair",
    )(own, come)


def first_back_kernel(own, come, other, tok, stream_grad, table, out_ref):
    hat, factor = rows_hat(tok[...].astype(F32))
    grad = own[0] + come[0].astype(F32) + other[...].astype(F32)
    out_ref[...] = stream_grad[...] + rows_back(grad * line(table, GAIN_1), hat, factor)


def first_back_call(own, come, other, tok, stream_grad, table):
    part, width = tok.shape
    block = min(TILE, part)
    rows = pl.BlockSpec((block, width), lambda i: (i, 0))
    return pl.pallas_call(
        first_back_kernel,
        grid=(part // block,),
        in_specs=[pl.BlockSpec((1, block, width), lambda i: (0, i, 0))] * 2
        + [rows] * 3
        + [whole(table.shape)],
        out_specs=rows,
        out_shape=jax.ShapeDtypeStruct((part, width), F32),
        compiler_params=params(10),
        cost_estimate=took(1),
        name="first_back",
    )(own, come, other, tok, stream_grad, table)


def own_rows(vector, group, amount):
    return lax.dynamic_slice_in_dim(vector, group * amount, amount)


def local(
    tokens,
    teacher,
    picture_lengths,
    first_gain,
    first_shift,
    input_weight,
    input_bias,
    query_gain,
    key_gain,
    output_weight,
    output_bias,
    second_gain,
    second_shift,
    expand_weight,
    expand_bias,
    reduce_weight,
    reduce_bias,
):
    assert tokens.shape[0] == 1 and lax.axis_size("gx") == 4
    part, width = tokens.shape[1:]
    groups = 4
    group = lax.axis_index("gx")
    hd = query_gain.shape[0]
    wide = input_weight.shape[1]
    heads = wide // (3 * hd)
    heads_here = heads * hd
    hidden = expand_weight.shape[1]
    shard_rows = input_weight.shape[0]

    me = group.reshape(1).astype(jnp.int32)
    lengths = picture_lengths[0]
    out_shard = output_weight.T
    out_pair = swap(out_shard, "gx", 2)
    tok0 = after(tokens[0], out_pair)
    tok2 = swap(tok0, "gx", 2)
    w_own = lax.all_gather(
        jnp.concatenate([expand_weight, reduce_weight.T, out_shard, out_pair], axis=1),
        ("dp", "gy"),
        axis=0,
        tiled=True,
    )
    table_rows = [first_gain, first_shift, second_gain, second_shift, output_bias, reduce_bias]
    table_rows += [own_rows(expand_bias, group, hidden), own_rows(expand_bias, group ^ 1, hidden)]
    table_rows += [jnp.pad(own_rows(input_bias, group, wide), (0, width - wide))]
    table = jnp.stack(table_rows)
    gains = jnp.stack([query_gain, key_gain], axis=1)
    counted = jnp.full((8, 128), jnp.sum(lengths), jnp.int32)
    in_part = input_weight
    for mask in reversed(bits_of("gy")):
        more = swap(counted, "gy", mask)
        in_part = joined("gy", mask, in_part, shard_rows, table, gains, more)
        counted = counted + more
    w_in = in_part
    for mask in bits_of("dp"):
        more = swap(counted, "dp", mask)
        w_in = joined("dp", mask, w_in, w_in.shape[0], more)
        counted = counted + more
    tok3 = swap(after(tok2, in_part), "gx", 1)
    tok1 = swap(after(tok0, in_part), "gx", 1)
    toks = (tok0, tok1, tok2, tok3)

    low, mixed, hats, scales = mixed_call(toks, table, w_in, gains, heads, hd)
    *atts, raw, log = attend_call(me, lengths, mixed, heads, hd)
    att_pair = [atts[2]] + [swap(atts[j ^ 2], "gx", j) for j in range(1, 4)]
    w_own = after(w_own, raw)
    w_sib = swap(w_own, "gx", 1)
    atts = after(atts, *att_pair)
    att_own = [atts[0]] + [swap(atts[j], "gx", j) for j in range(1, 4)]

    def forward_of(pieces, tok, to_send):
        return forward_call(pieces, tok, w_own, w_sib, table, hidden, to_send)

    _, low_p, active_p, slope_p, *parts_p = forward_of(att_pair, tok2, True)
    stream, low_o, active_o, slope_o, part_o, *out_weights = forward_of(att_own, tok0, False)
    parts_in = [swap(parts_p[0], "gx", 2)]
    parts_in += [swap(after(piece, part_o), "gx", 2) for piece in parts_p[1:]]
    state, pairs = (), []
    for n, piece in enumerate(parts_in):
        if state:
            piece = after(piece, state[0])
        *state, low_sent = loss_call(
            n, me, lengths, stream, part_o, piece, table, teacher[0], counted, state
        )
        pairs.append(swap(low_sent, "gx", 2))
    layer_output, result_grad, reduce_low, sums_3 = state

    hidden_o, _, back_o, up_sum_o = backward_call(reduce_low, slope_o, w_own, w_sib, hidden, F32)
    state = ()
    for n, piece in enumerate(pairs):
        if state:
            piece = after(piece, state[0])
        state = backward_call(piece, slope_p, w_own, w_sib, hidden, BF16, n, state)
    hidden_p, reduce_pair, back_p, up_sum_p = state
    back_in = swap(back_p, "gx", 2)

    lefts = ((low_o, low_p), (reduce_low, reduce_pair))
    rights = ((hidden_o, hidden_p), (active_o, active_p))
    sib_terms = swap(weight_terms_call(lefts, rights, 1, hidden, None), "gx", 1)
    weight_terms = weight_terms_call(lefts, rights, 0, hidden, sib_terms)
    weight_grads = lax.psum_scatter(weight_terms, ("dp", "gy"), scatter_dimension=0, tiled=True)
    stream_grad, branch_low, sums_2, *heads_grad = second_call(
        back_o,
        after(back_in, weight_terms),
        stream,
        result_grad,
        table,
        out_weights,
        groups,
        heads_here,
    )
    grads = [heads_grad[0]] + [swap(heads_grad[j], "gx", j) for j in range(1, 4)]

    out_sent, out_held = out_terms_call(branch_low, att_own)
    out_held = out_held + swap(out_sent, "gx", 1).astype(F32)
    out_own = out_held[:, :heads_here] + swap(
        out_held[:, heads_here:].astype(BF16), "gx", 2
    ).astype(F32)

    mixed_low, gain_sums, bias_sums = attend_back_call(
        me, lengths, mixed, hats, scales, raw, log, grads, gains, heads, hd
    )
    sums_s, sent = first_grad_call(after(mixed_low, out_own), w_in, toks, (1, 3), BF16)
    sib_in = swap(sent, "gx", 1)
    late_sent, late_kept = late_terms_call(low, after(mixed_low, sent), out_own)
    come = swap(late_sent, "dp", top_bit("dp")[1])
    sums_k, kept = first_grad_call(after(mixed_low, late_kept), w_in, toks, (0, 2), F32)
    pair_sent = pair_call(kept, sib_in)
    pair_in = swap(pair_sent, "gx", 2)

    sums = pack_call(
        me, groups, up_sum_o, up_sum_p, sums_2, sums_3, sums_s, sums_k, bias_sums, gain_sums
    )
    sums = after(sums, pair_sent)
    sums = sum_over(sums + swap(sums, "gx", 1), "gy")
    come = after(come, sums, weight_grads)
    for mask in reversed(bits_of("dp")[:-1]):
        late_kept, come = halved("dp", mask, late_kept, come, late_kept.shape[0] // 2)
    first, *others = bits_of("gy")
    late_kept, come = halved("gy", first, late_kept, come, shard_rows)
    sums = sum_over(after(sums, late_kept), "dp")
    come = after(come, sums)
    tokens_gradient = first_back_call(kept, sib_in, pair_in, tok0, stream_grad, table)
    for mask in others:
        late_kept, come = halved("gy", mask, late_kept, come, shard_rows)
    sums = sums + swap(after(sums, tokens_gradient, late_kept), "gx", 2)
    expand_out, reduce_out = weight_final_call(after(weight_grads, late_kept))
    input_out, output_out = late_final_call(late_kept, after(come, sums), wide)
    row = 2 * groups
    return (
        layer_output[None],
        jnp.sum(sums[row + 4]),
        tokens_gradient[None],
        sums[row + 5],
        sums[row + 6],
        input_out,
        sums[groups:row, :wide].reshape(-1),
        sums[row + 7, :hd],
        sums[row + 7, hd : 2 * hd],
        output_out,
        sums[row + 2],
        sums[row],
        sums[row + 1],
        expand_out,
        sums[:groups, :hidden].reshape(-1),
        reduce_out,
        sums[row + 3],
    )


def solution(mesh):
    rows = P(("dp", "gy"), "gx", None)
    by_rows = P(("dp", "gy"), "gx")
    by_cols = P("gx", ("dp", "gy"))
    return jax.shard_map(
        local,
        mesh=mesh,
        in_specs=(
            rows,
            rows,
            P(("dp", "gy"), None),
            P(),
            P(),
            by_rows,
            P(),
            P(),
            P(),
            by_cols,
            P(),
            P(),
            P(),
            by_rows,
            P(),
            by_cols,
            P(),
        ),
        out_specs=(
            rows,
            P(),
            rows,
            P(),
            P(),
            by_rows,
            P(),
            P(),
            P(),
            by_cols,
            P(),
            P(),
            P(),
            by_rows,
            P(),
            by_cols,
            P(),
        ),
        check_vma=False,
    )
```

```python
from functools import partial

import jax
import jax.numpy as jnp
from jax import lax
from jax.experimental import pallas as pl
from jax.experimental.pallas import tpu as pltpu
from jax.sharding import PartitionSpec as P

EPS = 1e-06
APART = 1024.0
TILE = 256
KEY_TILE = 512
BACK_KEY_TILE = 256
MIB = 1 << 20
F32 = jnp.float32
BF16 = jnp.bfloat16

NN = (((1,), (0,)), ((), ()))
NT = (((1,), (1,)), ((), ()))


def mm(left, right, dims=NN):
    return lax.dot_general(left, right, dims, preferred_element_type=F32)


def took(us):
    return pl.CostEstimate(flops=int(us * 1.15e9), bytes_accessed=0, transcendentals=0)


def params(limit):
    return pltpu.CompilerParams(vmem_limit_bytes=limit * MIB)


def whole(shape):
    rank = len(shape)
    return pl.BlockSpec(shape, lambda *_: (0,) * rank)


def inside():
    return pl.BlockSpec(memory_space=pltpu.VMEM)


def once(shape):
    rank = len(shape)
    return pl.BlockSpec(shape, lambda *_: (0,) * rank, pipeline_mode=pl.Buffered(1))


def rows_hat(values):
    mean = jnp.mean(values, axis=-1, keepdims=True)
    centered = values - mean
    factor = lax.rsqrt(jnp.mean(centered * centered, axis=-1, keepdims=True) + EPS)
    return centered * factor, factor


def rows_back(grad_hat, hat, factor):
    return factor * (
        grad_hat
        - jnp.mean(grad_hat, axis=-1, keepdims=True)
        - hat * jnp.mean(grad_hat * hat, axis=-1, keepdims=True)
    )


def swap(array, axis, mask):
    size = lax.axis_size(axis)
    return lax.ppermute(array, axis, [(i, i ^ mask) for i in range(size)])


def bits_of(axis):
    size = lax.axis_size(axis)
    masks = []
    mask = 1
    while mask < size:
        masks.append(mask)
        mask *= 2
    return masks


def order_kernel(blocks, rows, pos, *refs):
    pieces, out = refs[:-1], refs[-1]
    count = len(pieces)
    for j in range(count):
        for d in range(blocks):
            start = pl.multiple_of((d * count + (pos[0] ^ j)) * rows, rows)
            out[pl.ds(start, rows), :] = pieces[j][d * rows : (d + 1) * rows, :]


def ordered(pieces, rows, me):
    height, cols = pieces[0].shape
    count = len(pieces)
    if rows % 16:
        out = jnp.zeros((height // rows, count, rows, cols), pieces[0].dtype)
        for j, piece in enumerate(pieces):
            piece = piece.reshape(-1, 1, rows, cols)
            out = lax.dynamic_update_slice(out, piece, (0, me ^ j, 0, 0))
        return out.reshape(height * count, cols)
    return pl.pallas_call(
        partial(order_kernel, height // rows, rows),
        grid_spec=pltpu.PrefetchScalarGridSpec(
            num_scalar_prefetch=1,
            grid=(1,),
            in_specs=[inside()] * count,
            out_specs=inside(),
        ),
        out_shape=jax.ShapeDtypeStruct((height * count, cols), pieces[0].dtype),
        compiler_params=params(10),
        cost_estimate=took(1),
        name="ordered",
    )(me.reshape(1).astype(jnp.int32), *pieces)


def joined(axis, mask, held, rows, *earlier):
    mine = ((lax.axis_index(axis) & mask) != 0).astype(jnp.int32)
    return ordered([held, after(swap(held, axis, mask), *earlier)], rows, mine)


def along_gy(held, rows, *earlier):
    for mask in reversed(bits_of("gy")):
        held = joined("gy", mask, held, rows, *earlier)
    return held


def along_dp(held, *earlier):
    for mask in bits_of("dp"):
        held = joined("dp", mask, held, held.shape[0], *earlier)
    return held


def top_bit(axis):
    mask = bits_of(axis)[-1]
    return ((lax.axis_index(axis) & mask) != 0).astype(jnp.int32), mask


def step_kernel(blocks, rows, bit, kept, come, out, keep):
    for d in range(blocks):
        for side in range(2):
            span = slice((2 * d + side) * rows, (2 * d + side + 1) * rows)
            total = kept[span, :] + come[span, :].astype(F32)
            to = slice(d * rows, (d + 1) * rows)

            @pl.when(bit[0] == side)
            def _():
                keep[to, :] = total

            @pl.when(bit[0] != side)
            def _():
                out[to, :] = total.astype(BF16)


def step_call(bit, kept, come, rows):
    height, cols = kept.shape
    half = (height // 2, cols)
    return pl.pallas_call(
        partial(step_kernel, height // (2 * rows), rows),
        grid_spec=pltpu.PrefetchScalarGridSpec(
            num_scalar_prefetch=1,
            grid=(1,),
            in_specs=[inside()] * 2,
            out_specs=[inside()] * 2,
        ),
        out_shape=[jax.ShapeDtypeStruct(half, BF16), jax.ShapeDtypeStruct(half, F32)],
        compiler_params=params(12),
        cost_estimate=took(1),
        name="scatter_step",
    )(bit.reshape(1), kept, come)


def halved(axis, mask, kept, come, rows):
    bit = ((lax.axis_index(axis) & mask) != 0).astype(jnp.int32)
    out, kept = step_call(bit, kept, come, rows)
    return kept, swap(out, axis, mask)


def after(value, *earlier):
    return lax.optimization_barrier((value, *earlier))[0]


def sum_over(values, axis):
    for mask in bits_of(axis):
        values = values + swap(values, axis, mask)
    return values


GAIN_1, SHIFT_1, GAIN_2, SHIFT_2, OUT_BIAS, DOWN_BIAS, UP_BIAS, UP_BIAS_SIB, IN_BIAS = range(9)


def line(table, row):
    return table[row : row + 1, :]


def pack_kernel(groups, me, up_o, up_p, early_2, early_3, late_s, late_k, bias, gains, out):
    width = out.shape[1]
    wide = bias.shape[0]
    out[...] = jnp.zeros_like(out)
    up = up_o[...] + up_p[...]
    out[pl.ds(me[0], 1), :] = up[:, :width]
    out[pl.ds(me[0] ^ 1, 1), :] = up[:, width:]
    out[pl.ds(groups + me[0], 1), 0:wide] = jnp.sum(bias[...].T, axis=0, keepdims=True)
    row = 2 * groups
    out[row : row + 3, :] = early_2[0:3, :]
    out[row + 3 : row + 5, :] = early_3[0:2, :]
    out[row + 5 : row + 7, :] = late_s[0:2, :] + late_k[0:2, :]
    out[row + 7 : row + 8, 0 : gains.shape[0]] = jnp.sum(gains[...].T, axis=0, keepdims=True)


def pack_call(me, groups, *parts):
    width = parts[2].shape[1]
    return pl.pallas_call(
        partial(pack_kernel, groups),
        grid_spec=pltpu.PrefetchScalarGridSpec(
            num_scalar_prefetch=1,
            grid=(1,),
            in_specs=[whole(a.shape) for a in parts],
            out_specs=whole((2 * groups + 8, width)),
        ),
        out_shape=jax.ShapeDtypeStruct((2 * groups + 8, width), F32),
        compiler_params=params(6),
        cost_estimate=took(1),
        name="pack",
    )(me, *parts)


def mixed_kernel(count, heads, hd, *refs):
    toks = refs[:count]
    table, weight, gains = refs[count : count + 3]
    low_ref, mixed_ref, hat_ref, scale_ref = refs[count + 3 :]
    wide = heads * 3 * hd
    gain, shift, bias = line(table, GAIN_1), line(table, SHIFT_1), line(table, IN_BIAS)[:, :wide]
    q_gain, k_gain = gains[:, 0:1], gains[:, 1:2]
    for j in range(count):
        hat, _ = rows_hat(toks[j][...].astype(F32))
        low = (hat * gain + shift).astype(BF16)
        low_ref[j] = low
        mixed = (mm(low, weight[...]) + bias).T
        scales = []
        for h in range(heads):
            for kind, a_gain, factor in ((0, q_gain, hd**-0.5), (1, k_gain, 1.0)):
                start = (h * 3 + kind) * hd
                raw = mixed[start : start + hd]
                centered = raw - jnp.mean(raw, axis=0, keepdims=True)
                scale = lax.rsqrt(jnp.mean(centered * centered, axis=0, keepdims=True) + EPS)
                unit = centered * scale
                hat_ref[j, (h * 2 + kind) * hd : (h * 2 + kind + 1) * hd, :] = unit
                scales.append(scale)
                normed = (unit * a_gain).astype(BF16)
                if factor != 1.0:
                    normed = normed * jnp.asarray(factor, BF16)
                mixed_ref[j, start : start + hd, :] = normed
            start = (h * 3 + 2) * hd
            mixed_ref[j, start : start + hd, :] = mixed[start : start + hd].astype(BF16)
        for n, scale in enumerate(scales):
            scale_ref[j, n : n + 1, :] = scale


def mixed_call(pieces, table, weight, gains, heads, hd):
    count = len(pieces)
    part, width = pieces[0].shape
    block = min(TILE, part)
    wide = heads * 3 * hd
    piece_spec = pl.BlockSpec((block, width), lambda i: (i, 0))

    def lanes(rows):
        return pl.BlockSpec((count, rows, block), lambda i: (0, 0, i))

    scale_rows = 8 * -(-2 * heads // 8)
    return pl.pallas_call(
        partial(mixed_kernel, count, heads, hd),
        grid=(part // block,),
        in_specs=[piece_spec] * count
        + [whole(a.shape) for a in (table, weight, gains)],
        out_specs=[
            pl.BlockSpec((count, block, width), lambda i: (0, i, 0)),
            lanes(wide),
            lanes(heads * 2 * hd),
            lanes(scale_rows),
        ],
        out_shape=[
            pltpu.HBM((count, part, width), BF16),
            pltpu.HBM((count, wide, part), BF16),
            pltpu.HBM((count, heads * 2 * hd, part), F32),
            jax.ShapeDtypeStruct((count, scale_rows, part), F32),
        ],
        compiler_params=params(24),
        cost_estimate=took(6),
        name="mixed",
    )(*pieces, table, weight, gains)


def picture_ends(lengths):
    ends = []
    total = jnp.int32(0)
    for k in range(lengths.shape[0]):
        total = total + lengths[k]
        ends.append(total)
    return ends


def key_tiles(ends, first, amount, row, tile):
    begin, until = jnp.int32(0), jnp.int32(row)
    for end in ends:
        begin = jnp.where(end <= first, end, begin)
    for end in reversed(ends):
        until = jnp.where(end >= first + amount, end, until)
    return lax.div(begin, tile), lax.div(until + tile - 1, tile)


def one_hot(ends, start, amount):
    place = start + lax.broadcasted_iota(jnp.int32, (1, amount), 1)
    number = jnp.zeros((1, amount), jnp.int32)
    for end in ends:
        number = number + (end <= place).astype(jnp.int32)
    return (lax.broadcasted_iota(jnp.int32, (32, amount), 0) == number).astype(F32)


def lay_out(me, ends, source, heads, hd, part, keys_tok, queries_lane):
    for j in range(4):
        start = pl.multiple_of((me ^ j) * part, part)
        marks = one_hot(ends, start, part)
        away = ((marks - 1.0) * APART).astype(BF16)
        blank = jnp.zeros((32, part), F32)
        for h in range(heads):
            base = h * 3 * hd
            queries_lane[h, 0:hd, pl.ds(start, part)] = source[j, base : base + hd, :]
            queries_lane[h, hd : hd + 32, pl.ds(start, part)] = away
            queries_lane[h, hd + 32 : hd + 64, pl.ds(start, part)] = blank.astype(BF16)
            key = source[j, base + hd : base + 2 * hd, :].astype(F32)
            keys_tok[h, pl.ds(start, part), :] = (
                jnp.concatenate([key, marks, blank], axis=0).T.astype(BF16)
            )


def attend_kernel(
    heads, hd, part, pos, lens, mixed, a0, a1, a2, a3, raw, log, keys_tok, queries_lane, vals, acc
):
    i = pl.program_id(0)
    block = part
    me = pos[0]
    ends = picture_ends(lens)

    @pl.when(i == 0)
    def _():
        lay_out(me, ends, mixed, heads, hd, part, keys_tok, queries_lane)
        for j in range(4):
            start = pl.multiple_of((me ^ j) * part, part)
            for h in range(heads):
                base = (h * 3 + 2) * hd
                vals[h, 0:hd, pl.ds(start, part)] = mixed[j, base : base + hd, :]
                vals[h, hd : hd + 16, pl.ds(start, part)] = jnp.ones((16, part), BF16)

    own = pl.ds(pl.multiple_of(i * block, block), block)
    acc[...] = jnp.zeros_like(acc)

    def step(t, carry):
        there = pl.ds(pl.multiple_of(t * KEY_TILE, KEY_TILE), KEY_TILE)
        scores = [mm(keys_tok[h, there, :], queries_lane[h, :, own]) for h in range(heads)]
        weights = [jnp.exp(scores[h]).astype(BF16) for h in range(heads)]
        for h in range(heads):
            acc[h] += mm(vals[h, :, there], weights[h])
        return carry

    low, high = key_tiles(ends, i * block, block, 4 * part, KEY_TILE)
    lax.fori_loop(low, high, step, 0)
    for h in range(heads):
        total = acc[h, hd : hd + 1, :]
        raw[0, h * hd : (h + 1) * hd, :] = acc[h, 0:hd, :] / total
        log[0, h : h + 1, :] = jnp.log(total)
    for j, att in enumerate((a0, a1, a2, a3)):

        @pl.when((i ^ me) == j)
        def _():
            att[...] = raw[0].astype(BF16)


def attend_call(me, lengths, mixed, heads, hd):
    part = mixed.shape[2]
    row = 4 * part

    def lanes(rows):
        return pl.BlockSpec((1, rows, part), lambda i, s, n: (i ^ s[0], 0, 0))

    return pl.pallas_call(
        partial(attend_kernel, heads, hd, part),
        grid_spec=pltpu.PrefetchScalarGridSpec(
            num_scalar_prefetch=2,
            grid=(4,),
            in_specs=[once(mixed.shape)],
            out_specs=[once((heads * hd, part))] * 4 + [lanes(heads * hd), lanes(8)],
            scratch_shapes=[
                pltpu.VMEM((heads, row, 2 * hd), BF16),
                pltpu.VMEM((heads, 2 * hd, row), BF16),
                pltpu.VMEM((heads, hd + 16, row), BF16),
                pltpu.VMEM((heads, hd + 16, part), F32),
            ],
        ),
        out_shape=[jax.ShapeDtypeStruct((heads * hd, part), BF16)] * 4
        + [
            pltpu.HBM((4, heads * hd, part), F32),
            jax.ShapeDtypeStruct((4, 8, part), F32),
        ],
        compiler_params=params(20),
        cost_estimate=took(11),
        name="attend",
    )(me, lengths, mixed)


def attend_back_kernel(
    heads,
    hd,
    part,
    pos,
    lens,
    mixed,
    hats,
    scales,
    raw,
    log,
    d0,
    d1,
    d2,
    d3,
    gains,
    out_ref,
    gain_ref,
    bias_ref,
    keys_tok,
    queries_lane,
    vals_tok,
    keys_lane,
    grads_lane,
    log_row,
    inner_row,
    d_key,
    d_val,
    d_query,
):
    i = pl.program_id(0)
    blocks = pl.num_programs(0)
    block = part
    me = pos[0]
    grads = (d0, d1, d2, d3)
    ends = picture_ends(lens)
    q_gain, k_gain = gains[:, 0:1], gains[:, 1:2]

    @pl.when(i == 0)
    def _():
        lay_out(me, ends, mixed, heads, hd, part, keys_tok, queries_lane)
        for j in range(4):
            start = pl.multiple_of((me ^ j) * part, part)
            there = pl.ds(start, part)
            log_row[:, there] = log[j]
            for h in range(heads):
                base = h * 3 * hd
                keys_lane[h, :, there] = mixed[j, base + hd : base + 2 * hd, :]
                vals_tok[h, there, :] = (
                    mixed[j, base + 2 * hd : base + 3 * hd, :].astype(F32).T.astype(BF16)
                )
                grad = grads[j][h * hd : (h + 1) * hd, :]
                grads_lane[h, :, there] = grad
                inner_row[h : h + 1, there] = jnp.sum(
                    grad.astype(F32) * raw[j, h * hd : (h + 1) * hd, :], axis=0, keepdims=True
                )
        d_key[...] = jnp.zeros_like(d_key)
        d_val[...] = jnp.zeros_like(d_val)

    own = pl.ds(pl.multiple_of(i * block, block), block)
    d_query[:, :, own] = jnp.zeros((heads, hd, block), F32)
    low, high = key_tiles(ends, i * block, block, 4 * part, BACK_KEY_TILE)
    high = jnp.minimum(high, lax.div(ends[-1] + BACK_KEY_TILE - 1, BACK_KEY_TILE))

    @pl.when((i * block < ends[-1]) & (high > low))
    def _():
        queries_tok = [queries_lane[h, 0:hd, own].astype(F32).T.astype(BF16) for h in range(heads)]
        grads_tok = [grads_lane[h, :, own].astype(F32).T.astype(BF16) for h in range(heads)]

        def step(t, carry):
            there = pl.ds(pl.multiple_of(t * BACK_KEY_TILE, BACK_KEY_TILE), BACK_KEY_TILE)
            each = range(heads)
            scores = [mm(keys_tok[h, there, :], queries_lane[h, :, own]) for h in each]
            chance_grad = [mm(vals_tok[h, there, :], grads_lane[h, :, own]) for h in each]
            chance = [jnp.exp(scores[h] - log_row[h : h + 1, own]) for h in each]
            chance_low = [chance[h].astype(BF16) for h in each]
            score_grad = [
                (chance[h] * (chance_grad[h] - inner_row[h : h + 1, own])).astype(BF16)
                for h in each
            ]
            for h in each:
                d_val[h, there, :] += mm(chance_low[h], grads_tok[h])
                d_key[h, there, :] += mm(score_grad[h], queries_tok[h])
                d_query[h, :, own] += mm(keys_lane[h, :, there], score_grad[h])
            return carry

        lax.fori_loop(low, high, step, 0)

    @pl.when(i == blocks - 1)
    def _():
        def fold(values):
            return sum(values[:, n * 128 : (n + 1) * 128] for n in range(values.shape[1] // 128))

        gain_ref[...] = jnp.zeros_like(gain_ref)
        bias_ref[...] = jnp.zeros_like(bias_ref)
        for j in range(4):
            start = pl.multiple_of((me ^ j) * part, part)
            there = pl.ds(start, part)
            for h in range(heads):
                for kind, a_gain in ((0, q_gain), (1, k_gain)):
                    if kind == 0:
                        grad = d_query[h, :, there] * hd**-0.5
                    else:
                        grad = d_key[h, there, :].T
                    slot = h * 2 + kind
                    hat = hats[j, slot * hd : (slot + 1) * hd, :]
                    scale = scales[j, slot : slot + 1, :]
                    gain_ref[kind * hd : (kind + 1) * hd, :] += fold(grad * hat)
                    inner = grad * a_gain
                    back = scale * (
                        inner
                        - jnp.mean(inner, axis=0, keepdims=True)
                        - hat * jnp.mean(inner * hat, axis=0, keepdims=True)
                    )
                    rows = slice((h * 3 + kind) * hd, (h * 3 + kind + 1) * hd)
                    back = back.astype(BF16)
                    out_ref[j, rows, :] = back
                    bias_ref[rows, :] += fold(back.astype(F32))
                rows = slice((h * 3 + 2) * hd, (h * 3 + 3) * hd)
                back = d_val[h, there, :].T.astype(BF16)
                out_ref[j, rows, :] = back
                bias_ref[rows, :] += fold(back.astype(F32))


def attend_back_call(me, lengths, mixed, hats, scales, raw, log, grads, gains, heads, hd):
    part = mixed.shape[2]
    row = 4 * part
    wide = heads * 3 * hd
    operands = (mixed, hats, scales, raw, log, *grads, gains)
    return pl.pallas_call(
        partial(attend_back_kernel, heads, hd, part),
        grid_spec=pltpu.PrefetchScalarGridSpec(
            num_scalar_prefetch=2,
            grid=(4,),
            in_specs=[inside() for a in operands],
            out_specs=[once((4, wide, part)), once((2 * hd, 128)), once((wide, 128))],
            scratch_shapes=[
                pltpu.VMEM((heads, row, 2 * hd), BF16),
                pltpu.VMEM((heads, 2 * hd, row), BF16),
                pltpu.VMEM((heads, row, hd), BF16),
                pltpu.VMEM((heads, hd, row), BF16),
                pltpu.VMEM((heads, hd, row), BF16),
                pltpu.VMEM((8, row), F32),
                pltpu.VMEM((8, row), F32),
                pltpu.VMEM((heads, row, hd), F32),
                pltpu.VMEM((heads, row, hd), F32),
                pltpu.VMEM((heads, hd, row), F32),
            ],
        ),
        out_shape=[
            jax.ShapeDtypeStruct((4, wide, part), BF16),
            jax.ShapeDtypeStruct((2 * hd, 128), F32),
            jax.ShapeDtypeStruct((wide, 128), F32),
        ],
        compiler_params=params(36),
        cost_estimate=took(1),
        name="attend_back",
    )(me, lengths, *operands)


def gelu_parts(x):
    size = jnp.abs(x)
    t = 1.0 / (1.0 + (0.3275911 * 2.0**-0.5) * size)
    bell = jnp.exp(-0.5 * x * x)
    poly = t * (
        0.127414796
        + t * (-0.142248368 + t * (0.7107068705 + t * (-0.7265760135 + t * 0.5307027145)))
    )
    upper = poly * bell
    below = jnp.where(x >= 0, 1.0 - upper, upper)
    return x * below, below + x * bell * 0.3989422804014327


def forward_kernel(groups, hidden, to_send, *refs):
    atts = refs[:groups]
    tok, w_own, w_sib, table = refs[groups : groups + 4]
    stream_ref, low_ref, active_ref, slope_ref, *part_refs = refs[groups + 4 :]
    heads_here = atts[0].shape[0]
    block = stream_ref.shape[0]
    here = pl.ds(pl.multiple_of(pl.program_id(0) * block, block), block)
    branch = None
    for j in range(groups):
        start = 2 * hidden + (j // 2) * heads_here
        term = mm((w_own, w_sib)[j % 2][:, start : start + heads_here], atts[j][:, here])
        branch = term if branch is None else branch + term
    stream = tok[here, :].astype(F32) + branch.T + line(table, OUT_BIAS)
    stream_ref[...] = stream
    hat, _ = rows_hat(stream)
    low = (hat * line(table, GAIN_2) + line(table, SHIFT_2)).astype(BF16)
    low_ref[...] = low
    total = None
    for n, source in enumerate((w_own, w_sib)):
        cols = slice(n * hidden, (n + 1) * hidden)
        raised = mm(low, source[:, :hidden]) + line(table, UP_BIAS + n)[:, :hidden]
        active, slope = gelu_parts(raised)
        active = active.astype(BF16)
        active_ref[:, cols] = active
        slope_ref[:, cols] = slope
        term = mm(active, source[:, hidden : 2 * hidden], NT)
        total = term if total is None else total + term
    if to_send:
        for n, part_ref in enumerate(part_refs):

            @pl.when(pl.program_id(0) == n)
            def _():
                part_ref[...] = total.astype(BF16)

    else:
        part_refs[0][...] = total
        part_refs[1][...] = w_own[:, 2 * hidden :]
        part_refs[2][...] = w_sib[:, 2 * hidden :]


def forward_call(atts, tok, w_own, w_sib, table, hidden, to_send):
    groups = len(atts)
    part, width = tok.shape
    block = min(TILE, part)
    heads_here = atts[0].shape[0]

    def rows(cols):
        return pl.BlockSpec((block, cols), lambda i: (i, 0))

    fixed = (w_own, w_sib, table)
    return pl.pallas_call(
        partial(forward_kernel, groups, hidden, to_send),
        grid=(part // block,),
        in_specs=[inside() for a in (*atts, tok, *fixed)],
        out_specs=[rows(width), rows(width), rows(2 * hidden), rows(2 * hidden)]
        + (
            [whole((block, width))] * (part // block)
            if to_send
            else [rows(width)] + [whole((width, 2 * heads_here))] * 2
        ),
        out_shape=[
            jax.ShapeDtypeStruct((part, width), F32),
            jax.ShapeDtypeStruct((part, width), BF16),
            jax.ShapeDtypeStruct((part, 2 * hidden), BF16),
            jax.ShapeDtypeStruct((part, 2 * hidden), F32),
        ]
        + (
            [jax.ShapeDtypeStruct((block, width), BF16)] * (part // block)
            if to_send
            else [jax.ShapeDtypeStruct((part, width), F32)]
            + [jax.ShapeDtypeStruct((width, 2 * heads_here), BF16)] * 2
        ),
        compiler_params=params(20),
        cost_estimate=took(10),
        name="forward",
    )(*atts, tok, *fixed)


def loss_kernel(
    part, n, pos, lens, stream, own, other, table, teacher, count, *refs
):
    out, grad_ref, low_ref, sums_ref, send = refs[-5:]
    block, width = stream.shape
    counted = count[0:1, 0:1].astype(F32)
    token = pos[0] * part + n * block + lax.broadcasted_iota(jnp.int32, (block, 1), 0)
    valid = (token < picture_ends(lens)[-1]).astype(F32)
    result = stream[...] + (own[...] + other[...].astype(F32)) + line(table, DOWN_BIAS)
    out[...] = result.astype(BF16)
    error = (result - teacher[...].astype(F32)) * valid
    grad = error * (2.0 / counted)
    grad_ref[...] = grad
    low = grad.astype(BF16)
    low_ref[...] = low
    send[...] = low
    old = refs[3][...] if len(refs) > 5 else jnp.zeros_like(sums_ref)
    sums_ref[...] = old
    sums_ref[0:1, :] += jnp.sum(low.astype(F32), axis=0, keepdims=True)
    squares = jnp.sum(error * error, axis=0, keepdims=True)
    sums_ref[1:2, :] += squares / counted


def loss_call(n, me, lengths, stream, own, other, table, teacher, count, before):
    part, width = stream.shape
    block = other.shape[0]
    rows = pl.BlockSpec((block, width), lambda i, s, r: (n, 0))
    piece = whole((block, width))
    return pl.pallas_call(
        partial(loss_kernel, part, n),
        grid_spec=pltpu.PrefetchScalarGridSpec(
            num_scalar_prefetch=2,
            grid=(1,),
            in_specs=[rows, rows, piece, whole(table.shape), rows, whole(count.shape)]
            + [pl.BlockSpec(memory_space=pl.ANY)] * (3 if before else 0)
            + [whole((8, width))] * (1 if before else 0),
            out_specs=[rows, rows, rows, whole((8, width)), piece],
        ),
        out_shape=[
            jax.ShapeDtypeStruct((part, width), BF16),
            pltpu.HBM((part, width), F32),
            jax.ShapeDtypeStruct((part, width), BF16),
            jax.ShapeDtypeStruct((8, width), F32),
            jax.ShapeDtypeStruct((block, width), BF16),
        ],
        input_output_aliases={8: 0, 9: 1, 10: 2} if before else {},
        compiler_params=params(8),
        cost_estimate=took(3),
        name="loss",
    )(me, lengths, stream, own, other, table, teacher, count, *before)


def backward_kernel(hidden, blocks, first, *refs):
    grad, slope, w_own, w_sib = refs[:4]
    low_ref, grad_ref, part_ref, bias_ref = refs[-4:]

    @pl.when(pl.program_id(0) == 0)
    def _():
        bias_ref[...] = jnp.zeros_like(bias_ref) if first else refs[7][...]

    total = None
    for n, source in enumerate((w_own, w_sib)):
        cols = slice(n * hidden, (n + 1) * hidden)
        low = (mm(grad[...], source[:, hidden : 2 * hidden]) * slope[:, cols]).astype(BF16)
        low_ref[:, cols] = low
        bias_ref[:, cols] += jnp.sum(low.astype(F32), axis=0, keepdims=True)
        term = mm(low, source[:, :hidden], NT)
        total = term if total is None else total + term
    grad_ref[...] = grad[...]
    part_ref[...] = total.astype(part_ref.dtype)


def backward_call(grad, slope, w_own, w_sib, hidden, part_type, n=0, before=()):
    part = slope.shape[0]
    height, width = grad.shape
    block = min(TILE, part)
    start = n * height // block

    def rows(cols):
        return pl.BlockSpec((block, cols), lambda i: (start + i, 0))

    here = pl.BlockSpec((block, width), lambda i: (i, 0))
    return pl.pallas_call(
        partial(backward_kernel, hidden, height // block, not before),
        grid=(height // block,),
        in_specs=[here, rows(2 * hidden)]
        + [inside()] * 2
        + [pl.BlockSpec(memory_space=pl.ANY)] * (3 if before else 0)
        + [whole((1, 2 * hidden))] * (1 if before else 0),
        out_specs=[rows(2 * hidden), rows(width), rows(width), whole((1, 2 * hidden))],
        out_shape=[
            jax.ShapeDtypeStruct((part, 2 * hidden), BF16),
            jax.ShapeDtypeStruct((part, width), BF16),
            (pltpu.HBM if part_type == F32 else jax.ShapeDtypeStruct)((part, width), part_type),
            jax.ShapeDtypeStruct((1, 2 * hidden), F32),
        ],
        input_output_aliases={4: 0, 5: 1, 6: 2} if before else {},
        compiler_params=params(14),
        cost_estimate=took(6 if part_type == BF16 else 0.1),
        name="backward",
    )(grad, slope, w_own, w_sib, *before)


def weight_terms_kernel(count, *refs):
    lefts, rights = refs[: 2 * count], refs[2 * count : 4 * count]
    come, out = refs[4 * count : -1], refs[-1]
    dims = (((0,), (0,)), ((), ()))
    half = out.shape[1] // 2
    for n in range(2):
        total = sum(mm(lefts[n * count + m][...], rights[n * count + m][...], dims) for m in range(count))
        cols = slice(n * half, (n + 1) * half)
        if come:
            total = total + come[0][:, cols].astype(F32)
        out[:, cols] = total.astype(BF16)


def weight_terms_call(lefts, rights, side, hidden, come):
    count = len(lefts[0])
    part, width = lefts[0][0].shape
    shape = (width, 2 * hidden)
    more = [] if come is None else [come]
    return pl.pallas_call(
        partial(weight_terms_kernel, count),
        grid=(1,),
        in_specs=[once((part, width))] * (2 * count)
        + [
            pl.BlockSpec((part, hidden), lambda i: (0, side), pipeline_mode=pl.Buffered(1))
        ]
        * (2 * count)
        + [once(shape)] * len(more),
        out_specs=once(shape),
        out_shape=jax.ShapeDtypeStruct(shape, BF16),
        compiler_params=params(26),
        cost_estimate=took(0.1),
        name="weight_terms",
    )(*lefts[0], *lefts[1], *rights[0], *rights[1], *more)


def out_terms_kernel(low, att_0, att_1, att_2, att_3, sent, kept):
    size = att_0.shape[0]
    for n, (first, second) in enumerate(((att_1, att_3), (att_0, att_2))):
        both = mm(jnp.concatenate([first[...], second[...]], axis=0), low[...]).T
        if n == 0:
            sent[...] = both.astype(BF16)
        else:
            kept[...] = both


def out_terms_call(low, atts):
    width = low.shape[1]
    cols = 2 * atts[0].shape[0]
    return pl.pallas_call(
        out_terms_kernel,
        out_shape=[
            jax.ShapeDtypeStruct((width, cols), BF16),
            jax.ShapeDtypeStruct((width, cols), F32),
        ],
        compiler_params=params(16),
        cost_estimate=took(0.1),
        name="out_terms",
    )(low, *atts)


def second_kernel(
    own, other, stream, result_grad, table, out_own, out_sib, *outs
):
    grad_ref, low_ref, sums_ref = outs[:3]
    heads_refs = outs[3:]

    @pl.when(pl.program_id(0) == 0)
    def _():
        sums_ref[...] = jnp.zeros_like(sums_ref)

    second_grad = own[...] + other[...].astype(F32)
    hat, factor = rows_hat(stream[...])
    sums_ref[0:1, :] += jnp.sum(second_grad * hat, axis=0, keepdims=True)
    sums_ref[1:2, :] += jnp.sum(second_grad, axis=0, keepdims=True)
    stream_grad = result_grad[...] + rows_back(second_grad * line(table, GAIN_2), hat, factor)
    grad_ref[...] = stream_grad
    low = stream_grad.astype(BF16)
    low_ref[...] = low
    sums_ref[2:3, :] += jnp.sum(low.astype(F32), axis=0, keepdims=True)
    for n, weight in enumerate((out_own, out_sib)):
        both = mm(low, weight[...]).T.astype(BF16)
        rows = both.shape[0] // 2
        heads_refs[n][...] = both[:rows]
        heads_refs[n + 2][...] = both[rows:]


def second_call(own, other, stream, result_grad, table, out_weights, groups, heads_here):
    part, width = own.shape
    block = min(TILE, part)
    rows = pl.BlockSpec((block, width), lambda i: (i, 0))
    lanes = pl.BlockSpec((heads_here, block), lambda i: (0, i))
    return pl.pallas_call(
        second_kernel,
        grid=(part // block,),
        in_specs=[rows] * 4
        + [once(table.shape)]
        + [once((width, 2 * heads_here))] * 2,
        out_specs=[rows, rows, whole((8, width))] + [lanes] * groups,
        out_shape=[
            jax.ShapeDtypeStruct((part, width), F32),
            jax.ShapeDtypeStruct((part, width), BF16),
            jax.ShapeDtypeStruct((8, width), F32),
        ]
        + [jax.ShapeDtypeStruct((heads_here, part), BF16)] * groups,
        compiler_params=params(56),
        cost_estimate=took(5),
        name="second_back",
    )(own, other, stream, result_grad, table, *out_weights)


def first_grad_kernel(wide, order, mixed, weight, *refs):
    count = len(order)
    toks = refs[:count]
    sums_ref = refs[count]
    outs = refs[count + 1 :]

    @pl.when(pl.program_id(0) == 0)
    def _():
        sums_ref[...] = jnp.zeros_like(sums_ref)

    for n, j in enumerate(order):
        grad = mm(weight[...], mixed[j]).T
        hat, _ = rows_hat(toks[n][...].astype(F32))
        sums_ref[0:1, :] += jnp.sum(grad * hat, axis=0, keepdims=True)
        sums_ref[1:2, :] += jnp.sum(grad, axis=0, keepdims=True)
        outs[0][n] = grad.astype(outs[0].dtype)


def first_grad_call(mixed, weight, toks, order, out_type):
    groups, wide, part = mixed.shape
    width = weight.shape[0]
    block = min(TILE, part)
    rows = pl.BlockSpec((block, width), lambda i: (i, 0))
    return pl.pallas_call(
        partial(first_grad_kernel, wide, order),
        grid=(part // block,),
        in_specs=[pl.BlockSpec((groups, wide, block), lambda i: (0, 0, i)), inside()]
        + [rows] * len(order),
        out_specs=[
            whole((8, width)),
            pl.BlockSpec((len(order), block, width), lambda i: (0, i, 0)),
        ],
        out_shape=[
            jax.ShapeDtypeStruct((8, width), F32),
            jax.ShapeDtypeStruct((len(order), part, width), out_type),
        ],
        compiler_params=params(16),
        cost_estimate=took(0.1),
        name="first_grad",
    )(mixed, weight, *[toks[j] for j in order])


def late_terms_kernel(bit, lows, mixed, out_terms, sent, kept):
    total = None
    for j in range(4):
        term = mm(mixed[j], lows[j])
        total = term if total is None else total + term
    wide = total.shape[0]

    @pl.when(pl.program_id(0) == 0)
    def _():
        sent[:, :wide] = total.T.astype(BF16)
        sent[:, wide:] = out_terms[...].astype(BF16)

    @pl.when(pl.program_id(0) == 1)
    def _():
        kept[:, :wide] = total.T
        kept[:, wide:] = out_terms[...]


def late_terms_call(lows, mixed, out_terms):
    part, width = lows.shape[1:]
    wide = mixed.shape[1]
    cols = wide + out_terms.shape[1]
    half = width // 2
    bit = top_bit("dp")[0].reshape(1)

    def side(i, s):
        return s[0] ^ 1 ^ i

    return pl.pallas_call(
        late_terms_kernel,
        grid_spec=pltpu.PrefetchScalarGridSpec(
            num_scalar_prefetch=1,
            grid=(2,),
            in_specs=[
                pl.BlockSpec((4, part, half), lambda i, s: (0, 0, side(i, s))),
                inside(),
                pl.BlockSpec((half, out_terms.shape[1]), lambda i, s: (side(i, s), 0)),
            ],
            out_specs=[whole((half, cols)), whole((half, cols))],
        ),
        out_shape=[
            jax.ShapeDtypeStruct((half, cols), BF16),
            jax.ShapeDtypeStruct((half, cols), F32),
        ],
        compiler_params=params(20),
        cost_estimate=took(5),
        name="late_terms",
    )(bit, lows, mixed, out_terms)


def late_final_kernel(kept, come, in_ref, out_ref):
    total = kept[...] + come[...].astype(F32)
    wide = in_ref.shape[1]
    in_ref[...] = total[:, :wide]
    out_ref[...] = total[:, wide:].T


def late_final_call(kept, come, wide):
    rows, cols = kept.shape
    return pl.pallas_call(
        late_final_kernel,
        out_shape=[
            jax.ShapeDtypeStruct((rows, wide), F32),
            jax.ShapeDtypeStruct((cols - wide, rows), F32),
        ],
        compiler_params=params(6),
        cost_estimate=took(1),
        name="late_final",
    )(kept, come)


def weight_final_kernel(grads, up_ref, down_ref):
    half = up_ref.shape[1]
    up_ref[...] = grads[:, :half].astype(F32)
    down_ref[...] = grads[:, half:].astype(F32).T


def weight_final_call(grads):
    rows, cols = grads.shape
    half = cols // 2
    return pl.pallas_call(
        weight_final_kernel,
        out_shape=[
            jax.ShapeDtypeStruct((rows, half), F32),
            jax.ShapeDtypeStruct((half, rows), F32),
        ],
        compiler_params=params(6),
        cost_estimate=took(1),
        name="weight_final",
    )(grads)


def pair_kernel(own, come, out):
    out[...] = (own[0] + come[0].astype(F32)).astype(BF16)


def pair_call(own, come):
    part, width = own.shape[1:]
    block = min(TILE, part)
    second = pl.BlockSpec((1, block, width), lambda i: (1, i, 0))
    return pl.pallas_call(
        pair_kernel,
        grid=(part // block,),
        in_specs=[second] * 2,
        out_specs=pl.BlockSpec((block, width), lambda i: (i, 0)),
        out_shape=jax.ShapeDtypeStruct((part, width), BF16),
        compiler_params=params(8),
        cost_estimate=took(0.1),
        name="pair",
    )(own, come)


def first_back_kernel(own, come, other, tok, stream_grad, table, out_ref):
    hat, factor = rows_hat(tok[...].astype(F32))
    grad = own[0] + come[0].astype(F32) + other[...].astype(F32)
    out_ref[...] = stream_grad[...] + rows_back(grad * line(table, GAIN_1), hat, factor)


def first_back_call(own, come, other, tok, stream_grad, table):
    part, width = tok.shape
    block = min(TILE, part)
    rows = pl.BlockSpec((block, width), lambda i: (i, 0))
    return pl.pallas_call(
        first_back_kernel,
        grid=(part // block,),
        in_specs=[pl.BlockSpec((1, block, width), lambda i: (0, i, 0))] * 2
        + [rows] * 3
        + [whole(table.shape)],
        out_specs=rows,
        out_shape=jax.ShapeDtypeStruct((part, width), F32),
        compiler_params=params(10),
        cost_estimate=took(1),
        name="first_back",
    )(own, come, other, tok, stream_grad, table)


def own_rows(vector, group, amount):
    return lax.dynamic_slice_in_dim(vector, group * amount, amount)


def local(
    tokens,
    teacher,
    picture_lengths,
    first_gain,
    first_shift,
    input_weight,
    input_bias,
    query_gain,
    key_gain,
    output_weight,
    output_bias,
    second_gain,
    second_shift,
    expand_weight,
    expand_bias,
    reduce_weight,
    reduce_bias,
):
    assert tokens.shape[0] == 1 and lax.axis_size("gx") == 4
    part, width = tokens.shape[1:]
    groups = 4
    group = lax.axis_index("gx")
    hd = query_gain.shape[0]
    wide = input_weight.shape[1]
    heads = wide // (3 * hd)
    heads_here = heads * hd
    hidden = expand_weight.shape[1]
    shard_rows = input_weight.shape[0]

    me = group.reshape(1).astype(jnp.int32)
    lengths = picture_lengths[0]
    out_shard = output_weight.T
    out_pair = swap(out_shard, "gx", 2)
    tok0 = tokens[0]
    tok2 = swap(tok0, "gx", 2)
    table_rows = [first_gain, first_shift, second_gain, second_shift, output_bias, reduce_bias]
    table_rows += [own_rows(expand_bias, group, hidden), own_rows(expand_bias, group ^ 1, hidden)]
    table_rows += [jnp.pad(own_rows(input_bias, group, wide), (0, width - wide))]
    table = jnp.stack(table_rows)
    gains = jnp.stack([query_gain, key_gain], axis=1)
    counted = jnp.full((8, 128), jnp.sum(lengths), jnp.int32)
    in_part, w_own = input_weight, None
    for mask in reversed(bits_of("gy")):
        more = swap(counted, "gy", mask)
        in_part = joined("gy", mask, in_part, shard_rows, table, gains, more)
        counted = counted + more
        if w_own is None:
            w_own = lax.all_gather(
                after(
                    jnp.concatenate([expand_weight, reduce_weight.T, out_shard, out_pair], axis=1), in_part
                ),
                ("dp", "gy"),
                axis=0,
                tiled=True,
            )
    w_in = in_part
    for mask in bits_of("dp"):
        more = swap(counted, "dp", mask)
        w_in = joined("dp", mask, w_in, w_in.shape[0], more)
        counted = counted + more
    tok3 = swap(after(tok2, w_in), "gx", 1)
    tok1 = swap(after(tok0, in_part), "gx", 1)
    toks = (tok0, tok1, tok2, tok3)

    low, mixed, hats, scales = mixed_call(toks, table, w_in, gains, heads, hd)
    *atts, raw, log = attend_call(me, lengths, mixed, heads, hd)
    att_pair = [atts[2]] + [swap(atts[j ^ 2], "gx", j) for j in range(1, 4)]
    w_own = after(w_own, raw, att_pair[2])
    w_sib = swap(w_own, "gx", 1)
    atts = after(atts, *att_pair)
    att_own = [atts[0]] + [swap(atts[j], "gx", j) for j in range(1, 4)]

    def forward_of(pieces, tok, to_send):
        return forward_call(pieces, tok, w_own, w_sib, table, hidden, to_send)

    _, low_p, active_p, slope_p, *parts_p = forward_of(att_pair, tok2, True)
    stream, low_o, active_o, slope_o, part_o, *out_weights = forward_of(att_own, tok0, False)
    parts_in = [swap(parts_p[0], "gx", 2)]
    parts_in += [swap(after(piece, part_o), "gx", 2) for piece in parts_p[1:]]
    state, pairs = (), []
    for n, piece in enumerate(parts_in):
        if state:
            piece = after(piece, state[0])
        *state, low_sent = loss_call(
            n, me, lengths, stream, part_o, piece, table, teacher[0], counted, state
        )
        pairs.append(swap(low_sent, "gx", 2))
    layer_output, result_grad, reduce_low, sums_3 = state

    hidden_o, _, back_o, up_sum_o = backward_call(reduce_low, slope_o, w_own, w_sib, hidden, F32)
    state = ()
    for n, piece in enumerate(pairs):
        if state:
            piece = after(piece, state[0])
        state = backward_call(piece, slope_p, w_own, w_sib, hidden, BF16, n, state)
    hidden_p, reduce_pair, back_p, up_sum_p = state
    back_in = swap(back_p, "gx", 2)

    lefts = ((low_o, low_p), (reduce_low, reduce_pair))
    rights = ((hidden_o, hidden_p), (active_o, active_p))
    sib_terms = swap(weight_terms_call(lefts, rights, 1, hidden, None), "gx", 1)
    weight_terms = weight_terms_call(lefts, rights, 0, hidden, sib_terms)
    weight_grads = lax.psum_scatter(weight_terms, ("dp", "gy"), scatter_dimension=0, tiled=True)
    stream_grad, branch_low, sums_2, *heads_grad = second_call(
        back_o,
        after(back_in, weight_terms),
        stream,
        result_grad,
        table,
        out_weights,
        groups,
        heads_here,
    )
    grads = [heads_grad[0]] + [swap(heads_grad[j], "gx", j) for j in range(1, 4)]

    out_sent, out_held = out_terms_call(branch_low, att_own)
    out_held = out_held + swap(out_sent, "gx", 1).astype(F32)
    out_own = out_held[:, :heads_here] + swap(
        out_held[:, heads_here:].astype(BF16), "gx", 2
    ).astype(F32)

    mixed_low, gain_sums, bias_sums = attend_back_call(
        me, lengths, mixed, hats, scales, raw, log, grads, gains, heads, hd
    )
    sums_s, sent = first_grad_call(after(mixed_low, out_own), w_in, toks, (1, 3), BF16)
    sib_in = swap(sent, "gx", 1)
    late_sent, late_kept = late_terms_call(low, after(mixed_low, sent), out_own)
    come = swap(late_sent, "dp", top_bit("dp")[1])
    sums_k, kept = first_grad_call(after(mixed_low, late_kept), w_in, toks, (0, 2), F32)
    pair_sent = pair_call(kept, sib_in)
    pair_in = swap(pair_sent, "gx", 2)

    sums = pack_call(
        me, groups, up_sum_o, up_sum_p, sums_2, sums_3, sums_s, sums_k, bias_sums, gain_sums
    )
    sums = after(sums, pair_sent)
    sums = sum_over(sums + swap(sums, "gx", 1), "gy")
    come = after(come, sums, weight_grads)
    for mask in reversed(bits_of("dp")[:-1]):
        late_kept, come = halved("dp", mask, late_kept, come, late_kept.shape[0] // 2)
    first, *others = bits_of("gy")
    late_kept, come = halved("gy", first, late_kept, come, shard_rows)
    sums = sum_over(after(sums, late_kept), "dp")
    come = after(come, sums)
    tokens_gradient = first_back_call(kept, sib_in, pair_in, tok0, stream_grad, table)
    for mask in others:
        late_kept, come = halved("gy", mask, late_kept, come, shard_rows)
    sums = sums + swap(after(sums, tokens_gradient, late_kept), "gx", 2)
    expand_out, reduce_out = weight_final_call(after(weight_grads, late_kept))
    input_out, output_out = late_final_call(late_kept, after(come, sums), wide)
    row = 2 * groups
    return (
        layer_output[None],
        jnp.sum(sums[row + 4]),
        tokens_gradient[None],
        sums[row + 5],
        sums[row + 6],
        input_out,
        sums[groups:row, :wide].reshape(-1),
        sums[row + 7, :hd],
        sums[row + 7, hd : 2 * hd],
        output_out,
        sums[row + 2],
        sums[row],
        sums[row + 1],
        expand_out,
        sums[:groups, :hidden].reshape(-1),
        reduce_out,
        sums[row + 3],
    )


def solution(mesh):
    rows = P(("dp", "gy"), "gx", None)
    by_rows = P(("dp", "gy"), "gx")
    by_cols = P("gx", ("dp", "gy"))
    return jax.shard_map(
        local,
        mesh=mesh,
        in_specs=(
            rows,
            rows,
            P(("dp", "gy"), None),
            P(),
            P(),
            by_rows,
            P(),
            P(),
            P(),
            by_cols,
            P(),
            P(),
            P(),
            by_rows,
            P(),
            by_cols,
            P(),
        ),
        out_specs=(
            rows,
            P(),
            rows,
            P(),
            P(),
            by_rows,
            P(),
            P(),
            P(),
            by_cols,
            P(),
            P(),
            P(),
            by_rows,
            P(),
            by_cols,
            P(),
        ),
        check_vma=False,
    )
```

```python
from functools import partial

import jax
import jax.numpy as jnp
from jax import lax
from jax.experimental import pallas as pl
from jax.experimental.pallas import tpu as pltpu
from jax.sharding import PartitionSpec as P

EPS = 1e-06
APART = 1024.0
TILE = 256
KEY_TILE = 512
BACK_KEY_TILE = 256
MIB = 1 << 20
F32 = jnp.float32
BF16 = jnp.bfloat16

NN = (((1,), (0,)), ((), ()))
NT = (((1,), (1,)), ((), ()))


def mm(left, right, dims=NN):
    return lax.dot_general(left, right, dims, preferred_element_type=F32)


def took(us):
    return pl.CostEstimate(flops=int(us * 1.15e9), bytes_accessed=0, transcendentals=0)


def params(limit):
    return pltpu.CompilerParams(vmem_limit_bytes=limit * MIB)


def whole(shape):
    rank = len(shape)
    return pl.BlockSpec(shape, lambda *_: (0,) * rank)


def inside():
    return pl.BlockSpec(memory_space=pltpu.VMEM)


def once(shape):
    rank = len(shape)
    return pl.BlockSpec(shape, lambda *_: (0,) * rank, pipeline_mode=pl.Buffered(1))


def rows_hat(values):
    mean = jnp.mean(values, axis=-1, keepdims=True)
    centered = values - mean
    factor = lax.rsqrt(jnp.mean(centered * centered, axis=-1, keepdims=True) + EPS)
    return centered * factor, factor


def rows_back(grad_hat, hat, factor):
    return factor * (
        grad_hat
        - jnp.mean(grad_hat, axis=-1, keepdims=True)
        - hat * jnp.mean(grad_hat * hat, axis=-1, keepdims=True)
    )


def swap(array, axis, mask):
    size = lax.axis_size(axis)
    return lax.ppermute(array, axis, [(i, i ^ mask) for i in range(size)])


def bits_of(axis):
    size = lax.axis_size(axis)
    masks = []
    mask = 1
    while mask < size:
        masks.append(mask)
        mask *= 2
    return masks


def order_kernel(blocks, rows, pos, *refs):
    pieces, out = refs[:-1], refs[-1]
    count = len(pieces)
    for j in range(count):
        for d in range(blocks):
            start = pl.multiple_of((d * count + (pos[0] ^ j)) * rows, rows)
            out[pl.ds(start, rows), :] = pieces[j][d * rows : (d + 1) * rows, :]


def ordered(pieces, rows, me):
    height, cols = pieces[0].shape
    count = len(pieces)
    if rows % 16:
        out = jnp.zeros((height // rows, count, rows, cols), pieces[0].dtype)
        for j, piece in enumerate(pieces):
            piece = piece.reshape(-1, 1, rows, cols)
            out = lax.dynamic_update_slice(out, piece, (0, me ^ j, 0, 0))
        return out.reshape(height * count, cols)
    return pl.pallas_call(
        partial(order_kernel, height // rows, rows),
        grid_spec=pltpu.PrefetchScalarGridSpec(
            num_scalar_prefetch=1,
            grid=(1,),
            in_specs=[inside()] * count,
            out_specs=inside(),
        ),
        out_shape=jax.ShapeDtypeStruct((height * count, cols), pieces[0].dtype),
        compiler_params=params(10),
        cost_estimate=took(1),
        name="ordered",
    )(me.reshape(1).astype(jnp.int32), *pieces)


def joined(axis, mask, held, rows, *earlier):
    mine = ((lax.axis_index(axis) & mask) != 0).astype(jnp.int32)
    return ordered([held, after(swap(held, axis, mask), *earlier)], rows, mine)


def along_gy(held, rows, *earlier):
    for mask in reversed(bits_of("gy")):
        held = joined("gy", mask, held, rows, *earlier)
    return held


def along_dp(held, *earlier):
    for mask in bits_of("dp"):
        held = joined("dp", mask, held, held.shape[0], *earlier)
    return held


def top_bit(axis):
    mask = bits_of(axis)[-1]
    return ((lax.axis_index(axis) & mask) != 0).astype(jnp.int32), mask


def step_kernel(blocks, rows, bit, kept, come, out, keep):
    for d in range(blocks):
        for side in range(2):
            span = slice((2 * d + side) * rows, (2 * d + side + 1) * rows)
            total = kept[span, :] + come[span, :].astype(F32)
            to = slice(d * rows, (d + 1) * rows)

            @pl.when(bit[0] == side)
            def _():
                keep[to, :] = total

            @pl.when(bit[0] != side)
            def _():
                out[to, :] = total.astype(BF16)


def step_call(bit, kept, come, rows):
    height, cols = kept.shape
    half = (height // 2, cols)
    return pl.pallas_call(
        partial(step_kernel, height // (2 * rows), rows),
        grid_spec=pltpu.PrefetchScalarGridSpec(
            num_scalar_prefetch=1,
            grid=(1,),
            in_specs=[inside()] * 2,
            out_specs=[inside()] * 2,
        ),
        out_shape=[jax.ShapeDtypeStruct(half, BF16), jax.ShapeDtypeStruct(half, F32)],
        compiler_params=params(12),
        cost_estimate=took(1),
        name="scatter_step",
    )(bit.reshape(1), kept, come)


def halved(axis, mask, kept, come, rows):
    bit = ((lax.axis_index(axis) & mask) != 0).astype(jnp.int32)
    out, kept = step_call(bit, kept, come, rows)
    return kept, swap(out, axis, mask)


def after(value, *earlier):
    return lax.optimization_barrier((value, *earlier))[0]


def sum_over(values, axis):
    for mask in bits_of(axis):
        values = values + swap(values, axis, mask)
    return values


GAIN_1, SHIFT_1, GAIN_2, SHIFT_2, OUT_BIAS, DOWN_BIAS, UP_BIAS, UP_BIAS_SIB, IN_BIAS = range(9)


def line(table, row):
    return table[row : row + 1, :]


def pack_kernel(groups, me, up_o, up_p, early_2, early_3, late_s, late_k, bias, gains, out):
    width = out.shape[1]
    wide = bias.shape[0]
    out[...] = jnp.zeros_like(out)
    up = up_o[...] + up_p[...]
    out[pl.ds(me[0], 1), :] = up[:, :width]
    out[pl.ds(me[0] ^ 1, 1), :] = up[:, width:]
    out[pl.ds(groups + me[0], 1), 0:wide] = jnp.sum(bias[...].T, axis=0, keepdims=True)
    row = 2 * groups
    out[row : row + 3, :] = early_2[0:3, :]
    out[row + 3 : row + 5, :] = early_3[0:2, :]
    out[row + 5 : row + 7, :] = late_s[0:2, :] + late_k[0:2, :]
    out[row + 7 : row + 8, 0 : gains.shape[0]] = jnp.sum(gains[...].T, axis=0, keepdims=True)


def pack_call(me, groups, *parts):
    width = parts[2].shape[1]
    return pl.pallas_call(
        partial(pack_kernel, groups),
        grid_spec=pltpu.PrefetchScalarGridSpec(
            num_scalar_prefetch=1,
            grid=(1,),
            in_specs=[whole(a.shape) for a in parts],
            out_specs=whole((2 * groups + 8, width)),
        ),
        out_shape=jax.ShapeDtypeStruct((2 * groups + 8, width), F32),
        compiler_params=params(6),
        cost_estimate=took(1),
        name="pack",
    )(me, *parts)


def mixed_kernel(count, heads, hd, *refs):
    toks = refs[:count]
    table, weight, gains = refs[count : count + 3]
    low_ref, mixed_ref, kept_ref, hat_ref, scale_ref = refs[count + 3 :]
    wide = heads * 3 * hd
    gain, shift, bias = line(table, GAIN_1), line(table, SHIFT_1), line(table, IN_BIAS)[:, :wide]
    q_gain, k_gain = gains[:, 0:1], gains[:, 1:2]
    for j in range(count):
        hat, _ = rows_hat(toks[j][...].astype(F32))
        low = (hat * gain + shift).astype(BF16)
        low_ref[j] = low
        mixed = (mm(low, weight[...]) + bias).T
        scales = []
        for h in range(heads):
            for kind, a_gain, factor in ((0, q_gain, hd**-0.5), (1, k_gain, 1.0)):
                start = (h * 3 + kind) * hd
                raw = mixed[start : start + hd]
                centered = raw - jnp.mean(raw, axis=0, keepdims=True)
                scale = lax.rsqrt(jnp.mean(centered * centered, axis=0, keepdims=True) + EPS)
                unit = centered * scale
                hat_ref[j, (h * 2 + kind) * hd : (h * 2 + kind + 1) * hd, :] = unit
                scales.append(scale)
                normed = (unit * a_gain).astype(BF16)
                if factor != 1.0:
                    normed = normed * jnp.asarray(factor, BF16)
                mixed_ref[j, start : start + hd, :] = normed
            start = (h * 3 + 2) * hd
            mixed_ref[j, start : start + hd, :] = mixed[start : start + hd].astype(BF16)
        kept_ref[j] = mixed_ref[j]
        for n, scale in enumerate(scales):
            scale_ref[j, n : n + 1, :] = scale


def mixed_call(pieces, table, weight, gains, heads, hd):
    count = len(pieces)
    part, width = pieces[0].shape
    block = min(TILE, part)
    wide = heads * 3 * hd
    piece_spec = pl.BlockSpec((block, width), lambda i: (i, 0))

    def lanes(rows):
        return pl.BlockSpec((count, rows, block), lambda i: (0, 0, i))

    scale_rows = 8 * -(-2 * heads // 8)
    return pl.pallas_call(
        partial(mixed_kernel, count, heads, hd),
        grid=(part // block,),
        in_specs=[piece_spec] * count
        + [whole(a.shape) for a in (table, weight, gains)],
        out_specs=[
            pl.BlockSpec((count, block, width), lambda i: (0, i, 0)),
            lanes(wide),
            lanes(wide),
            lanes(heads * 2 * hd),
            lanes(scale_rows),
        ],
        out_shape=[
            pltpu.HBM((count, part, width), BF16),
            jax.ShapeDtypeStruct((count, wide, part), BF16),
            pltpu.HBM((count, wide, part), BF16),
            pltpu.HBM((count, heads * 2 * hd, part), F32),
            jax.ShapeDtypeStruct((count, scale_rows, part), F32),
        ],
        compiler_params=params(24),
        cost_estimate=took(6),
        name="mixed",
    )(*pieces, table, weight, gains)


def picture_ends(lengths):
    ends = []
    total = jnp.int32(0)
    for k in range(lengths.shape[0]):
        total = total + lengths[k]
        ends.append(total)
    return ends


def key_tiles(ends, first, amount, row, tile):
    begin, until = jnp.int32(0), jnp.int32(row)
    for end in ends:
        begin = jnp.where(end <= first, end, begin)
    for end in reversed(ends):
        until = jnp.where(end >= first + amount, end, until)
    return lax.div(begin, tile), lax.div(until + tile - 1, tile)


def one_hot(ends, start, amount):
    place = start + lax.broadcasted_iota(jnp.int32, (1, amount), 1)
    number = jnp.zeros((1, amount), jnp.int32)
    for end in ends:
        number = number + (end <= place).astype(jnp.int32)
    return (lax.broadcasted_iota(jnp.int32, (32, amount), 0) == number).astype(F32)


def lay_out(me, ends, source, heads, hd, part, keys_tok, queries_lane):
    for j in range(4):
        start = pl.multiple_of((me ^ j) * part, part)
        marks = one_hot(ends, start, part)
        away = ((marks - 1.0) * APART).astype(BF16)
        blank = jnp.zeros((32, part), F32)
        for h in range(heads):
            base = h * 3 * hd
            queries_lane[h, 0:hd, pl.ds(start, part)] = source[j, base : base + hd, :]
            queries_lane[h, hd : hd + 32, pl.ds(start, part)] = away
            queries_lane[h, hd + 32 : hd + 64, pl.ds(start, part)] = blank.astype(BF16)
            key = source[j, base + hd : base + 2 * hd, :].astype(F32)
            keys_tok[h, pl.ds(start, part), :] = (
                jnp.concatenate([key, marks, blank], axis=0).T.astype(BF16)
            )


def attend_kernel(
    heads, hd, part, pos, lens, mixed, a0, a1, a2, a3, raw, log, keys_tok, queries_lane, vals, acc
):
    i = pl.program_id(0)
    block = part
    me = pos[0]
    ends = picture_ends(lens)

    @pl.when(i == 0)
    def _():
        lay_out(me, ends, mixed, heads, hd, part, keys_tok, queries_lane)
        for j in range(4):
            start = pl.multiple_of((me ^ j) * part, part)
            for h in range(heads):
                base = (h * 3 + 2) * hd
                vals[h, 0:hd, pl.ds(start, part)] = mixed[j, base : base + hd, :]
                vals[h, hd : hd + 16, pl.ds(start, part)] = jnp.ones((16, part), BF16)

    own = pl.ds(pl.multiple_of(i * block, block), block)
    acc[...] = jnp.zeros_like(acc)

    def step(t, carry):
        there = pl.ds(pl.multiple_of(t * KEY_TILE, KEY_TILE), KEY_TILE)
        scores = [mm(keys_tok[h, there, :], queries_lane[h, :, own]) for h in range(heads)]
        weights = [jnp.exp(scores[h]).astype(BF16) for h in range(heads)]
        for h in range(heads):
            acc[h] += mm(vals[h, :, there], weights[h])
        return carry

    low, high = key_tiles(ends, i * block, block, 4 * part, KEY_TILE)
    lax.fori_loop(low, high, step, 0)
    for h in range(heads):
        total = acc[h, hd : hd + 1, :]
        raw[0, h * hd : (h + 1) * hd, :] = acc[h, 0:hd, :] / total
        log[0, h : h + 1, :] = jnp.log(total)
    for j, att in enumerate((a0, a1, a2, a3)):

        @pl.when((i ^ me) == j)
        def _():
            att[...] = raw[0].astype(BF16)


def attend_call(me, lengths, mixed, heads, hd):
    part = mixed.shape[2]
    row = 4 * part

    def lanes(rows):
        return pl.BlockSpec((1, rows, part), lambda i, s, n: (i ^ s[0], 0, 0))

    return pl.pallas_call(
        partial(attend_kernel, heads, hd, part),
        grid_spec=pltpu.PrefetchScalarGridSpec(
            num_scalar_prefetch=2,
            grid=(4,),
            in_specs=[inside()],
            out_specs=[once((heads * hd, part))] * 4 + [lanes(heads * hd), lanes(8)],
            scratch_shapes=[
                pltpu.VMEM((heads, row, 2 * hd), BF16),
                pltpu.VMEM((heads, 2 * hd, row), BF16),
                pltpu.VMEM((heads, hd + 16, row), BF16),
                pltpu.VMEM((heads, hd + 16, part), F32),
            ],
        ),
        out_shape=[jax.ShapeDtypeStruct((heads * hd, part), BF16)] * 4
        + [
            pltpu.HBM((4, heads * hd, part), F32),
            jax.ShapeDtypeStruct((4, 8, part), F32),
        ],
        compiler_params=params(20),
        cost_estimate=took(11),
        name="attend",
    )(me, lengths, mixed)


def attend_back_kernel(
    heads,
    hd,
    part,
    pos,
    lens,
    mixed,
    hats,
    scales,
    raw,
    log,
    d0,
    d1,
    d2,
    d3,
    gains,
    out_ref,
    gain_ref,
    bias_ref,
    keys_tok,
    queries_lane,
    vals_tok,
    keys_lane,
    grads_lane,
    log_row,
    inner_row,
    d_key,
    d_val,
    d_query,
):
    i = pl.program_id(0)
    blocks = pl.num_programs(0)
    block = part
    me = pos[0]
    grads = (d0, d1, d2, d3)
    ends = picture_ends(lens)
    q_gain, k_gain = gains[:, 0:1], gains[:, 1:2]

    @pl.when(i == 0)
    def _():
        lay_out(me, ends, mixed, heads, hd, part, keys_tok, queries_lane)
        for j in range(4):
            start = pl.multiple_of((me ^ j) * part, part)
            there = pl.ds(start, part)
            log_row[:, there] = log[j]
            for h in range(heads):
                base = h * 3 * hd
                keys_lane[h, :, there] = mixed[j, base + hd : base + 2 * hd, :]
                vals_tok[h, there, :] = (
                    mixed[j, base + 2 * hd : base + 3 * hd, :].astype(F32).T.astype(BF16)
                )
                grad = grads[j][h * hd : (h + 1) * hd, :]
                grads_lane[h, :, there] = grad
                inner_row[h : h + 1, there] = jnp.sum(
                    grad.astype(F32) * raw[j, h * hd : (h + 1) * hd, :], axis=0, keepdims=True
                )
        d_key[...] = jnp.zeros_like(d_key)
        d_val[...] = jnp.zeros_like(d_val)

    own = pl.ds(pl.multiple_of(i * block, block), block)
    d_query[:, :, own] = jnp.zeros((heads, hd, block), F32)
    low, high = key_tiles(ends, i * block, block, 4 * part, BACK_KEY_TILE)
    high = jnp.minimum(high, lax.div(ends[-1] + BACK_KEY_TILE - 1, BACK_KEY_TILE))

    @pl.when((i * block < ends[-1]) & (high > low))
    def _():
        queries_tok = [queries_lane[h, 0:hd, own].astype(F32).T.astype(BF16) for h in range(heads)]
        grads_tok = [grads_lane[h, :, own].astype(F32).T.astype(BF16) for h in range(heads)]

        def step(t, carry):
            there = pl.ds(pl.multiple_of(t * BACK_KEY_TILE, BACK_KEY_TILE), BACK_KEY_TILE)
            each = range(heads)
            scores = [mm(keys_tok[h, there, :], queries_lane[h, :, own]) for h in each]
            chance_grad = [mm(vals_tok[h, there, :], grads_lane[h, :, own]) for h in each]
            chance = [jnp.exp(scores[h] - log_row[h : h + 1, own]) for h in each]
            chance_low = [chance[h].astype(BF16) for h in each]
            score_grad = [
                (chance[h] * (chance_grad[h] - inner_row[h : h + 1, own])).astype(BF16)
                for h in each
            ]
            for h in each:
                d_val[h, there, :] += mm(chance_low[h], grads_tok[h])
                d_key[h, there, :] += mm(score_grad[h], queries_tok[h])
                d_query[h, :, own] += mm(keys_lane[h, :, there], score_grad[h])
            return carry

        lax.fori_loop(low, high, step, 0)

    @pl.when(i == blocks - 1)
    def _():
        def fold(values):
            return sum(values[:, n * 128 : (n + 1) * 128] for n in range(values.shape[1] // 128))

        gain_ref[...] = jnp.zeros_like(gain_ref)
        bias_ref[...] = jnp.zeros_like(bias_ref)
        for j in range(4):
            start = pl.multiple_of((me ^ j) * part, part)
            there = pl.ds(start, part)
            for h in range(heads):
                for kind, a_gain in ((0, q_gain), (1, k_gain)):
                    if kind == 0:
                        grad = d_query[h, :, there] * hd**-0.5
                    else:
                        grad = d_key[h, there, :].T
                    slot = h * 2 + kind
                    hat = hats[j, slot * hd : (slot + 1) * hd, :]
                    scale = scales[j, slot : slot + 1, :]
                    gain_ref[kind * hd : (kind + 1) * hd, :] += fold(grad * hat)
                    inner = grad * a_gain
                    back = scale * (
                        inner
                        - jnp.mean(inner, axis=0, keepdims=True)
                        - hat * jnp.mean(inner * hat, axis=0, keepdims=True)
                    )
                    rows = slice((h * 3 + kind) * hd, (h * 3 + kind + 1) * hd)
                    back = back.astype(BF16)
                    out_ref[j, rows, :] = back
                    bias_ref[rows, :] += fold(back.astype(F32))
                rows = slice((h * 3 + 2) * hd, (h * 3 + 3) * hd)
                back = d_val[h, there, :].T.astype(BF16)
                out_ref[j, rows, :] = back
                bias_ref[rows, :] += fold(back.astype(F32))


def attend_back_call(me, lengths, mixed, hats, scales, raw, log, grads, gains, heads, hd):
    part = mixed.shape[2]
    row = 4 * part
    wide = heads * 3 * hd
    operands = (mixed, hats, scales, raw, log, *grads, gains)
    return pl.pallas_call(
        partial(attend_back_kernel, heads, hd, part),
        grid_spec=pltpu.PrefetchScalarGridSpec(
            num_scalar_prefetch=2,
            grid=(4,),
            in_specs=[inside() for a in operands],
            out_specs=[once((4, wide, part)), once((2 * hd, 128)), once((wide, 128))],
            scratch_shapes=[
                pltpu.VMEM((heads, row, 2 * hd), BF16),
                pltpu.VMEM((heads, 2 * hd, row), BF16),
                pltpu.VMEM((heads, row, hd), BF16),
                pltpu.VMEM((heads, hd, row), BF16),
                pltpu.VMEM((heads, hd, row), BF16),
                pltpu.VMEM((8, row), F32),
                pltpu.VMEM((8, row), F32),
                pltpu.VMEM((heads, row, hd), F32),
                pltpu.VMEM((heads, row, hd), F32),
                pltpu.VMEM((heads, hd, row), F32),
            ],
        ),
        out_shape=[
            jax.ShapeDtypeStruct((4, wide, part), BF16),
            jax.ShapeDtypeStruct((2 * hd, 128), F32),
            jax.ShapeDtypeStruct((wide, 128), F32),
        ],
        compiler_params=params(36),
        cost_estimate=took(1),
        name="attend_back",
    )(me, lengths, *operands)


def gelu_parts(x):
    size = jnp.abs(x)
    t = 1.0 / (1.0 + (0.3275911 * 2.0**-0.5) * size)
    bell = jnp.exp(-0.5 * x * x)
    poly = t * (
        0.127414796
        + t * (-0.142248368 + t * (0.7107068705 + t * (-0.7265760135 + t * 0.5307027145)))
    )
    upper = poly * bell
    below = jnp.where(x >= 0, 1.0 - upper, upper)
    return x * below, below + x * bell * 0.3989422804014327


def forward_kernel(groups, hidden, to_send, *refs):
    atts = refs[:groups]
    tok, w_own, w_sib, table = refs[groups : groups + 4]
    stream_ref, low_ref, active_ref, slope_ref, *part_refs = refs[groups + 4 :]
    heads_here = atts[0].shape[0]
    block = stream_ref.shape[0]
    here = pl.ds(pl.multiple_of(pl.program_id(0) * block, block), block)
    branch = None
    for j in range(groups):
        start = 2 * hidden + (j // 2) * heads_here
        term = mm((w_own, w_sib)[j % 2][:, start : start + heads_here], atts[j][:, here])
        branch = term if branch is None else branch + term
    stream = tok[here, :].astype(F32) + branch.T + line(table, OUT_BIAS)
    stream_ref[...] = stream
    hat, _ = rows_hat(stream)
    low = (hat * line(table, GAIN_2) + line(table, SHIFT_2)).astype(BF16)
    low_ref[...] = low
    total = None
    for n, source in enumerate((w_own, w_sib)):
        cols = slice(n * hidden, (n + 1) * hidden)
        raised = mm(low, source[:, :hidden]) + line(table, UP_BIAS + n)[:, :hidden]
        active, slope = gelu_parts(raised)
        active = active.astype(BF16)
        active_ref[:, cols] = active
        slope_ref[:, cols] = slope
        term = mm(active, source[:, hidden : 2 * hidden], NT)
        total = term if total is None else total + term
    if to_send:
        for n, part_ref in enumerate(part_refs):

            @pl.when(pl.program_id(0) == n)
            def _():
                part_ref[...] = total.astype(BF16)

    else:
        part_refs[0][...] = total
        part_refs[1][...] = w_own[:, 2 * hidden :]
        part_refs[2][...] = w_sib[:, 2 * hidden :]


def forward_call(atts, tok, w_own, w_sib, table, hidden, to_send):
    groups = len(atts)
    part, width = tok.shape
    block = min(TILE, part)
    heads_here = atts[0].shape[0]

    def rows(cols):
        return pl.BlockSpec((block, cols), lambda i: (i, 0))

    fixed = (w_own, w_sib, table)
    return pl.pallas_call(
        partial(forward_kernel, groups, hidden, to_send),
        grid=(part // block,),
        in_specs=[inside() for a in (*atts, tok, *fixed)],
        out_specs=[rows(width), rows(width), rows(2 * hidden), rows(2 * hidden)]
        + (
            [whole((block, width))] * (part // block)
            if to_send
            else [rows(width)] + [whole((width, 2 * heads_here))] * 2
        ),
        out_shape=[
            jax.ShapeDtypeStruct((part, width), F32),
            jax.ShapeDtypeStruct((part, width), BF16),
            jax.ShapeDtypeStruct((part, 2 * hidden), BF16),
            jax.ShapeDtypeStruct((part, 2 * hidden), F32),
        ]
        + (
            [jax.ShapeDtypeStruct((block, width), BF16)] * (part // block)
            if to_send
            else [jax.ShapeDtypeStruct((part, width), F32)]
            + [jax.ShapeDtypeStruct((width, 2 * heads_here), BF16)] * 2
        ),
        compiler_params=params(20),
        cost_estimate=took(10),
        name="forward",
    )(*atts, tok, *fixed)


def loss_kernel(
    part, n, pos, lens, stream, own, other, table, teacher, count, *refs
):
    out, grad_ref, low_ref, sums_ref, send = refs[-5:]
    block, width = stream.shape
    counted = count[0:1, 0:1].astype(F32)
    token = pos[0] * part + n * block + lax.broadcasted_iota(jnp.int32, (block, 1), 0)
    valid = (token < picture_ends(lens)[-1]).astype(F32)
    result = stream[...] + (own[...] + other[...].astype(F32)) + line(table, DOWN_BIAS)
    out[...] = result.astype(BF16)
    error = (result - teacher[...].astype(F32)) * valid
    grad = error * (2.0 / counted)
    grad_ref[...] = grad
    low = grad.astype(BF16)
    low_ref[...] = low
    send[...] = low
    old = refs[3][...] if len(refs) > 5 else jnp.zeros_like(sums_ref)
    sums_ref[...] = old
    sums_ref[0:1, :] += jnp.sum(low.astype(F32), axis=0, keepdims=True)
    squares = jnp.sum(error * error, axis=0, keepdims=True)
    sums_ref[1:2, :] += squares / counted


def loss_call(n, me, lengths, stream, own, other, table, teacher, count, before):
    part, width = stream.shape
    block = other.shape[0]
    rows = pl.BlockSpec((block, width), lambda i, s, r: (n, 0))
    piece = whole((block, width))
    return pl.pallas_call(
        partial(loss_kernel, part, n),
        grid_spec=pltpu.PrefetchScalarGridSpec(
            num_scalar_prefetch=2,
            grid=(1,),
            in_specs=[rows, rows, piece, whole(table.shape), rows, whole(count.shape)]
            + [pl.BlockSpec(memory_space=pl.ANY)] * (3 if before else 0)
            + [whole((8, width))] * (1 if before else 0),
            out_specs=[rows, rows, rows, whole((8, width)), piece],
        ),
        out_shape=[
            jax.ShapeDtypeStruct((part, width), BF16),
            pltpu.HBM((part, width), F32),
            jax.ShapeDtypeStruct((part, width), BF16),
            jax.ShapeDtypeStruct((8, width), F32),
            jax.ShapeDtypeStruct((block, width), BF16),
        ],
        input_output_aliases={8: 0, 9: 1, 10: 2} if before else {},
        compiler_params=params(8),
        cost_estimate=took(3),
        name="loss",
    )(me, lengths, stream, own, other, table, teacher, count, *before)


def backward_kernel(hidden, blocks, first, *refs):
    grad, slope, w_own, w_sib = refs[:4]
    low_ref, grad_ref, part_ref, bias_ref = refs[-4:]

    @pl.when(pl.program_id(0) == 0)
    def _():
        bias_ref[...] = jnp.zeros_like(bias_ref) if first else refs[7][...]

    total = None
    for n, source in enumerate((w_own, w_sib)):
        cols = slice(n * hidden, (n + 1) * hidden)
        low = (mm(grad[...], source[:, hidden : 2 * hidden]) * slope[:, cols]).astype(BF16)
        low_ref[:, cols] = low
        bias_ref[:, cols] += jnp.sum(low.astype(F32), axis=0, keepdims=True)
        term = mm(low, source[:, :hidden], NT)
        total = term if total is None else total + term
    grad_ref[...] = grad[...]
    part_ref[...] = total.astype(part_ref.dtype)


def backward_call(grad, slope, w_own, w_sib, hidden, part_type, n=0, before=()):
    part = slope.shape[0]
    height, width = grad.shape
    block = min(TILE, part)
    start = n * height // block

    def rows(cols):
        return pl.BlockSpec((block, cols), lambda i: (start + i, 0))

    here = pl.BlockSpec((block, width), lambda i: (i, 0))
    return pl.pallas_call(
        partial(backward_kernel, hidden, height // block, not before),
        grid=(height // block,),
        in_specs=[here, rows(2 * hidden)]
        + [inside()] * 2
        + [pl.BlockSpec(memory_space=pl.ANY)] * (3 if before else 0)
        + [whole((1, 2 * hidden))] * (1 if before else 0),
        out_specs=[rows(2 * hidden), rows(width), rows(width), whole((1, 2 * hidden))],
        out_shape=[
            jax.ShapeDtypeStruct((part, 2 * hidden), BF16),
            jax.ShapeDtypeStruct((part, width), BF16),
            (pltpu.HBM if part_type == F32 else jax.ShapeDtypeStruct)((part, width), part_type),
            jax.ShapeDtypeStruct((1, 2 * hidden), F32),
        ],
        input_output_aliases={4: 0, 5: 1, 6: 2} if before else {},
        compiler_params=params(14),
        cost_estimate=took(6 if part_type == BF16 else 0.1),
        name="backward",
    )(grad, slope, w_own, w_sib, *before)


def weight_terms_kernel(count, *refs):
    lefts, rights = refs[: 2 * count], refs[2 * count : 4 * count]
    come, out = refs[4 * count : -1], refs[-1]
    dims = (((0,), (0,)), ((), ()))
    half = out.shape[1] // 2
    for n in range(2):
        total = sum(mm(lefts[n * count + m][...], rights[n * count + m][...], dims) for m in range(count))
        cols = slice(n * half, (n + 1) * half)
        if come:
            total = total + come[0][:, cols].astype(F32)
        out[:, cols] = total.astype(BF16)


def weight_terms_call(lefts, rights, side, hidden, come):
    count = len(lefts[0])
    part, width = lefts[0][0].shape
    shape = (width, 2 * hidden)
    more = [] if come is None else [come]
    return pl.pallas_call(
        partial(weight_terms_kernel, count),
        grid=(1,),
        in_specs=[once((part, width))] * (2 * count)
        + [
            pl.BlockSpec((part, hidden), lambda i: (0, side), pipeline_mode=pl.Buffered(1))
        ]
        * (2 * count)
        + [once(shape)] * len(more),
        out_specs=once(shape),
        out_shape=jax.ShapeDtypeStruct(shape, BF16),
        compiler_params=params(26),
        cost_estimate=took(0.1),
        name="weight_terms",
    )(*lefts[0], *lefts[1], *rights[0], *rights[1], *more)


def out_terms_kernel(low, att_0, att_1, att_2, att_3, sent, kept):
    size = att_0.shape[0]
    for n, (first, second) in enumerate(((att_1, att_3), (att_0, att_2))):
        both = mm(jnp.concatenate([first[...], second[...]], axis=0), low[...]).T
        if n == 0:
            sent[...] = both.astype(BF16)
        else:
            kept[...] = both


def out_terms_call(low, atts):
    width = low.shape[1]
    cols = 2 * atts[0].shape[0]
    return pl.pallas_call(
        out_terms_kernel,
        out_shape=[
            jax.ShapeDtypeStruct((width, cols), BF16),
            jax.ShapeDtypeStruct((width, cols), F32),
        ],
        compiler_params=params(16),
        cost_estimate=took(0.1),
        name="out_terms",
    )(low, *atts)


def second_kernel(
    own, other, stream, result_grad, table, out_own, out_sib, *outs
):
    grad_ref, low_ref, sums_ref = outs[:3]
    heads_refs = outs[3:]

    @pl.when(pl.program_id(0) == 0)
    def _():
        sums_ref[...] = jnp.zeros_like(sums_ref)

    second_grad = own[...] + other[...].astype(F32)
    hat, factor = rows_hat(stream[...])
    sums_ref[0:1, :] += jnp.sum(second_grad * hat, axis=0, keepdims=True)
    sums_ref[1:2, :] += jnp.sum(second_grad, axis=0, keepdims=True)
    stream_grad = result_grad[...] + rows_back(second_grad * line(table, GAIN_2), hat, factor)
    grad_ref[...] = stream_grad
    low = stream_grad.astype(BF16)
    low_ref[...] = low
    sums_ref[2:3, :] += jnp.sum(low.astype(F32), axis=0, keepdims=True)
    for n, weight in enumerate((out_own, out_sib)):
        both = mm(low, weight[...]).T.astype(BF16)
        rows = both.shape[0] // 2
        heads_refs[n][...] = both[:rows]
        heads_refs[n + 2][...] = both[rows:]


def second_call(own, other, stream, result_grad, table, out_weights, groups, heads_here):
    part, width = own.shape
    block = min(TILE, part)
    rows = pl.BlockSpec((block, width), lambda i: (i, 0))
    lanes = pl.BlockSpec((heads_here, block), lambda i: (0, i))
    return pl.pallas_call(
        second_kernel,
        grid=(part // block,),
        in_specs=[rows] * 4
        + [once(table.shape)]
        + [once((width, 2 * heads_here))] * 2,
        out_specs=[rows, rows, whole((8, width))] + [lanes] * groups,
        out_shape=[
            jax.ShapeDtypeStruct((part, width), F32),
            jax.ShapeDtypeStruct((part, width), BF16),
            jax.ShapeDtypeStruct((8, width), F32),
        ]
        + [jax.ShapeDtypeStruct((heads_here, part), BF16)] * groups,
        compiler_params=params(56),
        cost_estimate=took(5),
        name="second_back",
    )(own, other, stream, result_grad, table, *out_weights)


def first_grad_kernel(wide, order, mixed, weight, *refs):
    count = len(order)
    toks = refs[:count]
    sums_ref = refs[count]
    outs = refs[count + 1 :]

    @pl.when(pl.program_id(0) == 0)
    def _():
        sums_ref[...] = jnp.zeros_like(sums_ref)

    for n, j in enumerate(order):
        grad = mm(weight[...], mixed[j]).T
        hat, _ = rows_hat(toks[n][...].astype(F32))
        sums_ref[0:1, :] += jnp.sum(grad * hat, axis=0, keepdims=True)
        sums_ref[1:2, :] += jnp.sum(grad, axis=0, keepdims=True)
        outs[0][n] = grad.astype(outs[0].dtype)


def first_grad_call(mixed, weight, toks, order, out_type):
    groups, wide, part = mixed.shape
    width = weight.shape[0]
    block = min(TILE, part)
    rows = pl.BlockSpec((block, width), lambda i: (i, 0))
    return pl.pallas_call(
        partial(first_grad_kernel, wide, order),
        grid=(part // block,),
        in_specs=[pl.BlockSpec((groups, wide, block), lambda i: (0, 0, i)), inside()]
        + [rows] * len(order),
        out_specs=[
            whole((8, width)),
            pl.BlockSpec((len(order), block, width), lambda i: (0, i, 0)),
        ],
        out_shape=[
            jax.ShapeDtypeStruct((8, width), F32),
            jax.ShapeDtypeStruct((len(order), part, width), out_type),
        ],
        compiler_params=params(16),
        cost_estimate=took(0.1),
        name="first_grad",
    )(mixed, weight, *[toks[j] for j in order])


def late_terms_kernel(bit, lows, mixed, out_terms, sent, kept):
    total = None
    for j in range(4):
        term = mm(mixed[j], lows[j])
        total = term if total is None else total + term
    wide = total.shape[0]

    @pl.when(pl.program_id(0) == 0)
    def _():
        sent[:, :wide] = total.T.astype(BF16)
        sent[:, wide:] = out_terms[...].astype(BF16)

    @pl.when(pl.program_id(0) == 1)
    def _():
        kept[:, :wide] = total.T
        kept[:, wide:] = out_terms[...]


def late_terms_call(lows, mixed, out_terms):
    part, width = lows.shape[1:]
    wide = mixed.shape[1]
    cols = wide + out_terms.shape[1]
    half = width // 2
    bit = top_bit("dp")[0].reshape(1)

    def side(i, s):
        return s[0] ^ 1 ^ i

    return pl.pallas_call(
        late_terms_kernel,
        grid_spec=pltpu.PrefetchScalarGridSpec(
            num_scalar_prefetch=1,
            grid=(2,),
            in_specs=[
                pl.BlockSpec((4, part, half), lambda i, s: (0, 0, side(i, s))),
                inside(),
                pl.BlockSpec((half, out_terms.shape[1]), lambda i, s: (side(i, s), 0)),
            ],
            out_specs=[whole((half, cols)), whole((half, cols))],
        ),
        out_shape=[
            jax.ShapeDtypeStruct((half, cols), BF16),
            jax.ShapeDtypeStruct((half, cols), F32),
        ],
        compiler_params=params(20),
        cost_estimate=took(5),
        name="late_terms",
    )(bit, lows, mixed, out_terms)


def late_final_kernel(kept, come, in_ref, out_ref):
    total = kept[...] + come[...].astype(F32)
    wide = in_ref.shape[1]
    in_ref[...] = total[:, :wide]
    out_ref[...] = total[:, wide:].T


def late_final_call(kept, come, wide):
    rows, cols = kept.shape
    return pl.pallas_call(
        late_final_kernel,
        out_shape=[
            jax.ShapeDtypeStruct((rows, wide), F32),
            jax.ShapeDtypeStruct((cols - wide, rows), F32),
        ],
        compiler_params=params(6),
        cost_estimate=took(1),
        name="late_final",
    )(kept, come)


def weight_final_kernel(grads, up_ref, down_ref):
    half = up_ref.shape[1]
    up_ref[...] = grads[:, :half].astype(F32)
    down_ref[...] = grads[:, half:].astype(F32).T


def weight_final_call(grads):
    rows, cols = grads.shape
    half = cols // 2
    return pl.pallas_call(
        weight_final_kernel,
        out_shape=[
            jax.ShapeDtypeStruct((rows, half), F32),
            jax.ShapeDtypeStruct((half, rows), F32),
        ],
        compiler_params=params(6),
        cost_estimate=took(1),
        name="weight_final",
    )(grads)


def pair_kernel(own, come, out):
    out[...] = (own[0] + come[0].astype(F32)).astype(BF16)


def pair_call(own, come):
    part, width = own.shape[1:]
    block = min(TILE, part)
    second = pl.BlockSpec((1, block, width), lambda i: (1, i, 0))
    return pl.pallas_call(
        pair_kernel,
        grid=(part // block,),
        in_specs=[second] * 2,
        out_specs=pl.BlockSpec((block, width), lambda i: (i, 0)),
        out_shape=jax.ShapeDtypeStruct((part, width), BF16),
        compiler_params=params(8),
        cost_estimate=took(0.1),
        name="pair",
    )(own, come)


def first_back_kernel(own, come, other, tok, stream_grad, table, out_ref):
    hat, factor = rows_hat(tok[...].astype(F32))
    grad = own[0] + come[0].astype(F32) + other[...].astype(F32)
    out_ref[...] = stream_grad[...] + rows_back(grad * line(table, GAIN_1), hat, factor)


def first_back_call(own, come, other, tok, stream_grad, table):
    part, width = tok.shape
    block = min(TILE, part)
    rows = pl.BlockSpec((block, width), lambda i: (i, 0))
    return pl.pallas_call(
        first_back_kernel,
        grid=(part // block,),
        in_specs=[pl.BlockSpec((1, block, width), lambda i: (0, i, 0))] * 2
        + [rows] * 3
        + [whole(table.shape)],
        out_specs=rows,
        out_shape=jax.ShapeDtypeStruct((part, width), F32),
        compiler_params=params(10),
        cost_estimate=took(1),
        name="first_back",
    )(own, come, other, tok, stream_grad, table)


def own_rows(vector, group, amount):
    return lax.dynamic_slice_in_dim(vector, group * amount, amount)


def local(
    tokens,
    teacher,
    picture_lengths,
    first_gain,
    first_shift,
    input_weight,
    input_bias,
    query_gain,
    key_gain,
    output_weight,
    output_bias,
    second_gain,
    second_shift,
    expand_weight,
    expand_bias,
    reduce_weight,
    reduce_bias,
):
    assert tokens.shape[0] == 1 and lax.axis_size("gx") == 4
    part, width = tokens.shape[1:]
    groups = 4
    group = lax.axis_index("gx")
    hd = query_gain.shape[0]
    wide = input_weight.shape[1]
    heads = wide // (3 * hd)
    heads_here = heads * hd
    hidden = expand_weight.shape[1]
    shard_rows = input_weight.shape[0]

    me = group.reshape(1).astype(jnp.int32)
    lengths = picture_lengths[0]
    out_shard = output_weight.T
    out_pair = swap(out_shard, "gx", 2)
    tok0 = tokens[0]
    tok2 = swap(tok0, "gx", 2)
    table_rows = [first_gain, first_shift, second_gain, second_shift, output_bias, reduce_bias]
    table_rows += [own_rows(expand_bias, group, hidden), own_rows(expand_bias, group ^ 1, hidden)]
    table_rows += [jnp.pad(own_rows(input_bias, group, wide), (0, width - wide))]
    table = jnp.stack(table_rows)
    gains = jnp.stack([query_gain, key_gain], axis=1)
    counted = jnp.full((8, 128), jnp.sum(lengths), jnp.int32)
    in_part, w_own = input_weight, None
    for mask in reversed(bits_of("gy")):
        more = swap(counted, "gy", mask)
        in_part = joined("gy", mask, in_part, shard_rows, table, gains, more)
        counted = counted + more
        if w_own is None:
            w_own = lax.all_gather(
                after(
                    jnp.concatenate([expand_weight, reduce_weight.T, out_shard, out_pair], axis=1), in_part
                ),
                ("dp", "gy"),
                axis=0,
                tiled=True,
            )
    w_in = in_part
    for mask in bits_of("dp"):
        more = swap(counted, "dp", mask)
        w_in = joined("dp", mask, w_in, w_in.shape[0], more)
        counted = counted + more
    tok3 = swap(after(tok2, w_in), "gx", 1)
    tok1 = swap(after(tok0, in_part), "gx", 1)
    toks = (tok0, tok1, tok2, tok3)

    low, mixed, mixed_kept, hats, scales = mixed_call(toks, table, w_in, gains, heads, hd)
    *atts, raw, log = attend_call(me, lengths, mixed, heads, hd)
    att_pair = [atts[2]] + [swap(atts[j ^ 2], "gx", j) for j in range(1, 4)]
    w_own = after(w_own, raw, att_pair[2])
    w_sib = swap(w_own, "gx", 1)
    atts = after(atts, *att_pair)
    att_own = [atts[0]] + [swap(atts[j], "gx", j) for j in range(1, 4)]

    def forward_of(pieces, tok, to_send):
        return forward_call(pieces, tok, w_own, w_sib, table, hidden, to_send)

    _, low_p, active_p, slope_p, *parts_p = forward_of(att_pair, tok2, True)
    stream, low_o, active_o, slope_o, part_o, *out_weights = forward_of(att_own, tok0, False)
    parts_in = [swap(parts_p[0], "gx", 2)]
    parts_in += [swap(after(piece, part_o), "gx", 2) for piece in parts_p[1:]]
    state, pairs = (), []
    for n, piece in enumerate(parts_in):
        if state:
            piece = after(piece, state[0])
        *state, low_sent = loss_call(
            n, me, lengths, stream, part_o, piece, table, teacher[0], counted, state
        )
        pairs.append(swap(low_sent, "gx", 2))
    layer_output, result_grad, reduce_low, sums_3 = state

    hidden_o, _, back_o, up_sum_o = backward_call(reduce_low, slope_o, w_own, w_sib, hidden, F32)
    state = ()
    for n, piece in enumerate(pairs):
        if state:
            piece = after(piece, state[0])
        state = backward_call(piece, slope_p, w_own, w_sib, hidden, BF16, n, state)
    hidden_p, reduce_pair, back_p, up_sum_p = state
    back_in = swap(back_p, "gx", 2)

    lefts = ((low_o, low_p), (reduce_low, reduce_pair))
    rights = ((hidden_o, hidden_p), (active_o, active_p))
    sib_terms = swap(weight_terms_call(lefts, rights, 1, hidden, None), "gx", 1)
    weight_terms = weight_terms_call(lefts, rights, 0, hidden, sib_terms)
    weight_grads = lax.psum_scatter(weight_terms, ("dp", "gy"), scatter_dimension=0, tiled=True)
    stream_grad, branch_low, sums_2, *heads_grad = second_call(
        back_o,
        after(back_in, weight_terms),
        stream,
        result_grad,
        table,
        out_weights,
        groups,
        heads_here,
    )
    grads = [heads_grad[0]] + [swap(heads_grad[j], "gx", j) for j in range(1, 4)]

    out_sent, out_held = out_terms_call(branch_low, att_own)
    out_held = out_held + swap(out_sent, "gx", 1).astype(F32)
    out_own = out_held[:, :heads_here] + swap(
        out_held[:, heads_here:].astype(BF16), "gx", 2
    ).astype(F32)

    mixed_low, gain_sums, bias_sums = attend_back_call(
        me, lengths, mixed_kept, hats, scales, raw, log, grads, gains, heads, hd
    )
    sums_s, sent = first_grad_call(after(mixed_low, out_own), w_in, toks, (1, 3), BF16)
    sib_in = swap(sent, "gx", 1)
    late_sent, late_kept = late_terms_call(low, after(mixed_low, sent), out_own)
    come = swap(late_sent, "dp", top_bit("dp")[1])
    sums_k, kept = first_grad_call(after(mixed_low, late_kept), w_in, toks, (0, 2), F32)
    pair_sent = pair_call(kept, sib_in)
    pair_in = swap(pair_sent, "gx", 2)

    sums = pack_call(
        me, groups, up_sum_o, up_sum_p, sums_2, sums_3, sums_s, sums_k, bias_sums, gain_sums
    )
    sums = after(sums, pair_sent)
    sums = sum_over(sums + swap(sums, "gx", 1), "gy")
    come = after(come, sums, weight_grads)
    for mask in reversed(bits_of("dp")[:-1]):
        late_kept, come = halved("dp", mask, late_kept, come, late_kept.shape[0] // 2)
    first, *others = bits_of("gy")
    late_kept, come = halved("gy", first, late_kept, come, shard_rows)
    sums = sum_over(after(sums, late_kept), "dp")
    come = after(come, sums)
    tokens_gradient = first_back_call(kept, sib_in, pair_in, tok0, stream_grad, table)
    for mask in others:
        late_kept, come = halved("gy", mask, late_kept, come, shard_rows)
    sums = sums + swap(after(sums, tokens_gradient, late_kept), "gx", 2)
    expand_out, reduce_out = weight_final_call(after(weight_grads, late_kept))
    input_out, output_out = late_final_call(late_kept, after(come, sums), wide)
    row = 2 * groups
    return (
        layer_output[None],
        jnp.sum(sums[row + 4]),
        tokens_gradient[None],
        sums[row + 5],
        sums[row + 6],
        input_out,
        sums[groups:row, :wide].reshape(-1),
        sums[row + 7, :hd],
        sums[row + 7, hd : 2 * hd],
        output_out,
        sums[row + 2],
        sums[row],
        sums[row + 1],
        expand_out,
        sums[:groups, :hidden].reshape(-1),
        reduce_out,
        sums[row + 3],
    )


def solution(mesh):
    rows = P(("dp", "gy"), "gx", None)
    by_rows = P(("dp", "gy"), "gx")
    by_cols = P("gx", ("dp", "gy"))
    return jax.shard_map(
        local,
        mesh=mesh,
        in_specs=(
            rows,
            rows,
            P(("dp", "gy"), None),
            P(),
            P(),
            by_rows,
            P(),
            P(),
            P(),
            by_cols,
            P(),
            P(),
            P(),
            by_rows,
            P(),
            by_cols,
            P(),
        ),
        out_specs=(
            rows,
            P(),
            rows,
            P(),
            P(),
            by_rows,
            P(),
            P(),
            P(),
            by_cols,
            P(),
            P(),
            P(),
            by_rows,
            P(),
            by_cols,
            P(),
        ),
        check_vma=False,
    )
```
